32 devices in a mesh: dp: 8 (over y, x, core), ctx: 4 (over z).
Axes of the slice: x: 2, y: 2, z: 4, core: 2. Of those that a mesh axis runs over, the one named last changes fastest.
Arguments:
- tokens: bfloat16 [8, 1536, 8192], P('dp', 'ctx'), may hold values from -24 to 24
- w_query: bfloat16 [8192, 512], P('dp'), may hold values from -0.09375 to 0.09375
- w_key: bfloat16 [8192, 128], P('dp'), may hold values from -0.09375 to 0.09375
- w_value: bfloat16 [8192, 128], P('dp'), may hold values from -0.0625 to 0.0625
- doc_lengths: int32 [8, 16], P('dp'), may hold values from 1 to 768, 1536 in all within a row
Outputs:
- attended: bfloat16 [8, 1536, 512], P('dp', 'ctx')
The draws below stay inside these ranges and needn't reach their ends.
Inputs may be any that keep to these rules, and one draw needn't show every extreme that they name: `doc_lengths`: each row holds the 16 document lengths of one sequence, summing to 1536, the largest exactly 768.
All inputs are finite; a program needn't handle non-finite values.
Results may differ from the reference program's by a relative error of at most 0.02.
Values may be sent and summed in bfloat16 or wider, within the bound.
No kernel may reach another device: no remote copies, remote signals or barrier semaphores. Data moves between devices by JAX's collectives and lax.ppermute only.
A program may use at most 64 MiB of HBM per device.

```python
import math
import jax
import jax.numpy as jnp
import numpy as np
from jax import lax

D = 8192
HEAD = 128
GROUP = 4
NDOCS = 16
SEQS = 8
SEQ_LEN = 1536
MOST = 768


def draw_tokens(key, part):
    shape = (SEQS, SEQ_LEN, D)
    drawn = jnp.clip(jax.random.normal(key, shape, jnp.float32), -6.0, 6.0)
    return drawn.astype(jnp.bfloat16)


def levels(stream_key, shape, cuts, low, high):
    factor_of = 1.0
    for position, shards_of in cuts:
        heights = jax.random.uniform(jax.random.fold_in(jax.random.fold_in(stream_key, 6), position), (shards_of,), jnp.float32, low / len(cuts), high / len(cuts))
        factor_of = factor_of * jnp.repeat(jnp.exp(heights), shape[position] // shards_of).reshape((-1,) + (1,) * (len(shape) - 1 - position))
    return factor_of


def length_profile(number_of, total, reach, skew):
    loads = [(1 << 20) // math.isqrt(standing ** skew) + 1 for standing in range(2, number_of + 1)]
    rest, given = total - reach - (number_of - 1), [1] * (number_of - 1)
    while rest > 0:
        movable = [i for i in range(number_of - 1) if given[i] < reach]
        pool, remaining = sum([loads[i] for i in movable]), rest
        for i in movable:
            more = min(reach - given[i], max(1, remaining * loads[i] // pool), rest)
            given[i] = given[i] + more
            rest = rest - more
    return np.array([reach] + given)


def ragged(rng, number_of, total, limit, slope):
    if number_of == 2:
        one = jax.random.randint(rng, (), max(1, total - limit), min(limit, total - 1) + 1)
        return jnp.stack([one, total - one])
    tallies = jnp.asarray(length_profile(number_of, total, limit, slope), jnp.int32)
    pairs = (number_of - 1) // 2
    donor, taker = tallies[1:1 + 2 * pairs:2], tallies[2:2 + 2 * pairs:2]
    room = jnp.minimum(donor - 1, limit - taker)
    passed = jax.random.randint(jax.random.fold_in(rng, 1), (pairs,), 0, 1 << 20) % (room + 1)
    tallies = tallies.at[1:1 + 2 * pairs:2].set(donor - passed).at[2:2 + 2 * pairs:2].set(taker + passed)
    return tallies[jax.random.permutation(jax.random.fold_in(rng, 2), number_of)]


def centred(own_key, extent, width, bound, shards=(), held_as=jnp.bfloat16):
    values = jax.random.normal(own_key, extent, jnp.float32) * width
    if len(shards) > 0:
        values = levels(own_key, extent, shards, -0.22, 0.18) * values
    return jnp.clip(values, min=-bound, max=bound).astype(held_as)


def setup_inputs(seed: int = 0) -> dict:
    keys = jax.random.split(jax.random.key(seed), 6)
    tokens = draw_tokens(jax.random.fold_in(keys[5], 71), 0)
    w_query = centred(keys[1], (D, GROUP * HEAD), (1.4 * D ** -0.5), 0.09375, ((0, 8),))
    w_key = centred(keys[2], (D, HEAD), (1.4 * D ** -0.5), 0.09375, ((0, 8),))
    w_value = centred(keys[3], (D, HEAD), D ** -0.5, 0.0625, ((0, 8),))
    doc_lengths = jax.vmap(lambda own: ragged(own, NDOCS, SEQ_LEN, MOST, 2))(jax.random.split(keys[4], SEQS)).reshape((SEQS, NDOCS)).astype(jnp.int32)
    return dict(tokens=tokens, w_query=w_query, w_key=w_key, w_value=w_value, doc_lengths=doc_lengths)


def rotate(vectors, positions):
    half_size = vectors.shape[-1] // 2
    exponent = jnp.arange(half_size, dtype=jnp.float32) * (2.0 / vectors.shape[-1])
    inverse = jnp.power(jnp.float32(500000.0), -exponent)
    angles = positions.astype(jnp.float32)[:, None] * inverse[None, :]
    cosine = jnp.cos(angles)
    sine_part = jnp.sin(angles)
    if vectors.ndim == 3:
        cosine = cosine[:, None, :]
        sine_part = sine_part[:, None, :]
    leading = vectors[..., :half_size]
    trailing = vectors[..., half_size:]
    return jnp.concatenate([leading * cosine - trailing * sine_part, trailing * cosine + leading * sine_part], axis=-1)

def doc_starts(doc_sizes, positions):
    doc_ends = jnp.cumsum(doc_sizes).astype(jnp.int32)
    doc_begin = (doc_ends - doc_sizes).astype(jnp.int32)
    chosen = jnp.where(doc_begin[None, :] <= positions[:, None], doc_begin[None, :], 0)
    return lax.optimization_barrier(jnp.max(chosen, axis=1)).astype(jnp.int32)

def reference(tokens, w_query, w_key, w_value, doc_lengths):
    scaling = 1.0 / math.sqrt(HEAD)

    def per_sequence(inputs):
        hidden, doc_sizes = inputs
        seq_rows = hidden.shape[0]
        positions = jnp.arange(seq_rows, dtype=jnp.int32)
        queries = rotate(jnp.dot(hidden, w_query, preferred_element_type=jnp.float32).reshape(seq_rows, GROUP, HEAD), positions).astype(jnp.bfloat16)
        own_keys = rotate(jnp.dot(hidden, w_key, preferred_element_type=jnp.float32), positions).astype(jnp.bfloat16)
        values_here = jnp.dot(hidden, w_value, preferred_element_type=jnp.float32).astype(jnp.bfloat16)
        queries, own_keys, values_here = lax.optimization_barrier((queries, own_keys, values_here))
        doc_first = doc_starts(doc_sizes, positions)
        block_rows = 512

        def attend_block(block_index):
            query_block = lax.dynamic_slice_in_dim(queries, block_index * block_rows, block_rows, 0)
            query_pos = block_index * block_rows + jnp.arange(block_rows, dtype=jnp.int32)
            first_block = lax.dynamic_slice_in_dim(doc_first, block_index * block_rows, block_rows, 0)
            scores = jnp.einsum('tgd,kd->tgk', query_block.astype(jnp.float32), own_keys.astype(jnp.float32)) * scaling
            allowed = (positions[None, :] <= query_pos[:, None]) & (positions[None, :] >= first_block[:, None])
            allowed = allowed[:, None, :]
            scores = jnp.where(allowed, scores, jnp.float32(-1e+30))
            running_max = lax.optimization_barrier(jnp.max(scores, axis=-1))
            exponents = jnp.where(allowed, jnp.exp(scores - running_max[..., None]), jnp.float32(0.0))
            denominator = lax.optimization_barrier(jnp.sum(exponents, axis=-1))
            weights = lax.optimization_barrier(exponents.astype(jnp.bfloat16))
            numerator = jnp.einsum('tgk,kd->tgd', weights.astype(jnp.float32), values_here.astype(jnp.float32))
            attended = numerator / denominator[..., None]
            return attended.reshape(block_rows, GROUP * HEAD).astype(jnp.bfloat16)
        blocks = lax.map(attend_block, jnp.arange(seq_rows // block_rows, dtype=jnp.int32))
        return blocks.reshape(seq_rows, GROUP * HEAD)
    return lax.map(per_sequence, (tokens, doc_lengths))
```

```python
import functools
import math

import jax
import jax.numpy as jnp
from jax import lax
from jax.experimental import pallas as pl
from jax.experimental.pallas import tpu as pltpu
from jax.sharding import PartitionSpec as P

ROW_TILE = 128


def rope_tables(positions, head_size):
    half_size = head_size // 2
    exponent = jnp.arange(half_size, dtype=jnp.float32) * (2.0 / head_size)
    inverse = jnp.power(jnp.float32(500000.0), -exponent)
    angles = positions.astype(jnp.float32)[:, None] * inverse[None, :]
    cosine = jnp.cos(angles)
    sine_part = jnp.sin(angles)
    return (
        jnp.concatenate([cosine, cosine], axis=-1),
        jnp.concatenate([-sine_part, sine_part], axis=-1),
    )


def doc_starts(doc_sizes, positions):
    doc_ends = jnp.cumsum(doc_sizes)
    doc_begin = doc_ends - doc_sizes
    chosen = jnp.where(doc_begin[None, :] <= positions[:, None], doc_begin[None, :], 0)
    return jnp.max(chosen, axis=1)


def attend_kernel(head_count, back, near, far, cosine, sine, first, keys_values, out, rotated):
    rows, head_size = cosine.shape
    base = keys_values.shape[0] - rows
    tiles = rows // ROW_TILE
    for head in range(head_count):
        columns = slice(head * head_size, (head + 1) * head_size)
        query = near[:, columns] + far[:, columns]
        swapped = pltpu.roll(query, head_size // 2, 1)
        turned = (query * cosine[...] + swapped * sine[...]).astype(jnp.bfloat16)
        for tile in range(tiles):
            rotated[tile, head * ROW_TILE : (head + 1) * ROW_TILE, :] = turned[
                tile * ROW_TILE : (tile + 1) * ROW_TILE
            ]
    scale = jnp.float32(math.log2(math.e) / math.sqrt(head_size))
    for tile in range(tiles):
        begin = base + tile * ROW_TILE - back
        window = keys_values[begin : begin + back + ROW_TILE, :]
        scores = lax.dot_general(
            rotated[tile],
            window[:, :head_size],
            (((1,), (1,)), ((), ())),
            preferred_element_type=jnp.float32,
        )
        shape = (ROW_TILE, back + ROW_TILE)
        key_place = lax.broadcasted_iota(jnp.int32, shape, 1) + (tile * ROW_TILE - back)
        row_place = lax.broadcasted_iota(jnp.int32, shape, 0) + tile * ROW_TILE
        lower = first[tile * ROW_TILE : (tile + 1) * ROW_TILE, :]
        allowed = (key_place <= row_place) & (key_place >= lower)
        for head in range(head_count):
            part = scores[head * ROW_TILE : (head + 1) * ROW_TILE]
            part = jnp.where(allowed, part, jnp.float32(-1e30))
            largest = jnp.max(part, axis=-1, keepdims=True)
            exponents = jnp.exp2((part - largest) * scale)
            denominator = jnp.sum(exponents, axis=-1, keepdims=True)
            numerator = jnp.dot(
                exponents.astype(jnp.bfloat16),
                window[:, head_size:],
                preferred_element_type=jnp.float32,
            )
            out[
                tile * ROW_TILE : (tile + 1) * ROW_TILE, head * head_size : (head + 1) * head_size
            ] = (numerator / denominator).astype(out.dtype)


def attend(near, far, cosine, sine, first, keys_values, back):
    rows, width = near.shape
    head_size = cosine.shape[1]
    head_count = width // head_size
    return pl.pallas_call(
        functools.partial(attend_kernel, head_count, back),
        out_shape=jax.ShapeDtypeStruct((rows, width), jnp.bfloat16),
        in_specs=[pl.BlockSpec(memory_space=pltpu.VMEM)] * 6,
        out_specs=pl.BlockSpec(memory_space=pltpu.VMEM),
        scratch_shapes=[
            pltpu.VMEM((rows // ROW_TILE, head_count * ROW_TILE, head_size), jnp.bfloat16)
        ],
        compiler_params=pltpu.CompilerParams(vmem_limit_bytes=48 * 1024 * 1024),
        cost_estimate=pl.CostEstimate(
            flops=4 * rows * width * (back + ROW_TILE),
            bytes_accessed=8 * rows * width,
            transcendentals=rows * head_count * (back + ROW_TILE),
        ),
    )(near, far, cosine, sine, first, keys_values)


def shards(dp_size, ctx_size, tokens, w_query, w_key, w_value, doc_lengths):
    hidden = tokens[0]
    row_count = hidden.shape[0]
    depth = w_query.shape[0]
    head_size = w_key.shape[1]
    chips = dp_size // 2
    bits = chips.bit_length() - 1
    me = lax.axis_index("dp")
    place = lax.axis_index("ctx")

    def swap(array, mask):
        return lax.ppermute(array, "dp", [(i, i ^ mask) for i in range(dp_size)])

    def fetch(array, order):
        held = {0: array}
        for bit in order:
            for chip in sorted(held):
                held[chip | (1 << bit)] = swap(held[chip], 2 << bit)
        return held

    def columns(core):
        return jnp.concatenate(
            [
                lax.dynamic_slice_in_dim(hidden, (me ^ (chip * 2 + core)) * depth, depth, 1)
                for chip in range(chips)
            ],
            axis=1,
        )

    half = depth // 2
    upward, downward = list(range(bits)), list(range(bits))[::-1]
    w_pair = jnp.concatenate([w_key, w_value], axis=1)
    pair_parts = (fetch(w_pair[:half], upward), fetch(w_pair[half:], downward))
    query_parts = (fetch(w_query[:half], upward), fetch(w_query[half:], downward))
    rows_here = jnp.concatenate([columns(0), swap(columns(1), 1)], axis=0)

    def project(parts):
        total = None
        for chip in range(chips):
            for side in range(2):
                begin = chip * depth + side * half
                term = jnp.dot(
                    rows_here[:, begin : begin + half],
                    parts[side][chip],
                    preferred_element_type=jnp.float32,
                )
                total = term if total is None else total + term
        return total[:row_count], swap(total[row_count:], 1)

    offset = place * row_count
    positions = offset + jnp.arange(row_count, dtype=jnp.int32)
    cosine, sine = rope_tables(positions, head_size)
    first = (doc_starts(doc_lengths[0], positions) - offset)[:, None]

    pair_near, pair_far = project(pair_parts)
    pair = pair_near + pair_far
    key = pair[:, :head_size]
    swapped = jnp.concatenate([key[:, head_size // 2 :], key[:, : head_size // 2]], axis=1)
    key = key * cosine + swapped * sine
    pair = jnp.concatenate([key, pair[:, head_size:]], axis=1).astype(jnp.bfloat16)

    longest = ctx_size * row_count // 2
    back = -(-(longest - 1) // ROW_TILE) * ROW_TILE
    hops = min(ctx_size - 1, -(-back // row_count))
    blocks = [
        lax.ppermute(pair, "ctx", [(i, i + hop) for i in range(ctx_size - hop)])
        for hop in range(hops, 0, -1)
    ]
    keys_values = jnp.concatenate(blocks + [pair], axis=0)

    query_near, query_far = project(query_parts)
    return attend(query_near, query_far, cosine, sine, first, keys_values, back)[None]


def solution(mesh):
    return jax.shard_map(
        functools.partial(shards, mesh.shape["dp"], mesh.shape["ctx"]),
        mesh=mesh,
        in_specs=(P("dp", "ctx", None), P("dp", None), P("dp", None), P("dp", None), P("dp", None)),
        out_specs=P("dp", "ctx", None),
        check_vma=False,
    )
```

```python
import functools
import math

import jax
import jax.numpy as jnp
from jax import lax
from jax.experimental import pallas as pl
from jax.experimental.pallas import tpu as pltpu
from jax.sharding import PartitionSpec as P

ROW_TILE = 128
VMEM_LIMIT = 48 * 1024 * 1024


def rope_tables(positions, head_size):
    half_size = head_size // 2
    exponent = jnp.arange(half_size, dtype=jnp.float32) * (2.0 / head_size)
    inverse = jnp.power(jnp.float32(500000.0), -exponent)
    angles = positions.astype(jnp.float32)[:, None] * inverse[None, :]
    cosine = jnp.cos(angles)
    sine_part = jnp.sin(angles)
    return (
        jnp.concatenate([cosine, cosine], axis=-1),
        jnp.concatenate([-sine_part, sine_part], axis=-1),
    )


def doc_starts(doc_sizes, positions):
    doc_ends = jnp.cumsum(doc_sizes)
    doc_begin = doc_ends - doc_sizes
    chosen = jnp.where(doc_begin[None, :] <= positions[:, None], doc_begin[None, :], 0)
    return jnp.max(chosen, axis=1)


def vmem(count):
    return [pl.BlockSpec(memory_space=pltpu.VMEM)] * count


def anywhere(count):
    return [pl.BlockSpec(memory_space=pl.ANY)] * count


def after(array, *earlier):
    return lax.optimization_barrier((array, *earlier))[0]


def project_kernel(chips, spots, carried, final, starts, near, far, *refs):
    weights = refs[: len(chips) * len(spots)]
    refs = refs[len(weights) :]
    if carried:
        carry, refs = refs[0], refs[1:]
    outs, (tokens, held, sems) = refs[:-3], refs[-3:]
    rows = near.shape[0]
    depth = held.shape[1]
    copies = []
    for step, chip in enumerate(chips):
        window = pl.ds(pl.multiple_of(starts[chip], 128), depth)
        batch = [
            pltpu.make_async_copy(near.at[:, window], tokens.at[step, :rows], sems.at[step, 0]),
            pltpu.make_async_copy(far.at[:, window], tokens.at[step, rows:], sems.at[step, 1]),
        ]
        for index, spot in enumerate(spots):
            batch.append(
                pltpu.make_async_copy(
                    weights[step * len(spots) + index],
                    held.at[(step, *spot)],
                    sems.at[step, 2 + index],
                )
            )
        for copy in batch:
            copy.start()
        copies.append(batch)
    total = carry[...] if carried else None
    for step, batch in enumerate(copies):
        for copy in batch:
            copy.wait()
        term = jnp.dot(tokens[step], held[step], preferred_element_type=jnp.float32)
        total = term if total is None else total + term
    if final:
        outs[0][...] = total[:rows]
        outs[1][...] = total[rows:]
    else:
        outs[0][...] = total


def project(chips, spots, depth, starts, near, far, weights, carry, final):
    rows = near.shape[0]
    width = sum(w.size for w in weights[: len(spots)]) // depth
    whole = jax.ShapeDtypeStruct((2 * rows, width), jnp.float32)
    part = jax.ShapeDtypeStruct((rows, width), jnp.float32)
    carries = [] if carry is None else [carry]
    return pl.pallas_call(
        functools.partial(project_kernel, chips, spots, carry is not None, final),
        out_shape=(part, part) if final else whole,
        in_specs=[pl.BlockSpec(memory_space=pltpu.SMEM)]
        + anywhere(2 + len(weights))
        + vmem(len(carries)),
        out_specs=tuple(vmem(2)) if final else vmem(1)[0],
        scratch_shapes=[
            pltpu.VMEM((len(chips), 2 * rows, depth), jnp.bfloat16),
            pltpu.VMEM((len(chips), depth, width), jnp.bfloat16),
            pltpu.SemaphoreType.DMA((len(chips), 2 + len(spots))),
        ],
        compiler_params=pltpu.CompilerParams(vmem_limit_bytes=VMEM_LIMIT),
        cost_estimate=pl.CostEstimate(
            flops=4 * rows * width * depth * len(chips),
            bytes_accessed=2 * len(chips) * depth * (2 * rows + width),
            transcendentals=0,
        ),
    )(starts, near, far, *weights, *carries)


def turn(vectors, cosine, sine):
    return vectors * cosine + pltpu.roll(vectors, vectors.shape[1] // 2, 1) * sine


def pair_kernel(near, far, cosine, sine, out):
    head_size = cosine.shape[1]
    pair = near[...] + far[...]
    out[:, :head_size] = turn(pair[:, :head_size], cosine[...], sine[...]).astype(out.dtype)
    out[:, head_size:] = pair[:, head_size:].astype(out.dtype)


def finish_pair(near, far, cosine, sine):
    return pl.pallas_call(
        pair_kernel,
        out_shape=jax.ShapeDtypeStruct(near.shape, jnp.bfloat16),
        in_specs=vmem(4),
        out_specs=vmem(1)[0],
        cost_estimate=pl.CostEstimate(
            flops=6 * near.size, bytes_accessed=14 * near.size, transcendentals=0
        ),
    )(near, far, cosine, sine)


def attend_kernel(back, near, far, cosine, sine, first, keys_values, *refs):
    earlier, (out, rotated) = refs[:-2], refs[-2:]
    rows, head_size = cosine.shape
    head_count = near.shape[1] // head_size
    base = keys_values.shape[0] - rows
    tiles = rows // ROW_TILE
    filled = 0
    for ref in earlier:
        out[:, filled : filled + ref.shape[1]] = ref[...]
        filled += ref.shape[1]
    for head in range(head_count):
        columns = slice(head * head_size, (head + 1) * head_size)
        turned = turn(near[:, columns] + far[:, columns], cosine[...], sine[...])
        turned = turned.astype(jnp.bfloat16)
        for tile in range(tiles):
            rotated[tile, head * ROW_TILE : (head + 1) * ROW_TILE, :] = turned[
                tile * ROW_TILE : (tile + 1) * ROW_TILE
            ]
    scale = jnp.float32(math.log2(math.e) / math.sqrt(head_size))
    for tile in range(tiles):
        begin = base + tile * ROW_TILE - back
        window = keys_values[begin : begin + back + ROW_TILE, :]
        scores = lax.dot_general(
            rotated[tile],
            window[:, :head_size],
            (((1,), (1,)), ((), ())),
            preferred_element_type=jnp.float32,
        )
        shape = (ROW_TILE, back + ROW_TILE)
        key_place = lax.broadcasted_iota(jnp.int32, shape, 1) + (tile * ROW_TILE - back)
        row_place = lax.broadcasted_iota(jnp.int32, shape, 0) + tile * ROW_TILE
        lower = first[tile * ROW_TILE : (tile + 1) * ROW_TILE, :]
        allowed = (key_place <= row_place) & (key_place >= lower)
        for head in range(head_count):
            part = scores[head * ROW_TILE : (head + 1) * ROW_TILE]
            part = jnp.where(allowed, part, jnp.float32(-1e30))
            largest = jnp.max(part, axis=-1, keepdims=True)
            exponents = jnp.exp2((part - largest) * scale)
            denominator = jnp.sum(exponents, axis=-1, keepdims=True)
            numerator = jnp.dot(
                exponents.astype(jnp.bfloat16),
                window[:, head_size:],
                preferred_element_type=jnp.float32,
            )
            left = filled + head * head_size
            out[tile * ROW_TILE : (tile + 1) * ROW_TILE, left : left + head_size] = (
                numerator / denominator
            ).astype(out.dtype)


def attend(near, far, cosine, sine, first, keys_values, back, earlier):
    rows, width = near.shape
    head_size = cosine.shape[1]
    head_count = width // head_size
    full_width = width + sum(array.shape[1] for array in earlier)
    return pl.pallas_call(
        functools.partial(attend_kernel, back),
        out_shape=jax.ShapeDtypeStruct((rows, full_width), jnp.bfloat16),
        in_specs=vmem(6 + len(earlier)),
        out_specs=vmem(1)[0],
        scratch_shapes=[
            pltpu.VMEM((rows // ROW_TILE, head_count * ROW_TILE, head_size), jnp.bfloat16)
        ],
        compiler_params=pltpu.CompilerParams(vmem_limit_bytes=VMEM_LIMIT),
        cost_estimate=pl.CostEstimate(
            flops=4 * rows * width * (back + ROW_TILE),
            bytes_accessed=8 * rows * width,
            transcendentals=rows * head_count * (back + ROW_TILE),
        ),
    )(near, far, cosine, sine, first, keys_values, *earlier)


def shards(dp_size, ctx_size, tokens, w_query, w_key, w_value, doc_lengths):
    hidden = tokens[0]
    row_count = hidden.shape[0]
    depth, query_width = w_query.shape
    head_size = w_key.shape[1]
    chips = dp_size // 2
    bits = chips.bit_length() - 1
    me = lax.axis_index("dp")
    place = lax.axis_index("ctx")

    def swap(array, mask):
        return lax.ppermute(array, "dp", [(i, i ^ mask) for i in range(dp_size)])

    def fetch(pair, gates):
        held = ({0: pair[0]}, {0: pair[1]})
        for step in range(bits):
            axes = (step, bits - 1 - step)
            present = [sorted(held[side]) for side in range(2)]
            for sources in zip(*present):
                for side, source in enumerate(sources):
                    array = held[side][source]
                    if source == 0 and gates:
                        array = after(array, *gates[min(step, len(gates) - 1)])
                    held[side][source | (1 << axes[side])] = swap(array, 2 << axes[side])
        return held

    half = depth // 2
    middle = query_width // 2
    tops = [w_query[:half, :middle], w_query[:half, middle:]]
    bottoms = [w_query[half:, :middle], w_query[half:, middle:]]
    side_by_side = (
        (slice(None), slice(0, head_size)),
        (slice(None), slice(head_size, 2 * head_size)),
    )
    stacked = ((slice(0, half), slice(None)), (slice(half, depth), slice(None)))

    sibling_hidden = swap(hidden, 1)

    offset = place * row_count
    positions = offset + jnp.arange(row_count, dtype=jnp.int32)
    cosine, sine = rope_tables(positions, head_size)
    first = (doc_starts(doc_lengths[0], positions) - offset)[:, None]
    starts = jnp.stack([(me ^ (2 * chip)) * depth for chip in range(chips)]).astype(jnp.int32)

    first_axis, last_axis = 1, 1 << (bits - 1)

    def gates_of(held, *more):
        return (
            (held[0][last_axis], held[1][first_axis], *more),
            (held[0][chips - 1], held[1][chips - 1]),
        )

    def products(held, spots, *gates):
        order = list(range(chips))
        weights = [held[side][chip] for chip in order for side in range(2)]
        split = 2 * (chips - 1)
        carry = project(
            order[:-1], spots, depth, starts, hidden, sibling_hidden, weights[:split], None, False
        )
        if gates:
            carry = after(carry, *gates)
        near, far = project(
            order[-1:], spots, depth, starts, hidden, sibling_hidden, weights[split:], carry, True
        )
        return near, swap(far, 1)

    held_pair = fetch((w_key, w_value), None)
    held_low = fetch((tops[0], bottoms[0]), gates_of(held_pair))
    near, far = products(held_pair, side_by_side)
    pair = finish_pair(near, far, cosine, sine)
    held_high = fetch((tops[1], bottoms[1]), gates_of(held_low, pair))

    longest = ctx_size * row_count // 2
    back = -(-(longest - 1) // ROW_TILE) * ROW_TILE
    hops = min(ctx_size - 1, -(-back // row_count))
    blocks = [
        lax.ppermute(pair, "ctx", [(i, i + hop) for i in range(ctx_size - hop)])
        for hop in range(hops, 0, -1)
    ]
    keys_values = jnp.concatenate(blocks + [pair], axis=0)

    near, far = products(held_low, stacked)
    low = attend(near, far, cosine, sine, first, keys_values, back, [])
    near, far = products(held_high, stacked, low)
    return attend(near, far, cosine, sine, first, keys_values, back, [low])[None]


def solution(mesh):
    return jax.shard_map(
        functools.partial(shards, mesh.shape["dp"], mesh.shape["ctx"]),
        mesh=mesh,
        in_specs=(P("dp", "ctx", None), P("dp", None), P("dp", None), P("dp", None), P("dp", None)),
        out_specs=P("dp", "ctx", None),
        check_vma=False,
    )
```

```python
import functools
import math

import jax
import jax.numpy as jnp
from jax import lax
from jax.experimental import pallas as pl
from jax.experimental.pallas import tpu as pltpu
from jax.sharding import PartitionSpec as P

ROW_TILE = 128
MIB = 1024 * 1024


def rope_tables(positions, head_size):
    half_size = head_size // 2
    exponent = jnp.arange(half_size, dtype=jnp.float32) * (2.0 / head_size)
    inverse = jnp.power(jnp.float32(500000.0), -exponent)
    angles = positions.astype(jnp.float32)[:, None] * inverse[None, :]
    cosine = jnp.cos(angles)
    sine_part = jnp.sin(angles)
    return (
        jnp.concatenate([cosine, cosine], axis=-1),
        jnp.concatenate([-sine_part, sine_part], axis=-1),
    )


def doc_starts(doc_sizes, positions):
    doc_ends = jnp.cumsum(doc_sizes)
    doc_begin = doc_ends - doc_sizes
    chosen = jnp.where(doc_begin[None, :] <= positions[:, None], doc_begin[None, :], 0)
    return jnp.max(chosen, axis=1)


def vmem(count):
    return [pl.BlockSpec(memory_space=pltpu.VMEM)] * count


def anywhere(count):
    return [pl.BlockSpec(memory_space=pl.ANY)] * count


def after(array, *earlier):
    return lax.optimization_barrier((array, *earlier))[0]


def project_kernel(steps, carried, final, starts, near, far, *refs):
    count = sum(len(spots) for _, spots in steps)
    weights, refs = refs[:count], refs[count:]
    if carried:
        carry, refs = refs[0], refs[1:]
    outs = refs[: 2 if final else 1]
    refs = refs[len(outs) :]
    tokens, held, sems = refs[: len(steps)], refs[len(steps) : 2 * len(steps)], refs[-1]
    rows = near.shape[0]
    copies = []
    used = 0
    for step, (depth, spots) in enumerate(steps):
        window = pl.ds(pl.multiple_of(starts[step], 128), depth)
        batch = [
            pltpu.make_async_copy(near.at[:, window], tokens[step].at[:rows], sems.at[step, 0]),
            pltpu.make_async_copy(far.at[:, window], tokens[step].at[rows:], sems.at[step, 1]),
        ]
        for index, columns in enumerate(spots):
            batch.append(
                pltpu.make_async_copy(
                    weights[used], held[step].at[:, columns], sems.at[step, 2 + index]
                )
            )
            used += 1
        for copy in batch:
            copy.start()
        copies.append(batch)
    total = carry[...] if carried else None
    for step, batch in enumerate(copies):
        for copy in batch:
            copy.wait()
        term = jnp.dot(tokens[step][...], held[step][...], preferred_element_type=jnp.float32)
        total = term if total is None else total + term
    if final:
        outs[0][...] = total[:rows]
        outs[1][...] = total[rows:]
    else:
        outs[0][...] = total


def project(terms, near, far, carry=None, final=False):
    rows = near.shape[0]
    width = sum(array.shape[1] for array in terms[0][1])
    steps = []
    for _, arrays in terms:
        edges = [sum(array.shape[1] for array in arrays[:i]) for i in range(len(arrays) + 1)]
        spots = [slice(*edge) for edge in zip(edges[:-1], edges[1:])]
        steps.append((arrays[0].shape[0], spots))
    depth = sum(step[0] for step in steps)
    starts = jnp.stack([start for start, _ in terms]).astype(jnp.int32)
    weights = [array for _, arrays in terms for array in arrays]
    whole = jax.ShapeDtypeStruct((2 * rows, width), jnp.float32)
    part = jax.ShapeDtypeStruct((rows, width), jnp.float32)
    carries = [] if carry is None else [carry]
    need = 2 * depth * (2 * rows + width) + 16 * rows * width
    return pl.pallas_call(
        functools.partial(project_kernel, steps, carry is not None, final),
        out_shape=(part, part) if final else whole,
        in_specs=[pl.BlockSpec(memory_space=pltpu.SMEM)]
        + anywhere(2 + len(weights))
        + vmem(len(carries)),
        out_specs=tuple(vmem(2)) if final else vmem(1)[0],
        scratch_shapes=[pltpu.VMEM((2 * rows, step[0]), jnp.bfloat16) for step in steps]
        + [pltpu.VMEM((step[0], width), jnp.bfloat16) for step in steps]
        + [pltpu.SemaphoreType.DMA((len(steps), 4))],
        compiler_params=pltpu.CompilerParams(vmem_limit_bytes=need + 8 * MIB),
        cost_estimate=pl.CostEstimate(
            flops=4 * rows * width * depth,
            bytes_accessed=2 * depth * (2 * rows + width),
            transcendentals=0,
        ),
    )(starts, near, far, *weights, *carries)


def turn(vectors, cosine, sine):
    return vectors * cosine + pltpu.roll(vectors, vectors.shape[1] // 2, 1) * sine


def pair_kernel(near, far, cosine, sine, out):
    head_size = cosine.shape[1]
    pair = near[...] + far[...]
    out[:, :head_size] = turn(pair[:, :head_size], cosine[...], sine[...]).astype(out.dtype)
    out[:, head_size:] = pair[:, head_size:].astype(out.dtype)


def finish_pair(near, far, cosine, sine):
    return pl.pallas_call(
        pair_kernel,
        out_shape=jax.ShapeDtypeStruct(near.shape, jnp.bfloat16),
        in_specs=vmem(4),
        out_specs=vmem(1)[0],
        compiler_params=pltpu.CompilerParams(vmem_limit_bytes=8 * MIB),
        cost_estimate=pl.CostEstimate(
            flops=6 * near.size, bytes_accessed=14 * near.size, transcendentals=0
        ),
    )(near, far, cosine, sine)


def attend_kernel(back, near, far, cosine, sine, first, keys_values, out, rotated):
    rows, head_size = cosine.shape
    head_count = near.shape[1] // head_size
    base = keys_values.shape[0] - rows
    tiles = rows // ROW_TILE
    for head in range(head_count):
        columns = slice(head * head_size, (head + 1) * head_size)
        turned = turn(near[:, columns] + far[:, columns], cosine[...], sine[...])
        turned = turned.astype(jnp.bfloat16)
        for tile in range(tiles):
            rotated[tile, head * ROW_TILE : (head + 1) * ROW_TILE, :] = turned[
                tile * ROW_TILE : (tile + 1) * ROW_TILE
            ]
    scale = jnp.float32(math.log2(math.e) / math.sqrt(head_size))
    for tile in range(tiles):
        begin = base + tile * ROW_TILE - back
        window = keys_values[begin : begin + back + ROW_TILE, :]
        scores = lax.dot_general(
            rotated[tile],
            window[:, :head_size],
            (((1,), (1,)), ((), ())),
            preferred_element_type=jnp.float32,
        )
        shape = (ROW_TILE, back + ROW_TILE)
        key_place = lax.broadcasted_iota(jnp.int32, shape, 1) + (tile * ROW_TILE - back)
        row_place = lax.broadcasted_iota(jnp.int32, shape, 0) + tile * ROW_TILE
        lower = first[tile * ROW_TILE : (tile + 1) * ROW_TILE, :]
        allowed = (key_place <= row_place) & (key_place >= lower)
        for head in range(head_count):
            part = scores[head * ROW_TILE : (head + 1) * ROW_TILE]
            part = jnp.where(allowed, part, jnp.float32(-1e30))
            largest = jnp.max(part, axis=-1, keepdims=True)
            exponents = jnp.exp2((part - largest) * scale)
            denominator = jnp.sum(exponents, axis=-1, keepdims=True)
            numerator = jnp.dot(
                exponents.astype(jnp.bfloat16),
                window[:, head_size:],
                preferred_element_type=jnp.float32,
            )
            left = head * head_size
            out[tile * ROW_TILE : (tile + 1) * ROW_TILE, left : left + head_size] = (
                numerator / denominator
            ).astype(out.dtype)


def attend(near, far, cosine, sine, first, keys_values, back):
    rows, width = near.shape
    head_size = cosine.shape[1]
    head_count = width // head_size
    window = back + ROW_TILE
    return pl.pallas_call(
        functools.partial(attend_kernel, back),
        out_shape=jax.ShapeDtypeStruct((rows, width), jnp.bfloat16),
        in_specs=vmem(6),
        out_specs=vmem(1)[0],
        scratch_shapes=[
            pltpu.VMEM((rows // ROW_TILE, head_count * ROW_TILE, head_size), jnp.bfloat16)
        ],
        compiler_params=pltpu.CompilerParams(
            vmem_limit_bytes=8 * MIB + 24 * head_count * ROW_TILE * window
        ),
        cost_estimate=pl.CostEstimate(
            flops=4 * rows * width * window,
            bytes_accessed=8 * rows * width,
            transcendentals=rows * head_count * window,
        ),
    )(near, far, cosine, sine, first, keys_values)


def shards(dp_size, ctx_size, tokens, w_query, w_key, w_value, doc_lengths):
    hidden = tokens[0]
    row_count = hidden.shape[0]
    depth, query_width = w_query.shape
    head_size = w_key.shape[1]
    chips = dp_size // 2
    bits = chips.bit_length() - 1
    me = lax.axis_index("dp")
    place = lax.axis_index("ctx")

    def swap(array, mask):
        return lax.ppermute(array, "dp", [(i, i ^ mask) for i in range(dp_size)])

    def fetch(pair, gates, assisted):
        held = [{0: [(0, array)]} for array in pair]
        for step in range(bits):
            axes = (step, bits - 1 - step)
            for sources in zip(*[sorted(side) for side in held]):
                for side, source in enumerate(sources):
                    array = held[side][source][0][1]
                    mask = 2 << axes[side]
                    if source == 0 and gates:
                        array = after(array, *gates[min(step, len(gates) - 1)])
                    if source == 0 and assisted and step == bits - 1:
                        some = array.shape[0] // 2
                        begin = (place % 2) * some
                        mine = swap(lax.dynamic_slice_in_dim(array, begin, some, 0), mask)
                        other = lax.ppermute(mine, "ctx", [(i, i ^ 1) for i in range(ctx_size)])
                        got = [(begin, mine), (some - begin, other)]
                    else:
                        got = [(0, swap(array, mask))]
                    held[side][source | (1 << axes[side])] = got
        return held

    sibling_hidden = swap(hidden, 1)

    offset = place * row_count
    positions = offset + jnp.arange(row_count, dtype=jnp.int32)
    cosine, sine = rope_tables(positions, head_size)
    first = (doc_starts(doc_lengths[0], positions) - offset)[:, None]

    def begins(chip):
        return (me ^ (2 * chip)) * depth

    first_axis, last_axis = 1, 1 << (bits - 1)
    last = chips - 1

    pair_held = fetch((w_key, w_value), None, False)
    pair_terms = [
        (begins(chip), [pair_held[side][chip][0][1] for side in range(2)]) for chip in range(chips)
    ]
    carry = project(pair_terms[:-1], hidden, sibling_hidden)
    gates = (
        [pair_held[0][last_axis][0][1], pair_held[1][first_axis][0][1]],
        [pair_held[0][last][0][1], pair_held[1][last][0][1], carry],
    )
    half = depth // 2
    query_held = fetch((w_query[:half], w_query[half:]), gates, ctx_size % 2 == 0)

    near, far = project(pair_terms[-1:], hidden, sibling_hidden, carry, True)
    pair = finish_pair(near, swap(far, 1), cosine, sine)
    longest = ctx_size * row_count // 2
    back = -(-(longest - 1) // ROW_TILE) * ROW_TILE
    hops = min(ctx_size - 1, -(-back // row_count))
    blocks = [
        lax.ppermute(pair, "ctx", [(i, i + hop) for i in range(ctx_size - hop)])
        for hop in range(hops, 0, -1)
    ]
    keys_values = jnp.concatenate(blocks + [pair], axis=0)

    def query_terms(wanted):
        return [
            (begins(chip) + side * half + begin, [array])
            for side, chip in wanted
            for begin, array in query_held[side][chip]
        ]

    early = [(0, 0), (1, 0), (0, first_axis), (1, last_axis)]
    late = [(0, last), (1, last)]
    rest = [
        (side, chip)
        for chip in range(chips)
        for side in range(2)
        if (side, chip) not in early + late
    ]
    carry = after(project(query_terms(early), hidden, sibling_hidden), pair)
    carry = project(query_terms(rest), hidden, sibling_hidden, carry)
    near, far = project(query_terms(late), hidden, sibling_hidden, carry, True)
    return attend(near, swap(far, 1), cosine, sine, first, keys_values, back)[None]


def solution(mesh):
    return jax.shard_map(
        functools.partial(shards, mesh.shape["dp"], mesh.shape["ctx"]),
        mesh=mesh,
        in_specs=(P("dp", "ctx", None), P("dp", None), P("dp", None), P("dp", None), P("dp", None)),
        out_specs=P("dp", "ctx", None),
        check_vma=False,
    )
```

```python
import functools
import math

import jax
import jax.numpy as jnp
from jax import lax
from jax.experimental import pallas as pl
from jax.experimental.pallas import tpu as pltpu
from jax.sharding import PartitionSpec as P

ROW_TILE = 128
MIB = 1024 * 1024


def rope_tables(positions, head_size):
    half_size = head_size // 2
    exponent = jnp.arange(half_size, dtype=jnp.float32) * (2.0 / head_size)
    inverse = jnp.power(jnp.float32(500000.0), -exponent)
    angles = positions.astype(jnp.float32)[:, None] * inverse[None, :]
    cosine = jnp.cos(angles)
    sine_part = jnp.sin(angles)
    return (
        jnp.concatenate([cosine, cosine], axis=-1),
        jnp.concatenate([-sine_part, sine_part], axis=-1),
    )


def doc_starts(doc_sizes, positions):
    doc_ends = jnp.cumsum(doc_sizes)
    doc_begin = doc_ends - doc_sizes
    chosen = jnp.where(doc_begin[None, :] <= positions[:, None], doc_begin[None, :], 0)
    return jnp.max(chosen, axis=1)


def vmem(count):
    return [pl.BlockSpec(memory_space=pltpu.VMEM)] * count


def anywhere(count):
    return [pl.BlockSpec(memory_space=pl.ANY)] * count


def after(array, *earlier):
    return lax.optimization_barrier((array, *earlier))[0]


def project_kernel(steps, carried, final, starts, near, far, *refs):
    count = sum(len(spots) for _, spots in steps)
    weights, refs = refs[:count], refs[count:]
    if carried:
        carry, refs = refs[0], refs[1:]
    outs, (tokens, held, sems) = refs[:-3], refs[-3:]
    rows = near.shape[0]
    batches = ([], [], [])
    used = row = 0
    for step, (depth, spots) in enumerate(steps):
        here = slice(row, row + depth)
        row += depth
        window = pl.ds(pl.multiple_of(starts[step], 128), depth)
        for index, columns in enumerate(spots):
            batches[0].append(
                pltpu.make_async_copy(
                    weights[used], held.at[here, columns], sems.at[step, 2 + index]
                )
            )
            used += 1
        for side, ref in enumerate((far, near)):
            batches[1 + side].append(
                pltpu.make_async_copy(
                    ref.at[:, window], tokens.at[side, :, here], sems.at[step, side]
                )
            )
    for batch in batches:
        for copy in batch:
            copy.start()
    for copy in batches[0]:
        copy.wait()
    for side in range(2):
        for copy in batches[1 + side]:
            copy.wait()
        total = jnp.dot(tokens[side], held[...], preferred_element_type=jnp.float32)
        place = slice((1 - side) * rows, (2 - side) * rows)
        if carried:
            total = total + carry[place, :]
        if final:
            outs[1 - side][...] = total
        else:
            outs[0][place, :] = total


def project(terms, near, far, carry=None, final=False):
    rows = near.shape[0]
    width = sum(array.shape[1] for array in terms[0][1])
    steps = []
    for _, arrays in terms:
        edges = [sum(array.shape[1] for array in arrays[:i]) for i in range(len(arrays) + 1)]
        spots = [slice(*edge) for edge in zip(edges[:-1], edges[1:])]
        steps.append((arrays[0].shape[0], spots))
    depth = sum(step[0] for step in steps)
    starts = jnp.stack([start for start, _ in terms]).astype(jnp.int32)
    weights = [array for _, arrays in terms for array in arrays]
    whole = jax.ShapeDtypeStruct((2 * rows, width), jnp.float32)
    part = jax.ShapeDtypeStruct((rows, width), jnp.float32)
    carries = [] if carry is None else [carry]
    return pl.pallas_call(
        functools.partial(project_kernel, steps, carry is not None, final),
        out_shape=(part, part) if final else whole,
        in_specs=[pl.BlockSpec(memory_space=pltpu.SMEM)]
        + anywhere(2 + len(weights))
        + vmem(len(carries)),
        out_specs=tuple(vmem(2)) if final else vmem(1)[0],
        scratch_shapes=[
            pltpu.VMEM((2, rows, depth), jnp.bfloat16),
            pltpu.VMEM((depth, width), jnp.bfloat16),
            pltpu.SemaphoreType.DMA((len(steps), 4)),
        ],
        compiler_params=pltpu.CompilerParams(vmem_limit_bytes=48 * MIB),
        cost_estimate=pl.CostEstimate(
            flops=4 * rows * width * depth,
            bytes_accessed=2 * depth * (2 * rows + width),
            transcendentals=0,
        ),
    )(starts, near, far, *weights, *carries)


def turn(vectors, cosine, sine):
    return vectors * cosine + pltpu.roll(vectors, vectors.shape[1] // 2, 1) * sine


def pair_kernel(near, far, cosine, sine, out):
    head_size = cosine.shape[1]
    pair = near[...] + far[...]
    out[:, :head_size] = turn(pair[:, :head_size], cosine[...], sine[...]).astype(out.dtype)
    out[:, head_size:] = pair[:, head_size:].astype(out.dtype)


def finish_pair(near, far, cosine, sine):
    return pl.pallas_call(
        pair_kernel,
        out_shape=jax.ShapeDtypeStruct(near.shape, jnp.bfloat16),
        in_specs=vmem(4),
        out_specs=vmem(1)[0],
        compiler_params=pltpu.CompilerParams(vmem_limit_bytes=8 * MIB),
        cost_estimate=pl.CostEstimate(
            flops=6 * near.size, bytes_accessed=14 * near.size, transcendentals=0
        ),
    )(near, far, cosine, sine)


def attend_kernel(back, near, far, cosine, sine, first, keys_values, out, rotated):
    rows, head_size = cosine.shape
    head_count = near.shape[1] // head_size
    base = keys_values.shape[0] - rows
    tiles = rows // ROW_TILE
    for head in range(head_count):
        columns = slice(head * head_size, (head + 1) * head_size)
        turned = turn(near[:, columns] + far[:, columns], cosine[...], sine[...])
        turned = turned.astype(jnp.bfloat16)
        for tile in range(tiles):
            rotated[tile, head * ROW_TILE : (head + 1) * ROW_TILE, :] = turned[
                tile * ROW_TILE : (tile + 1) * ROW_TILE
            ]
    scale = jnp.float32(math.log2(math.e) / math.sqrt(head_size))
    for tile in range(tiles):
        begin = base + tile * ROW_TILE - back
        window = keys_values[begin : begin + back + ROW_TILE, :]
        scores = lax.dot_general(
            rotated[tile],
            window[:, :head_size],
            (((1,), (1,)), ((), ())),
            preferred_element_type=jnp.float32,
        )
        shape = (ROW_TILE, back + ROW_TILE)
        key_place = lax.broadcasted_iota(jnp.int32, shape, 1) + (tile * ROW_TILE - back)
        row_place = lax.broadcasted_iota(jnp.int32, shape, 0) + tile * ROW_TILE
        lower = first[tile * ROW_TILE : (tile + 1) * ROW_TILE, :]
        allowed = (key_place <= row_place) & (key_place >= lower)
        for head in range(head_count):
            part = scores[head * ROW_TILE : (head + 1) * ROW_TILE]
            part = jnp.where(allowed, part, jnp.float32(-1e30))
            largest = jnp.max(part, axis=-1, keepdims=True)
            exponents = jnp.exp2((part - largest) * scale)
            denominator = jnp.sum(exponents, axis=-1, keepdims=True)
            numerator = jnp.dot(
                exponents.astype(jnp.bfloat16),
                window[:, head_size:],
                preferred_element_type=jnp.float32,
            )
            left = head * head_size
            out[tile * ROW_TILE : (tile + 1) * ROW_TILE, left : left + head_size] = (
                numerator / denominator
            ).astype(out.dtype)


def attend(near, far, cosine, sine, first, keys_values, back):
    rows, width = near.shape
    head_size = cosine.shape[1]
    head_count = width // head_size
    window = back + ROW_TILE
    return pl.pallas_call(
        functools.partial(attend_kernel, back),
        out_shape=jax.ShapeDtypeStruct((rows, width), jnp.bfloat16),
        in_specs=vmem(6),
        out_specs=vmem(1)[0],
        scratch_shapes=[
            pltpu.VMEM((rows // ROW_TILE, head_count * ROW_TILE, head_size), jnp.bfloat16)
        ],
        compiler_params=pltpu.CompilerParams(
            vmem_limit_bytes=8 * MIB + 24 * head_count * ROW_TILE * window
        ),
        cost_estimate=pl.CostEstimate(
            flops=4 * rows * width * window,
            bytes_accessed=8 * rows * width,
            transcendentals=rows * head_count * window,
        ),
    )(near, far, cosine, sine, first, keys_values)


def shards(dp_size, ctx_size, tokens, w_query, w_key, w_value, doc_lengths):
    hidden = tokens[0]
    row_count = hidden.shape[0]
    depth, query_width = w_query.shape
    head_size = w_key.shape[1]
    chips = dp_size // 2
    bits = chips.bit_length() - 1
    me = lax.axis_index("dp")
    place = lax.axis_index("ctx")

    def swap(array, mask):
        return lax.ppermute(array, "dp", [(i, i ^ mask) for i in range(dp_size)])

    def fetch(pair, gate, later, seconds):
        held = [{0: [(0, array)]} for array in pair]
        for step in range(bits):
            axes = (step, bits - 1 - step)
            for sources in zip(*[sorted(side) for side in held]):
                for side, source in enumerate(sources):
                    array = held[side][source][0][1]
                    mask = 2 << axes[side]
                    if source == 0 and step == bits - 1 and seconds:
                        got = seconds[side]
                    else:
                        array = after(array, *(gate if source == 0 else later))
                        got = [(0, swap(array, mask))]
                    held[side][source | (1 << axes[side])] = got
        return held

    sibling_hidden = swap(hidden, 1)

    offset = place * row_count
    positions = offset + jnp.arange(row_count, dtype=jnp.int32)
    cosine, sine = rope_tables(positions, head_size)
    first = (doc_starts(doc_lengths[0], positions) - offset)[:, None]

    def begins(chip):
        return (me ^ (2 * chip)) * depth

    first_axis, last_axis = 1, 1 << (bits - 1)
    last = chips - 1

    half = depth // 2
    halves = [w_query[:half], w_query[half:]]
    parts = []
    if ctx_size % 2 == 0:
        begin = (place % 2) * (half // 2)
        parts = [
            lax.dynamic_slice_in_dim(w_query, side * half + begin, half // 2, 0)
            for side in range(2)
        ]

    pair_held = fetch((w_key, w_value), [], [], [])
    pair_terms = [
        (begins(chip), [pair_held[side][chip][0][1] for side in range(2)]) for chip in range(chips)
    ]
    carry = project(pair_terms[:-1], hidden, sibling_hidden)
    near, far = project(pair_terms[-1:], hidden, sibling_hidden, carry, True)
    gate = [pair_held[0][last_axis][0][1], pair_held[1][first_axis][0][1]]
    gate += [cosine, sine, first, *halves, *parts]
    mine = [swap(after(part, *gate), 2 << axis) for part, axis in zip(parts, (bits - 1, 0))]
    other = [lax.ppermute(part, "ctx", [(i, i ^ 1) for i in range(ctx_size)]) for part in mine]
    seconds = [
        [(begin, here), (half // 2 - begin, there)] for here, there in zip(mine, other)
    ]
    query_held = fetch(halves, gate, [near, *mine], seconds)

    pair = finish_pair(near, swap(far, 1), cosine, sine)
    longest = ctx_size * row_count // 2
    back = -(-(longest - 1) // ROW_TILE) * ROW_TILE
    hops = min(ctx_size - 1, -(-back // row_count))
    blocks = [
        lax.ppermute(after(pair, *other), "ctx", [(i, i + hop) for i in range(ctx_size - hop)])
        for hop in range(hops, 0, -1)
    ]
    keys_values = jnp.concatenate(blocks + [pair], axis=0)

    def query_terms(wanted, *gate):
        return [
            (begins(chip) + side * half + begin, [after(array, *gate)])
            for side, chip in wanted
            for begin, array in query_held[side][chip]
        ]

    late = [(0, last), (1, last)]
    early = [(side, chip) for chip in range(last) for side in range(2)]
    carry = project(query_terms(early, pair), hidden, sibling_hidden)
    near, far = project(query_terms(late, keys_values), hidden, sibling_hidden, carry, True)
    return attend(near, swap(far, 1), cosine, sine, first, keys_values, back)[None]


def solution(mesh):
    return jax.shard_map(
        functools.partial(shards, mesh.shape["dp"], mesh.shape["ctx"]),
        mesh=mesh,
        in_specs=(P("dp", "ctx", None), P("dp", None), P("dp", None), P("dp", None), P("dp", None)),
        out_specs=P("dp", "ctx", None),
        check_vma=False,
    )
```

```python
import functools
import math

import jax
import jax.numpy as jnp
from jax import lax
from jax.experimental import pallas as pl
from jax.experimental.pallas import tpu as pltpu
from jax.sharding import PartitionSpec as P

ROW_TILE = 128
MIB = 1024 * 1024


def rope_tables(positions, head_size):
    half_size = head_size // 2
    exponent = jnp.arange(half_size, dtype=jnp.float32) * (2.0 / head_size)
    inverse = jnp.power(jnp.float32(500000.0), -exponent)
    angles = positions.astype(jnp.float32)[:, None] * inverse[None, :]
    cosine = jnp.cos(angles)
    sine_part = jnp.sin(angles)
    return (
        jnp.concatenate([cosine, cosine], axis=-1),
        jnp.concatenate([-sine_part, sine_part], axis=-1),
    )


def doc_starts(doc_sizes, positions):
    doc_ends = jnp.cumsum(doc_sizes)
    doc_begin = doc_ends - doc_sizes
    chosen = jnp.where(doc_begin[None, :] <= positions[:, None], doc_begin[None, :], 0)
    return jnp.max(chosen, axis=1)


def vmem(count):
    return [pl.BlockSpec(memory_space=pltpu.VMEM)] * count


def anywhere(count):
    return [pl.BlockSpec(memory_space=pl.ANY)] * count


def after(array, *earlier):
    return lax.optimization_barrier((array, *earlier))[0]


def pack_kernel(begin, key, value, query, *refs):
    pair, top, bottom = refs[:3]
    parts, sems = refs[3:-1], refs[-1]
    head_size = key.shape[1]
    half = top.shape[0]
    copies = []
    for side, part in enumerate(parts):
        rows = pl.ds(pl.multiple_of(side * half + begin[0], 16), part.shape[0])
        copies.append((query.at[rows], part))
    copies += [
        (key, pair.at[:, :head_size]),
        (value, pair.at[:, head_size:]),
        (query.at[:half], top),
        (query.at[half:], bottom),
    ]
    copies = [pltpu.make_async_copy(*copy, sems.at[i]) for i, copy in enumerate(copies)]
    for copy in copies:
        copy.start()
    for copy in copies:
        copy.wait()


def pack(begin, key, value, query, halved):
    depth, width = query.shape
    shapes = [(depth, 2 * key.shape[1])] + [(depth // 2, width)] * 2
    shapes += [(depth // 4, width)] * (2 if halved else 0)
    return pl.pallas_call(
        pack_kernel,
        out_shape=[jax.ShapeDtypeStruct(shape, query.dtype) for shape in shapes],
        in_specs=[pl.BlockSpec(memory_space=pltpu.SMEM)] + anywhere(3),
        out_specs=anywhere(len(shapes)),
        scratch_shapes=[pltpu.SemaphoreType.DMA((6,))],
        compiler_params=pltpu.CompilerParams(vmem_limit_bytes=48 * MIB),
        cost_estimate=pl.CostEstimate(
            flops=0, bytes_accessed=8 * query.size, transcendentals=0
        ),
    )(begin, key, value, query)


def project_kernel(steps, carried, final, starts, near, far, *refs):
    weights, refs = refs[: len(steps)], refs[len(steps) :]
    if carried:
        carry, refs = refs[0], refs[1:]
    outs, (tokens, held, sems) = refs[:-3], refs[-3:]
    rows = near.shape[0]
    batches = ([], [], [])
    row = 0
    for step, depth in enumerate(steps):
        here = slice(row, row + depth)
        row += depth
        window = pl.ds(pl.multiple_of(starts[step], 128), depth)
        batches[0].append(
            pltpu.make_async_copy(weights[step], held.at[here], sems.at[step, 2])
        )
        for side, ref in enumerate((far, near)):
            batches[1 + side].append(
                pltpu.make_async_copy(
                    ref.at[:, window], tokens.at[side, :, here], sems.at[step, side]
                )
            )
    for batch in batches:
        for copy in batch:
            copy.start()
    for copy in batches[0]:
        copy.wait()
    for side in range(2):
        for copy in batches[1 + side]:
            copy.wait()
        total = jnp.dot(tokens[side], held[...], preferred_element_type=jnp.float32)
        place = slice((1 - side) * rows, (2 - side) * rows)
        if carried:
            total = total + carry[place, :]
        if final:
            outs[1 - side][...] = total
        else:
            outs[0][place, :] = total


def project(terms, near, far, carry=None, final=False):
    rows = near.shape[0]
    width = terms[0][1].shape[1]
    steps = [array.shape[0] for _, array in terms]
    depth = sum(steps)
    starts = jnp.stack([start for start, _ in terms]).astype(jnp.int32)
    whole = jax.ShapeDtypeStruct((2 * rows, width), jnp.float32)
    part = jax.ShapeDtypeStruct((rows, width), jnp.float32)
    carries = [] if carry is None else [carry]
    return pl.pallas_call(
        functools.partial(project_kernel, steps, carry is not None, final),
        out_shape=(part, part) if final else whole,
        in_specs=[pl.BlockSpec(memory_space=pltpu.SMEM)]
        + anywhere(2 + len(terms))
        + vmem(len(carries)),
        out_specs=tuple(vmem(2)) if final else vmem(1)[0],
        scratch_shapes=[
            pltpu.VMEM((2, rows, depth), jnp.bfloat16),
            pltpu.VMEM((depth, width), jnp.bfloat16),
            pltpu.SemaphoreType.DMA((len(steps), 3)),
        ],
        compiler_params=pltpu.CompilerParams(vmem_limit_bytes=48 * MIB),
        cost_estimate=pl.CostEstimate(
            flops=4 * rows * width * depth,
            bytes_accessed=2 * depth * (2 * rows + width),
            transcendentals=0,
        ),
    )(starts, near, far, *[array for _, array in terms], *carries)


def turn(vectors, cosine, sine):
    return vectors * cosine + pltpu.roll(vectors, vectors.shape[1] // 2, 1) * sine


def pair_kernel(near, far, cosine, sine, out):
    head_size = cosine.shape[1]
    pair = near[...] + far[...]
    out[:, :head_size] = turn(pair[:, :head_size], cosine[...], sine[...]).astype(out.dtype)
    out[:, head_size:] = pair[:, head_size:].astype(out.dtype)


def finish_pair(near, far, cosine, sine):
    return pl.pallas_call(
        pair_kernel,
        out_shape=jax.ShapeDtypeStruct(near.shape, jnp.bfloat16),
        in_specs=vmem(4),
        out_specs=vmem(1)[0],
        compiler_params=pltpu.CompilerParams(vmem_limit_bytes=8 * MIB),
        cost_estimate=pl.CostEstimate(
            flops=6 * near.size, bytes_accessed=14 * near.size, transcendentals=0
        ),
    )(near, far, cosine, sine)


def attend_kernel(back, near, far, cosine, sine, first, keys_values, out, rotated):
    rows, head_size = cosine.shape
    head_count = near.shape[1] // head_size
    base = keys_values.shape[0] - rows
    tiles = rows // ROW_TILE
    for head in range(head_count):
        columns = slice(head * head_size, (head + 1) * head_size)
        turned = turn(near[:, columns] + far[:, columns], cosine[...], sine[...])
        turned = turned.astype(jnp.bfloat16)
        for tile in range(tiles):
            rotated[tile, head * ROW_TILE : (head + 1) * ROW_TILE, :] = turned[
                tile * ROW_TILE : (tile + 1) * ROW_TILE
            ]
    scale = jnp.float32(math.log2(math.e) / math.sqrt(head_size))
    for tile in range(tiles):
        begin = base + tile * ROW_TILE - back
        window = keys_values[begin : begin + back + ROW_TILE, :]
        scores = lax.dot_general(
            rotated[tile],
            window[:, :head_size],
            (((1,), (1,)), ((), ())),
            preferred_element_type=jnp.float32,
        )
        shape = (ROW_TILE, back + ROW_TILE)
        key_place = lax.broadcasted_iota(jnp.int32, shape, 1) + (tile * ROW_TILE - back)
        row_place = lax.broadcasted_iota(jnp.int32, shape, 0) + tile * ROW_TILE
        lower = first[tile * ROW_TILE : (tile + 1) * ROW_TILE, :]
        allowed = (key_place <= row_place) & (key_place >= lower)
        for head in range(head_count):
            part = scores[head * ROW_TILE : (head + 1) * ROW_TILE]
            part = jnp.where(allowed, part, jnp.float32(-1e30))
            largest = jnp.max(part, axis=-1, keepdims=True)
            exponents = jnp.exp2((part - largest) * scale)
            denominator = jnp.sum(exponents, axis=-1, keepdims=True)
            numerator = jnp.dot(
                exponents.astype(jnp.bfloat16),
                window[:, head_size:],
                preferred_element_type=jnp.float32,
            )
            left = head * head_size
            out[tile * ROW_TILE : (tile + 1) * ROW_TILE, left : left + head_size] = (
                numerator / denominator
            ).astype(out.dtype)


def attend(near, far, cosine, sine, first, keys_values, back):
    rows, width = near.shape
    head_size = cosine.shape[1]
    head_count = width // head_size
    window = back + ROW_TILE
    return pl.pallas_call(
        functools.partial(attend_kernel, back),
        out_shape=jax.ShapeDtypeStruct((rows, width), jnp.bfloat16),
        in_specs=vmem(6),
        out_specs=vmem(1)[0],
        scratch_shapes=[
            pltpu.VMEM((rows // ROW_TILE, head_count * ROW_TILE, head_size), jnp.bfloat16)
        ],
        compiler_params=pltpu.CompilerParams(
            vmem_limit_bytes=8 * MIB + 24 * head_count * ROW_TILE * window
        ),
        cost_estimate=pl.CostEstimate(
            flops=4 * rows * width * window,
            bytes_accessed=8 * rows * width,
            transcendentals=rows * head_count * window,
        ),
    )(near, far, cosine, sine, first, keys_values)


def shards(dp_size, ctx_size, tokens, w_query, w_key, w_value, doc_lengths):
    hidden = tokens[0]
    row_count = hidden.shape[0]
    depth, query_width = w_query.shape
    head_size = w_key.shape[1]
    chips = dp_size // 2
    bits = chips.bit_length() - 1
    me = lax.axis_index("dp")
    place = lax.axis_index("ctx")

    def swap(array, mask):
        return lax.ppermute(array, "dp", [(i, i ^ mask) for i in range(dp_size)])

    def fetch(pair, given, gate, later):
        held = []
        for side, array in enumerate(pair):
            pieces = {0: [(0, array)], **given[side]}
            reached = [0]
            for axis in list(range(bits))[:: 1 - 2 * side]:
                for source in list(reached):
                    target = source | (1 << axis)
                    reached.append(target)
                    if target not in pieces:
                        sent = after(pieces[source][0][1], *(later if source else gate))
                        pieces[target] = [(0, swap(sent, 2 << axis))]
            held.append(pieces)
        return held

    sibling_hidden = swap(hidden, 1)

    offset = place * row_count
    positions = offset + jnp.arange(row_count, dtype=jnp.int32)
    cosine, sine = rope_tables(positions, head_size)
    first = (doc_starts(doc_lengths[0], positions) - offset)[:, None]

    axes = [1 << axis for axis in range(bits)]

    def begins(chip):
        return (me ^ (2 * chip)) * depth

    half = depth // 2
    halved = ctx_size % 2 == 0
    some = half // 2
    begin = (place % 2) * some
    packed = pack(begin[None], w_key, w_value, w_query, halved)
    pair_here, halves, parts = packed[0], packed[1:3], packed[3:]

    given = [{}, {}]
    mine = [swap(part, 2 << axis) for part, axis in zip(parts, (bits - 1, 0))]
    if halved:
        both = jnp.concatenate(mine, axis=0)
        both = lax.ppermute(both, "ctx", [(i, i ^ 1) for i in range(ctx_size)])
        given = [
            {1 << axis: [(begin, mine[side]), (some - begin, both[side * some : side * some + some])]}
            for side, axis in enumerate((bits - 1, 0))
        ]
    pairs = [pair_here] + [swap(pair_here, 2 << axis) for axis in range(bits)]
    sides = [slice(0, half), slice(half, depth)]
    pair_held = fetch(
        [pair_here[rows] for rows in sides],
        [{1 << axis: [(0, pairs[1 + axis][rows])] for axis in range(bits)} for rows in sides],
        [],
        [],
    )
    pair_terms = [(begins(chip), array) for chip, array in zip([0] + axes, pairs)]
    carry = project(pair_terms, hidden, sibling_hidden)
    pair_terms = [
        (begins(chip) + side * half, pair_held[side][chip][0][1])
        for chip in range(chips)
        if chip not in [0] + axes
        for side in range(2)
    ]
    near, far = project(pair_terms, hidden, sibling_hidden, carry, True)
    query_held = fetch(halves, given, [*mine, cosine, sine, first], [near])

    pair = finish_pair(near, swap(far, 1), cosine, sine)
    longest = ctx_size * row_count // 2
    back = -(-(longest - 1) // ROW_TILE) * ROW_TILE
    hops = min(ctx_size - 1, -(-back // row_count))
    blocks = [
        lax.ppermute(after(pair, both) if halved else pair, "ctx", [(i, i + hop) for i in range(ctx_size - hop)])
        for hop in range(hops, 0, -1)
    ]
    keys_values = jnp.concatenate(blocks + [pair], axis=0)

    def query_terms(wanted, *gate):
        return [
            (begins(chip) + side * half + row, after(array, *gate))
            for side, chip in wanted
            for row, array in query_held[side][chip]
        ]

    everything = [(side, chip) for chip in range(chips) for side in range(2)]
    early = [(side, chip) for side, chip in everything if chip in [0] + axes]
    late = [wanted for wanted in everything if wanted not in early]
    carry = project(query_terms(early, pair), hidden, sibling_hidden)
    near, far = project(query_terms(late, keys_values), hidden, sibling_hidden, carry, True)
    return attend(near, swap(far, 1), cosine, sine, first, keys_values, back)[None]


def solution(mesh):
    return jax.shard_map(
        functools.partial(shards, mesh.shape["dp"], mesh.shape["ctx"]),
        mesh=mesh,
        in_specs=(P("dp", "ctx", None), P("dp", None), P("dp", None), P("dp", None), P("dp", None)),
        out_specs=P("dp", "ctx", None),
        check_vma=False,
    )
```

```python
import functools
import math

import jax
import jax.numpy as jnp
from jax import lax
from jax.experimental import pallas as pl
from jax.experimental.pallas import tpu as pltpu
from jax.sharding import PartitionSpec as P

ROW_TILE = 128
MIB = 1024 * 1024


def rope_tables(positions, head_size):
    half_size = head_size // 2
    exponent = jnp.arange(half_size, dtype=jnp.float32) * (2.0 / head_size)
    inverse = jnp.power(jnp.float32(500000.0), -exponent)
    angles = positions.astype(jnp.float32)[:, None] * inverse[None, :]
    cosine = jnp.cos(angles)
    sine_part = jnp.sin(angles)
    return (
        jnp.concatenate([cosine, cosine], axis=-1),
        jnp.concatenate([-sine_part, sine_part], axis=-1),
    )


def doc_starts(doc_sizes, positions):
    doc_ends = jnp.cumsum(doc_sizes)
    doc_begin = doc_ends - doc_sizes
    chosen = jnp.where(doc_begin[None, :] <= positions[:, None], doc_begin[None, :], 0)
    return jnp.max(chosen, axis=1)


def vmem(count):
    return [pl.BlockSpec(memory_space=pltpu.VMEM)] * count


def in_hbm(count):
    return [pl.BlockSpec(memory_space=pltpu.HBM)] * count


def after(array, *earlier):
    return lax.optimization_barrier((array, *earlier))[0]


def copy_all(copies, sems):
    copies = [pltpu.make_async_copy(*copy, sems.at[i]) for i, copy in enumerate(copies)]
    for copy in copies:
        copy.start()
    for copy in copies:
        copy.wait()


def halves_kernel(begin, query, *refs):
    parts, sems = refs[:-1], refs[-1]
    copies = []
    for side, part in enumerate(parts):
        row = side * query.shape[0] // 2 + begin[0]
        copies.append((query.at[pl.ds(pl.multiple_of(row, 16), part.shape[0])], part))
    copy_all(copies, sems)


def pack_kernel(starts, key, value, query, tokens, pair, top, bottom, columns, sems):
    head_size = key.shape[1]
    half, depth = top.shape[0], query.shape[0]
    copies = [
        (key, pair.at[:, :head_size]),
        (value, pair.at[:, head_size:]),
        (query.at[:half], top),
        (query.at[half:], bottom),
    ]
    for chip in range(columns.shape[1] // depth):
        window = pl.ds(pl.multiple_of(starts[chip], 128), depth)
        copies.append((tokens.at[:, window], columns.at[:, chip * depth : (chip + 1) * depth]))
    copy_all(copies, sems)


def copy_call(kernel, places, arrays, shapes, count):
    return pl.pallas_call(
        kernel,
        out_shape=[jax.ShapeDtypeStruct(shape, jnp.bfloat16) for shape in shapes],
        in_specs=[pl.BlockSpec(memory_space=pltpu.SMEM)] + in_hbm(len(arrays)),
        out_specs=in_hbm(len(shapes)),
        scratch_shapes=[pltpu.SemaphoreType.DMA((count,))],
        compiler_params=pltpu.CompilerParams(vmem_limit_bytes=63 * MIB),
        cost_estimate=pl.CostEstimate(
            flops=0,
            bytes_accessed=4 * sum(math.prod(shape) for shape in shapes),
            transcendentals=0,
        ),
    )(places, *arrays)


def project_kernel(steps, carried, final, starts, near, far, *refs):
    weights, refs = refs[: len(steps)], refs[len(steps) :]
    if carried:
        carry, refs = refs[0], refs[1:]
    outs, (tokens, held, sems) = refs[:-3], refs[-3:]
    rows = near.shape[0]
    batches = ([], [], [])
    row = 0
    for step, depth in enumerate(steps):
        here = slice(row, row + depth)
        row += depth
        batches[0].append(
            pltpu.make_async_copy(weights[step], held.at[here], sems.at[step, 2])
        )
        for side, ref in enumerate((far, near)):
            window = pl.ds(pl.multiple_of(starts[side, step], 128), depth)
            batches[1 + side].append(
                pltpu.make_async_copy(
                    ref.at[:, window], tokens.at[side, :, here], sems.at[step, side]
                )
            )
    for batch in batches:
        for copy in batch:
            copy.start()
    for copy in batches[0]:
        copy.wait()
    for side in range(2):
        for copy in batches[1 + side]:
            copy.wait()
        total = jnp.dot(tokens[side], held[...], preferred_element_type=jnp.float32)
        place = slice((1 - side) * rows, (2 - side) * rows)
        if carried:
            total = total + carry[place, :]
        if final:
            outs[1 - side][...] = total
        else:
            outs[0][place, :] = total


def project(terms, near, far, carry=None, final=False):
    rows = near.shape[0]
    width = terms[0][0].shape[1]
    steps = [array.shape[0] for array, *_ in terms]
    depth = sum(steps)
    starts = jnp.stack(
        [jnp.stack([jnp.int32(term[1 + side]) for term in terms]) for side in range(2)]
    )
    whole = jax.ShapeDtypeStruct((2 * rows, width), jnp.float32)
    part = jax.ShapeDtypeStruct((rows, width), jnp.float32)
    carries = [] if carry is None else [carry]
    return pl.pallas_call(
        functools.partial(project_kernel, steps, carry is not None, final),
        out_shape=(part, part) if final else whole,
        in_specs=[pl.BlockSpec(memory_space=pltpu.SMEM)]
        + in_hbm(2 + len(terms))
        + vmem(len(carries)),
        out_specs=tuple(vmem(2)) if final else vmem(1)[0],
        scratch_shapes=[
            pltpu.VMEM((2, rows, depth), jnp.bfloat16),
            pltpu.VMEM((depth, width), jnp.bfloat16),
            pltpu.SemaphoreType.DMA((len(steps), 3)),
        ],
        compiler_params=pltpu.CompilerParams(vmem_limit_bytes=48 * MIB),
        cost_estimate=pl.CostEstimate(
            flops=4 * rows * width * depth,
            bytes_accessed=2 * depth * (2 * rows + width),
            transcendentals=0,
        ),
    )(starts, near, far, *[array for array, *_ in terms], *carries)


def turn(vectors, cosine, sine):
    return vectors * cosine + pltpu.roll(vectors, vectors.shape[1] // 2, 1) * sine


def pair_kernel(near, far, cosine, sine, out):
    head_size = cosine.shape[1]
    pair = near[...] + far[...]
    out[:, :head_size] = turn(pair[:, :head_size], cosine[...], sine[...]).astype(out.dtype)
    out[:, head_size:] = pair[:, head_size:].astype(out.dtype)


def finish_pair(near, far, cosine, sine):
    return pl.pallas_call(
        pair_kernel,
        out_shape=jax.ShapeDtypeStruct(near.shape, jnp.bfloat16),
        in_specs=vmem(4),
        out_specs=vmem(1)[0],
        compiler_params=pltpu.CompilerParams(vmem_limit_bytes=8 * MIB),
        cost_estimate=pl.CostEstimate(
            flops=6 * near.size, bytes_accessed=14 * near.size, transcendentals=0
        ),
    )(near, far, cosine, sine)


def attend_kernel(back, near, far, cosine, sine, first, keys_values, out, rotated):
    rows, head_size = cosine.shape
    head_count = near.shape[1] // head_size
    base = keys_values.shape[0] - rows
    tiles = rows // ROW_TILE
    for head in range(head_count):
        columns = slice(head * head_size, (head + 1) * head_size)
        turned = turn(near[:, columns] + far[:, columns], cosine[...], sine[...])
        turned = turned.astype(jnp.bfloat16)
        for tile in range(tiles):
            rotated[tile, head * ROW_TILE : (head + 1) * ROW_TILE, :] = turned[
                tile * ROW_TILE : (tile + 1) * ROW_TILE
            ]
    scale = jnp.float32(math.log2(math.e) / math.sqrt(head_size))
    for tile in range(tiles):
        begin = base + tile * ROW_TILE - back
        window = keys_values[begin : begin + back + ROW_TILE, :]
        scores = lax.dot_general(
            rotated[tile],
            window[:, :head_size],
            (((1,), (1,)), ((), ())),
            preferred_element_type=jnp.float32,
        )
        shape = (ROW_TILE, back + ROW_TILE)
        key_place = lax.broadcasted_iota(jnp.int32, shape, 1) + (tile * ROW_TILE - back)
        row_place = lax.broadcasted_iota(jnp.int32, shape, 0) + tile * ROW_TILE
        lower = first[tile * ROW_TILE : (tile + 1) * ROW_TILE, :]
        allowed = (key_place <= row_place) & (key_place >= lower)
        for head in range(head_count):
            part = scores[head * ROW_TILE : (head + 1) * ROW_TILE]
            part = jnp.where(allowed, part, jnp.float32(-1e30))
            largest = jnp.max(part, axis=-1, keepdims=True)
            exponents = jnp.exp2((part - largest) * scale)
            denominator = jnp.sum(exponents, axis=-1, keepdims=True)
            numerator = jnp.dot(
                exponents.astype(jnp.bfloat16),
                window[:, head_size:],
                preferred_element_type=jnp.float32,
            )
            left = head * head_size
            out[tile * ROW_TILE : (tile + 1) * ROW_TILE, left : left + head_size] = (
                numerator / denominator
            ).astype(out.dtype)


def attend(near, far, cosine, sine, first, keys_values, back):
    rows, width = near.shape
    head_size = cosine.shape[1]
    head_count = width // head_size
    window = back + ROW_TILE
    return pl.pallas_call(
        functools.partial(attend_kernel, back),
        out_shape=jax.ShapeDtypeStruct((rows, width), jnp.bfloat16),
        in_specs=vmem(6),
        out_specs=vmem(1)[0],
        scratch_shapes=[
            pltpu.VMEM((rows // ROW_TILE, head_count * ROW_TILE, head_size), jnp.bfloat16)
        ],
        compiler_params=pltpu.CompilerParams(
            vmem_limit_bytes=8 * MIB + 24 * head_count * ROW_TILE * window
        ),
        cost_estimate=pl.CostEstimate(
            flops=4 * rows * width * window,
            bytes_accessed=8 * rows * width,
            transcendentals=rows * head_count * window,
        ),
    )(near, far, cosine, sine, first, keys_values)


def shards(dp_size, ctx_size, tokens, w_query, w_key, w_value, doc_lengths):
    hidden = tokens[0]
    row_count = hidden.shape[0]
    depth, query_width = w_query.shape
    head_size = w_key.shape[1]
    chips = dp_size // 2
    bits = chips.bit_length() - 1
    me = lax.axis_index("dp")
    place = lax.axis_index("ctx")

    def swap(array, mask):
        return lax.ppermute(array, "dp", [(i, i ^ mask) for i in range(dp_size)])

    def fetch(pair, given, gate, later):
        held = []
        for side, array in enumerate(pair):
            pieces = {0: [(0, array)], **given[side]}
            reached = [0]
            for axis in list(range(bits))[:: 1 - 2 * side]:
                for source in list(reached):
                    target = source | (1 << axis)
                    reached.append(target)
                    if target not in pieces:
                        sent = after(pieces[source][0][1], *(later if source else gate))
                        pieces[target] = [(0, swap(sent, 2 << axis))]
            held.append(pieces)
        return held

    offset = place * row_count
    positions = offset + jnp.arange(row_count, dtype=jnp.int32)
    cosine, sine = rope_tables(positions, head_size)
    first = (doc_starts(doc_lengths[0], positions) - offset)[:, None]

    axes = [1 << axis for axis in range(bits)]
    half = depth // 2
    some = half // 2
    halved = ctx_size % 2 == 0
    begin = (place % 2) * some
    parts = []
    if halved:
        shapes = [(some, query_width)] * 2
        parts = copy_call(halves_kernel, begin[None], [w_query], shapes, 2)
    theirs = jnp.stack([(me ^ (2 * chip + 1)) * depth for chip in range(chips)])
    shapes = [(depth, 2 * head_size)] + [(half, query_width)] * 2 + [(row_count, chips * depth)]
    arrays = [after(w_key, *parts), w_value, w_query, hidden]
    pair_here, *halves, sent = copy_call(pack_kernel, theirs, arrays, shapes, 4 + chips)

    def term(array, chip, row):
        return (array, chip * depth + row, (me ^ (2 * chip)) * depth + row)

    given = [{}, {}]
    mine = [swap(part, 2 << axis) for part, axis in zip(parts, (bits - 1, 0))]
    if halved:
        both = jnp.concatenate(mine, axis=0)
        both = lax.ppermute(both, "ctx", [(i, i ^ 1) for i in range(ctx_size)])
        given = [
            {1 << axis: [(begin, mine[side]), (some - begin, both[side * some : side * some + some])]}
            for side, axis in enumerate((bits - 1, 0))
        ]
    pairs = [pair_here] + [swap(pair_here, 2 << axis) for axis in range(bits)]
    far_tokens = swap(sent, 1)
    sides = [slice(0, half), slice(half, depth)]
    pair_held = fetch(
        [pair_here[rows] for rows in sides],
        [{1 << axis: [(0, pairs[1 + axis][rows])] for axis in range(bits)} for rows in sides],
        [],
        [],
    )
    pair_terms = [term(array, chip, 0) for chip, array in zip([0] + axes, pairs)]
    carry = project(pair_terms, hidden, far_tokens)
    pair_terms = [
        term(pair_held[side][chip][0][1], chip, side * half)
        for chip in range(chips)
        if chip not in [0] + axes
        for side in range(2)
    ]
    near, far = project(pair_terms, hidden, far_tokens, carry, True)
    query_held = fetch(halves, given, [*pairs, cosine, sine, first], [near])

    pair = finish_pair(near, swap(far, 1), cosine, sine)
    longest = ctx_size * row_count // 2
    back = -(-(longest - 1) // ROW_TILE) * ROW_TILE
    hops = min(ctx_size - 1, -(-back // row_count))
    blocks = [after(pair, both) if halved else pair]
    for _ in range(hops):
        blocks.insert(0, lax.ppermute(blocks[0], "ctx", [(i, i + 1) for i in range(ctx_size - 1)]))
    keys_values = jnp.concatenate(blocks, axis=0)

    def query_terms(wanted, *gate):
        return [
            term(after(array, *gate), chip, side * half + row)
            for side, chip in wanted
            for row, array in query_held[side][chip]
        ]

    everything = [(side, chip) for chip in range(chips) for side in range(2)]
    early = [(side, chip) for side, chip in everything if chip in [0] + axes]
    late = [wanted for wanted in everything if wanted not in early]
    carry = project(query_terms(early, pair), hidden, far_tokens)
    near, far = project(query_terms(late, keys_values), hidden, far_tokens, carry, True)
    return attend(near, swap(far, 1), cosine, sine, first, keys_values, back)[None]


def solution(mesh):
    return jax.shard_map(
        functools.partial(shards, mesh.shape["dp"], mesh.shape["ctx"]),
        mesh=mesh,
        in_specs=(P("dp", "ctx", None), P("dp", None), P("dp", None), P("dp", None), P("dp", None)),
        out_specs=P("dp", "ctx", None),
        check_vma=False,
    )
```

```python
import functools
import math

import jax
import jax.numpy as jnp
from jax import lax
from jax.experimental import pallas as pl
from jax.experimental.pallas import tpu as pltpu
from jax.sharding import PartitionSpec as P

ROW_TILE = 128
MIB = 1024 * 1024


def rope_tables(positions, head_size):
    half_size = head_size // 2
    exponent = jnp.arange(half_size, dtype=jnp.float32) * (2.0 / head_size)
    inverse = jnp.power(jnp.float32(500000.0), -exponent)
    angles = positions.astype(jnp.float32)[:, None] * inverse[None, :]
    cosine = jnp.cos(angles)
    sine_part = jnp.sin(angles)
    return (
        jnp.concatenate([cosine, cosine], axis=-1),
        jnp.concatenate([-sine_part, sine_part], axis=-1),
    )


def doc_starts(doc_sizes, positions):
    doc_ends = jnp.cumsum(doc_sizes)
    doc_begin = doc_ends - doc_sizes
    chosen = jnp.where(doc_begin[None, :] <= positions[:, None], doc_begin[None, :], 0)
    return jnp.max(chosen, axis=1)


def vmem(count):
    return [pl.BlockSpec(memory_space=pltpu.VMEM)] * count


def in_hbm(count):
    return [pl.BlockSpec(memory_space=pltpu.HBM)] * count


def after(array, *earlier):
    return lax.optimization_barrier((array, *earlier))[0]


def copy_all(copies, buffers, sems):
    loads = []
    stores = []
    for i, ((source, target), buffer) in enumerate(zip(copies, buffers)):
        loads.append(pltpu.make_async_copy(source, buffer, sems.at[0, i]))
        stores.append(pltpu.make_async_copy(buffer, target, sems.at[1, i]))
    for load in loads:
        load.start()
    for load, store in zip(loads, stores):
        load.wait()
        store.start()
    for store in stores:
        store.wait()


def first_kernel(begin, key, value, query, pair, *refs):
    parts, buffers, sems = refs[: (len(refs) - 3) // 2], refs[(len(refs) - 3) // 2 : -1], refs[-1]
    head_size = key.shape[1]
    copies = [(key, pair.at[:, :head_size]), (value, pair.at[:, head_size:])]
    for side, part in enumerate(parts):
        row = side * (query.shape[0] // 2) + begin[0]
        copies.append((query.at[pl.ds(pl.multiple_of(row, 16), part.shape[0])], part))
    copy_all(copies, buffers, sems)


def second_kernel(starts, query, tokens, top, bottom, columns, *refs):
    buffers, sems = refs[:-1], refs[-1]
    half, depth = top.shape[0], query.shape[0]
    copies = [(query.at[:half], top), (query.at[half:], bottom)]
    for chip in range(columns.shape[1] // depth):
        window = pl.ds(pl.multiple_of(starts[chip], 128), depth)
        copies.append((tokens.at[:, window], columns.at[:, chip * depth : (chip + 1) * depth]))
    copy_all(copies, buffers, sems)


def copy_call(kernel, places, arrays, shapes, buffers):
    return pl.pallas_call(
        kernel,
        out_shape=[jax.ShapeDtypeStruct(shape, jnp.bfloat16) for shape in shapes],
        in_specs=[pl.BlockSpec(memory_space=pltpu.SMEM)] + in_hbm(len(arrays)),
        out_specs=in_hbm(len(shapes)),
        scratch_shapes=[pltpu.VMEM(shape, jnp.bfloat16) for shape in buffers]
        + [pltpu.SemaphoreType.DMA((2, len(buffers)))],
        compiler_params=pltpu.CompilerParams(vmem_limit_bytes=63 * MIB),
        cost_estimate=pl.CostEstimate(
            flops=0,
            bytes_accessed=4 * sum(math.prod(shape) for shape in shapes),
            transcendentals=0,
        ),
    )(places, *arrays)


def project_kernel(steps, carried, final, starts, near, far, *refs):
    weights, refs = refs[: len(steps)], refs[len(steps) :]
    if carried:
        carry, refs = refs[0], refs[1:]
    outs, (tokens, held, sems) = refs[:-3], refs[-3:]
    rows = near.shape[0]
    batches = ([], [], [])
    row = 0
    for step, depth in enumerate(steps):
        here = slice(row, row + depth)
        row += depth
        batches[0].append(
            pltpu.make_async_copy(weights[step], held.at[here], sems.at[step, 2])
        )
        for side, ref in enumerate((far, near)):
            window = pl.ds(pl.multiple_of(starts[side, step], 128), depth)
            batches[1 + side].append(
                pltpu.make_async_copy(
                    ref.at[:, window], tokens.at[side, :, here], sems.at[step, side]
                )
            )
    for batch in batches:
        for copy in batch:
            copy.start()
    for copy in batches[0]:
        copy.wait()
    for side in range(2):
        for copy in batches[1 + side]:
            copy.wait()
        total = jnp.dot(tokens[side], held[...], preferred_element_type=jnp.float32)
        place = slice((1 - side) * rows, (2 - side) * rows)
        if carried:
            total = total + carry[place, :]
        if final:
            outs[1 - side][...] = total
        else:
            outs[0][place, :] = total


def project(terms, near, far, carry=None, final=False):
    rows = near.shape[0]
    width = terms[0][0].shape[1]
    steps = [array.shape[0] for array, *_ in terms]
    depth = sum(steps)
    starts = jnp.stack(
        [jnp.stack([jnp.int32(term[1 + side]) for term in terms]) for side in range(2)]
    )
    whole = jax.ShapeDtypeStruct((2 * rows, width), jnp.float32)
    part = jax.ShapeDtypeStruct((rows, width), jnp.float32)
    carries = [] if carry is None else [carry]
    return pl.pallas_call(
        functools.partial(project_kernel, steps, carry is not None, final),
        out_shape=(part, part) if final else whole,
        in_specs=[pl.BlockSpec(memory_space=pltpu.SMEM)]
        + in_hbm(2 + len(terms))
        + vmem(len(carries)),
        out_specs=tuple(vmem(2)) if final else vmem(1)[0],
        scratch_shapes=[
            pltpu.VMEM((2, rows, depth), jnp.bfloat16),
            pltpu.VMEM((depth, width), jnp.bfloat16),
            pltpu.SemaphoreType.DMA((len(steps), 3)),
        ],
        compiler_params=pltpu.CompilerParams(vmem_limit_bytes=48 * MIB),
        cost_estimate=pl.CostEstimate(
            flops=4 * rows * width * depth,
            bytes_accessed=2 * depth * (2 * rows + width),
            transcendentals=0,
        ),
    )(starts, near, far, *[array for array, *_ in terms], *carries)


def turn(vectors, cosine, sine):
    return vectors * cosine + pltpu.roll(vectors, vectors.shape[1] // 2, 1) * sine


def pair_kernel(near, far, cosine, sine, out):
    head_size = cosine.shape[1]
    pair = near[...] + far[...]
    out[:, :head_size] = turn(pair[:, :head_size], cosine[...], sine[...]).astype(out.dtype)
    out[:, head_size:] = pair[:, head_size:].astype(out.dtype)


def finish_pair(near, far, cosine, sine):
    return pl.pallas_call(
        pair_kernel,
        out_shape=jax.ShapeDtypeStruct(near.shape, jnp.bfloat16),
        in_specs=vmem(4),
        out_specs=vmem(1)[0],
        compiler_params=pltpu.CompilerParams(vmem_limit_bytes=8 * MIB),
        cost_estimate=pl.CostEstimate(
            flops=6 * near.size, bytes_accessed=14 * near.size, transcendentals=0
        ),
    )(near, far, cosine, sine)


def attend_kernel(back, near, far, cosine, sine, first, keys_values, out, rotated):
    rows, head_size = cosine.shape
    head_count = near.shape[1] // head_size
    base = keys_values.shape[0] - rows
    tiles = rows // ROW_TILE
    for head in range(head_count):
        columns = slice(head * head_size, (head + 1) * head_size)
        turned = turn(near[:, columns] + far[:, columns], cosine[...], sine[...])
        turned = turned.astype(jnp.bfloat16)
        for tile in range(tiles):
            rotated[tile, head * ROW_TILE : (head + 1) * ROW_TILE, :] = turned[
                tile * ROW_TILE : (tile + 1) * ROW_TILE
            ]
    scale = jnp.float32(math.log2(math.e) / math.sqrt(head_size))
    for tile in range(tiles):
        begin = base + tile * ROW_TILE - back
        window = keys_values[begin : begin + back + ROW_TILE, :]
        scores = lax.dot_general(
            rotated[tile],
            window[:, :head_size],
            (((1,), (1,)), ((), ())),
            preferred_element_type=jnp.float32,
        )
        shape = (ROW_TILE, back + ROW_TILE)
        key_place = lax.broadcasted_iota(jnp.int32, shape, 1) + (tile * ROW_TILE - back)
        row_place = lax.broadcasted_iota(jnp.int32, shape, 0) + tile * ROW_TILE
        lower = first[tile * ROW_TILE : (tile + 1) * ROW_TILE, :]
        allowed = (key_place <= row_place) & (key_place >= lower)
        for head in range(head_count):
            part = scores[head * ROW_TILE : (head + 1) * ROW_TILE]
            part = jnp.where(allowed, part, jnp.float32(-1e30))
            largest = jnp.max(part, axis=-1, keepdims=True)
            exponents = jnp.exp2((part - largest) * scale)
            denominator = jnp.sum(exponents, axis=-1, keepdims=True)
            numerator = jnp.dot(
                exponents.astype(jnp.bfloat16),
                window[:, head_size:],
                preferred_element_type=jnp.float32,
            )
            left = head * head_size
            out[tile * ROW_TILE : (tile + 1) * ROW_TILE, left : left + head_size] = (
                numerator / denominator
            ).astype(out.dtype)


def attend(near, far, cosine, sine, first, keys_values, back):
    rows, width = near.shape
    head_size = cosine.shape[1]
    head_count = width // head_size
    window = back + ROW_TILE
    return pl.pallas_call(
        functools.partial(attend_kernel, back),
        out_shape=jax.ShapeDtypeStruct((rows, width), jnp.bfloat16),
        in_specs=vmem(6),
        out_specs=vmem(1)[0],
        scratch_shapes=[
            pltpu.VMEM((rows // ROW_TILE, head_count * ROW_TILE, head_size), jnp.bfloat16)
        ],
        compiler_params=pltpu.CompilerParams(
            vmem_limit_bytes=8 * MIB + 24 * head_count * ROW_TILE * window
        ),
        cost_estimate=pl.CostEstimate(
            flops=4 * rows * width * window,
            bytes_accessed=8 * rows * width,
            transcendentals=rows * head_count * window,
        ),
    )(near, far, cosine, sine, first, keys_values)


def shards(dp_size, ctx_size, tokens, w_query, w_key, w_value, doc_lengths):
    hidden = tokens[0]
    row_count = hidden.shape[0]
    depth, query_width = w_query.shape
    head_size = w_key.shape[1]
    chips = dp_size // 2
    bits = chips.bit_length() - 1
    me = lax.axis_index("dp")
    place = lax.axis_index("ctx")

    def swap(array, mask):
        return lax.ppermute(array, "dp", [(i, i ^ mask) for i in range(dp_size)])

    def fetch(pair, given, gate, later):
        held = []
        for side, array in enumerate(pair):
            pieces = {0: [(0, array)], **given[side]}
            reached = [0]
            for axis in list(range(bits))[:: 1 - 2 * side]:
                for source in list(reached):
                    target = source | (1 << axis)
                    reached.append(target)
                    if target not in pieces:
                        sent = after(pieces[source][0][1], *(later if source else gate))
                        pieces[target] = [(0, swap(sent, 2 << axis))]
            held.append(pieces)
        return held

    offset = place * row_count
    positions = offset + jnp.arange(row_count, dtype=jnp.int32)
    cosine, sine = rope_tables(positions, head_size)
    first = (doc_starts(doc_lengths[0], positions) - offset)[:, None]

    axes = [1 << axis for axis in range(bits)]
    half = depth // 2
    some = half // 2
    halved = ctx_size % 2 == 0
    begin = (place % 2) * some
    part_shapes = [(some, query_width)] * (2 if halved else 0)
    pair_here, *parts = copy_call(
        first_kernel,
        begin[None],
        [w_key, w_value, w_query],
        [(depth, 2 * head_size)] + part_shapes,
        [(depth, head_size)] * 2 + part_shapes,
    )
    theirs = jnp.stack([(me ^ (2 * chip + 1)) * depth for chip in range(chips)])
    half_shapes = [(half, query_width)] * 2
    *halves, sent = copy_call(
        second_kernel,
        theirs,
        [after(w_query, pair_here), hidden],
        half_shapes + [(row_count, chips * depth)],
        half_shapes + [(row_count, depth)] * chips,
    )

    def term(array, chip, row):
        return (array, chip * depth + row, (me ^ (2 * chip)) * depth + row)

    given = [{}, {}]
    mine = [swap(part, 2 << axis) for part, axis in zip(parts, (bits - 1, 0))]
    if halved:
        both = jnp.concatenate(mine, axis=0)
        both = lax.ppermute(both, "ctx", [(i, i ^ 1) for i in range(ctx_size)])
        given = [
            {1 << axis: [(begin, mine[side]), (some - begin, both[side * some : side * some + some])]}
            for side, axis in enumerate((bits - 1, 0))
        ]
    pairs = [pair_here] + [swap(pair_here, 2 << axis) for axis in range(bits)]
    far_tokens = swap(sent, 1)
    sides = [slice(0, half), slice(half, depth)]
    pair_held = fetch(
        [pair_here[rows] for rows in sides],
        [{1 << axis: [(0, pairs[1 + axis][rows])] for axis in range(bits)} for rows in sides],
        [],
        [],
    )
    pair_terms = [term(array, chip, 0) for chip, array in zip([0] + axes, pairs)] + [
        term(pair_held[side][chip][0][1], chip, side * half)
        for chip in range(chips)
        if chip not in [0] + axes
        for side in range(2)
    ]
    near, far = project(pair_terms, hidden, far_tokens, None, True)
    query_held = fetch(halves, given, [*pairs, cosine, sine, first], [near])

    pair = finish_pair(near, swap(far, 1), cosine, sine)
    longest = ctx_size * row_count // 2
    back = -(-(longest - 1) // ROW_TILE) * ROW_TILE
    hops = min(ctx_size - 1, -(-back // row_count))
    blocks = [after(pair, both) if halved else pair]
    for _ in range(hops):
        blocks.insert(0, lax.ppermute(blocks[0], "ctx", [(i, i + 1) for i in range(ctx_size - 1)]))
    keys_values = jnp.concatenate(blocks, axis=0)

    def query_terms(wanted, *gate):
        return [
            term(after(array, *gate), chip, side * half + row)
            for side, chip in wanted
            for row, array in query_held[side][chip]
        ]

    everything = [(side, chip) for chip in range(chips) for side in range(2)]
    early = [(side, chip) for side, chip in everything if chip in [0] + axes]
    late = [wanted for wanted in everything if wanted not in early]
    carry = project(query_terms(early, pair), hidden, far_tokens)
    near, far = project(query_terms(late, blocks[-2]), hidden, far_tokens, carry, True)
    return attend(near, swap(far, 1), cosine, sine, first, keys_values, back)[None]


def solution(mesh):
    return jax.shard_map(
        functools.partial(shards, mesh.shape["dp"], mesh.shape["ctx"]),
        mesh=mesh,
        in_specs=(P("dp", "ctx", None), P("dp", None), P("dp", None), P("dp", None), P("dp", None)),
        out_specs=P("dp", "ctx", None),
        check_vma=False,
    )
```

```python
import functools
import math

import jax
import jax.numpy as jnp
from jax import lax
from jax.experimental import pallas as pl
from jax.experimental.pallas import tpu as pltpu
from jax.sharding import PartitionSpec as P

ROW_TILE = 128
MIB = 1024 * 1024


def rope_tables(positions, head_size):
    half_size = head_size // 2
    exponent = jnp.arange(half_size, dtype=jnp.float32) * (2.0 / head_size)
    inverse = jnp.power(jnp.float32(500000.0), -exponent)
    angles = positions.astype(jnp.float32)[:, None] * inverse[None, :]
    cosine = jnp.cos(angles)
    sine_part = jnp.sin(angles)
    return (
        jnp.concatenate([cosine, cosine], axis=-1),
        jnp.concatenate([-sine_part, sine_part], axis=-1),
    )


def doc_starts(doc_sizes, positions):
    doc_ends = jnp.cumsum(doc_sizes)
    doc_begin = doc_ends - doc_sizes
    chosen = jnp.where(doc_begin[None, :] <= positions[:, None], doc_begin[None, :], 0)
    return jnp.max(chosen, axis=1)


def vmem(count):
    return [pl.BlockSpec(memory_space=pltpu.VMEM)] * count


def in_hbm(count):
    return [pl.BlockSpec(memory_space=pltpu.HBM)] * count


def after(array, *earlier):
    return lax.optimization_barrier((array, *earlier))[0]


def copy_all(copies, buffers, sems):
    loads = []
    stores = []
    for i, ((source, target), buffer) in enumerate(zip(copies, buffers)):
        loads.append(pltpu.make_async_copy(source, buffer, sems.at[0, i]))
        stores.append(pltpu.make_async_copy(buffer, target, sems.at[1, i]))
    for load in loads:
        load.start()
    for load, store in zip(loads, stores):
        load.wait()
        store.start()
    for store in stores:
        store.wait()


def cut_kernel(places, query, *refs):
    pieces, buffers, sems = refs[: len(refs) // 2], refs[len(refs) // 2 : -1], refs[-1]
    copies = []
    for i, piece in enumerate(pieces):
        rows = pl.ds(pl.multiple_of(places[i], 16), piece.shape[0])
        copies.append((query.at[rows], piece))
    copy_all(copies, buffers, sems)


def copy_call(kernel, places, arrays, shapes, buffers):
    return pl.pallas_call(
        kernel,
        out_shape=[jax.ShapeDtypeStruct(shape, jnp.bfloat16) for shape in shapes],
        in_specs=[pl.BlockSpec(memory_space=pltpu.SMEM)] + in_hbm(len(arrays)),
        out_specs=in_hbm(len(shapes)),
        scratch_shapes=[pltpu.VMEM(shape, jnp.bfloat16) for shape in buffers]
        + [pltpu.SemaphoreType.DMA((2, len(buffers)))],
        compiler_params=pltpu.CompilerParams(vmem_limit_bytes=63 * MIB),
        cost_estimate=pl.CostEstimate(
            flops=0,
            bytes_accessed=4 * sum(math.prod(shape) for shape in shapes),
            transcendentals=0,
        ),
    )(places, *arrays)


def project_kernel(steps, starts, near, far, *refs):
    count = sum(len(spots) for _, spots in steps)
    weights, refs = refs[:count], refs[count:]
    *carry, far_out, near_out, tokens, held, sems = refs
    rows = near.shape[0]
    batches = ([], [], [])
    used = row = 0
    for step, (depth, spots) in enumerate(steps):
        here = slice(row, row + depth)
        row += depth
        for index, columns in enumerate(spots):
            batches[0].append(
                pltpu.make_async_copy(
                    weights[used], held.at[here, columns], sems.at[step, 2 + index]
                )
            )
            used += 1
        window = pl.ds(pl.multiple_of(starts[step], 128), depth)
        for side, ref in enumerate((far, near)):
            batches[1 + side].append(
                pltpu.make_async_copy(
                    ref.at[:, window], tokens.at[side, :, here], sems.at[step, side]
                )
            )
    for batch in batches:
        for copy in batch:
            copy.start()
    for copy in batches[0]:
        copy.wait()
    for side, out in enumerate((far_out, near_out)):
        for copy in batches[1 + side]:
            copy.wait()
        total = jnp.dot(tokens[side], held[...], preferred_element_type=jnp.float32)
        out[...] = total + carry[side][...] if carry else total


def project(terms, near, far, carry=()):
    rows = near.shape[0]
    width = sum(array.shape[1] for array in terms[0][0])
    steps = []
    for arrays, _ in terms:
        edges = [sum(array.shape[1] for array in arrays[:i]) for i in range(len(arrays) + 1)]
        spots = [slice(*edge) for edge in zip(edges[:-1], edges[1:])]
        steps.append((arrays[0].shape[0], spots))
    depth = sum(step[0] for step in steps)
    starts = jnp.stack([jnp.int32(start) for _, start in terms])
    weights = [array for arrays, _ in terms for array in arrays]
    return pl.pallas_call(
        functools.partial(project_kernel, steps),
        out_shape=[jax.ShapeDtypeStruct((rows, width), jnp.float32)] * 2,
        in_specs=[pl.BlockSpec(memory_space=pltpu.SMEM)]
        + in_hbm(2 + len(weights))
        + vmem(len(carry)),
        out_specs=vmem(2),
        scratch_shapes=[
            pltpu.VMEM((2, rows, depth), jnp.bfloat16),
            pltpu.VMEM((depth, width), jnp.bfloat16),
            pltpu.SemaphoreType.DMA((len(steps), 4)),
        ],
        compiler_params=pltpu.CompilerParams(vmem_limit_bytes=48 * MIB),
        cost_estimate=pl.CostEstimate(
            flops=4 * rows * width * depth,
            bytes_accessed=2 * depth * (2 * rows + width),
            transcendentals=0,
        ),
    )(starts, near, far, *weights, *carry)


def turn(vectors, cosine, sine):
    return vectors * cosine + pltpu.roll(vectors, vectors.shape[1] // 2, 1) * sine


def pair_kernel(near, far, cosine, sine, out):
    head_size = cosine.shape[1]
    pair = near[...] + far[...]
    out[:, :head_size] = turn(pair[:, :head_size], cosine[...], sine[...]).astype(out.dtype)
    out[:, head_size:] = pair[:, head_size:].astype(out.dtype)


def finish_pair(near, far, cosine, sine):
    return pl.pallas_call(
        pair_kernel,
        out_shape=jax.ShapeDtypeStruct(near.shape, jnp.bfloat16),
        in_specs=vmem(4),
        out_specs=vmem(1)[0],
        compiler_params=pltpu.CompilerParams(vmem_limit_bytes=8 * MIB),
        cost_estimate=pl.CostEstimate(
            flops=6 * near.size, bytes_accessed=14 * near.size, transcendentals=0
        ),
    )(near, far, cosine, sine)


def attend_kernel(back, near, far, cosine, sine, first, keys_values, out, rotated):
    rows, head_size = cosine.shape
    head_count = near.shape[1] // head_size
    base = keys_values.shape[0] - rows
    tiles = rows // ROW_TILE
    for head in range(head_count):
        columns = slice(head * head_size, (head + 1) * head_size)
        turned = turn(near[:, columns] + far[:, columns], cosine[...], sine[...])
        turned = turned.astype(jnp.bfloat16)
        for tile in range(tiles):
            rotated[tile, head * ROW_TILE : (head + 1) * ROW_TILE, :] = turned[
                tile * ROW_TILE : (tile + 1) * ROW_TILE
            ]
    scale = jnp.float32(math.log2(math.e) / math.sqrt(head_size))
    for tile in range(tiles):
        begin = base + tile * ROW_TILE - back
        window = keys_values[begin : begin + back + ROW_TILE, :]
        scores = lax.dot_general(
            rotated[tile],
            window[:, :head_size],
            (((1,), (1,)), ((), ())),
            preferred_element_type=jnp.float32,
        )
        shape = (ROW_TILE, back + ROW_TILE)
        key_place = lax.broadcasted_iota(jnp.int32, shape, 1) + (tile * ROW_TILE - back)
        row_place = lax.broadcasted_iota(jnp.int32, shape, 0) + tile * ROW_TILE
        lower = first[tile * ROW_TILE : (tile + 1) * ROW_TILE, :]
        allowed = (key_place <= row_place) & (key_place >= lower)
        for head in range(head_count):
            part = scores[head * ROW_TILE : (head + 1) * ROW_TILE]
            part = jnp.where(allowed, part, jnp.float32(-1e30))
            largest = jnp.max(part, axis=-1, keepdims=True)
            exponents = jnp.exp2((part - largest) * scale)
            denominator = jnp.sum(exponents, axis=-1, keepdims=True)
            numerator = jnp.dot(
                exponents.astype(jnp.bfloat16),
                window[:, head_size:],
                preferred_element_type=jnp.float32,
            )
            left = head * head_size
            out[tile * ROW_TILE : (tile + 1) * ROW_TILE, left : left + head_size] = (
                numerator / denominator
            ).astype(out.dtype)


def attend(near, far, cosine, sine, first, keys_values, back):
    rows, width = near.shape
    head_size = cosine.shape[1]
    head_count = width // head_size
    window = back + ROW_TILE
    return pl.pallas_call(
        functools.partial(attend_kernel, back),
        out_shape=jax.ShapeDtypeStruct((rows, width), jnp.bfloat16),
        in_specs=vmem(6),
        out_specs=vmem(1)[0],
        scratch_shapes=[
            pltpu.VMEM((rows // ROW_TILE, head_count * ROW_TILE, head_size), jnp.bfloat16)
        ],
        compiler_params=pltpu.CompilerParams(
            vmem_limit_bytes=8 * MIB + 24 * head_count * ROW_TILE * window
        ),
        cost_estimate=pl.CostEstimate(
            flops=4 * rows * width * window,
            bytes_accessed=8 * rows * width,
            transcendentals=rows * head_count * window,
        ),
    )(near, far, cosine, sine, first, keys_values)


def shards(dp_size, ctx_size, tokens, w_query, w_key, w_value, doc_lengths):
    hidden = tokens[0]
    row_count = hidden.shape[0]
    depth, query_width = w_query.shape
    head_size = w_key.shape[1]
    chips = dp_size // 2
    bits = chips.bit_length() - 1
    me = lax.axis_index("dp")
    place = lax.axis_index("ctx")

    def swap(array, mask):
        return lax.ppermute(array, "dp", [(i, i ^ mask) for i in range(dp_size)])

    def fetch(pair, given, gate, later):
        held = []
        for side, array in enumerate(pair):
            pieces = {0: [(0, array)], **given[side]}
            reached = [0]
            for axis in list(range(bits))[:: 1 - 2 * side]:
                for source in list(reached):
                    target = source | (1 << axis)
                    reached.append(target)
                    if target not in pieces:
                        sent = after(pieces[source][0][1], *(later if source else gate))
                        pieces[target] = [(0, swap(sent, 2 << axis))]
            held.append(pieces)
        return held

    offset = place * row_count
    positions = offset + jnp.arange(row_count, dtype=jnp.int32)
    cosine, sine = rope_tables(positions, head_size)
    first = (doc_starts(doc_lengths[0], positions) - offset)[:, None]

    axes = [1 << axis for axis in range(bits)]
    half = depth // 2
    some = half // 2
    halved = ctx_size % 2 == 0
    begin = (place % 2) * some

    pair_held = fetch((w_key, w_value), [{}, {}], [], [])
    far_tokens = swap(hidden, 1)
    rows = [0, half] + ([begin, half + begin] if halved else [])
    shapes = [(half, query_width)] * 2 + [(some, query_width)] * (len(rows) - 2)
    places = jnp.stack([jnp.int32(row) for row in rows])
    halves = copy_call(cut_kernel, places, [w_query], shapes, shapes)
    parts = halves[2:]

    def term(arrays, chip, row):
        return (arrays, (me ^ (2 * chip)) * depth + row)

    direct = [pair_held[side][chip][0][1] for side in range(2) for chip in axes]
    gate = [*direct, cosine, sine, first]
    given, other = [{}, {}], []
    mine = [swap(part, 2 << axis) for part, axis in zip(parts, (bits - 1, 0))]
    if halved:
        other = [lax.ppermute(part, "ctx", [(i, i ^ 1) for i in range(ctx_size)]) for part in mine]
        given = [
            {1 << axis: [(begin, mine[side]), (some - begin, other[side])]}
            for side, axis in enumerate((bits - 1, 0))
        ]
    pair_terms = [
        term([pair_held[side][chip][0][1] for side in range(2)], chip, 0) for chip in range(chips)
    ]
    far, near = project(pair_terms, hidden, far_tokens)
    query_held = fetch(halves[:2], given, [*gate, *mine], [near, *other])

    pair = finish_pair(near, swap(far, 1), cosine, sine)
    longest = ctx_size * row_count // 2
    back = -(-(longest - 1) // ROW_TILE) * ROW_TILE
    hops = min(ctx_size - 1, -(-back // row_count))
    blocks = [pair]
    for _ in range(hops):
        blocks.insert(0, lax.ppermute(blocks[0], "ctx", [(i, i + 1) for i in range(ctx_size - 1)]))
    keys_values = jnp.concatenate(blocks, axis=0)

    def query_terms(wanted, *gate):
        return [
            term([after(array, *gate)], chip, side * half + row)
            for side, chip in wanted
            for row, array in query_held[side][chip]
        ]

    everything = [(side, chip) for chip in range(chips) for side in range(2)]
    early = [(0, 0), (1, 0), (0, axes[0]), (1, axes[-1])]
    late = [wanted for wanted in everything if wanted not in early]
    carry = project(query_terms(early, pair), hidden, far_tokens)
    far, near = project(query_terms(late, blocks[-2]), hidden, far_tokens, carry)
    return attend(near, swap(far, 1), cosine, sine, first, keys_values, back)[None]


def solution(mesh):
    return jax.shard_map(
        functools.partial(shards, mesh.shape["dp"], mesh.shape["ctx"]),
        mesh=mesh,
        in_specs=(P("dp", "ctx", None), P("dp", None), P("dp", None), P("dp", None), P("dp", None)),
        out_specs=P("dp", "ctx", None),
        check_vma=False,
    )
```

```python
import functools
import math

import jax
import jax.numpy as jnp
from jax import lax
from jax.experimental import pallas as pl
from jax.experimental.pallas import tpu as pltpu
from jax.sharding import PartitionSpec as P

ROW_TILE = 128
MIB = 1024 * 1024


def rope_tables(positions, head_size):
    half_size = head_size // 2
    exponent = jnp.arange(half_size, dtype=jnp.float32) * (2.0 / head_size)
    inverse = jnp.power(jnp.float32(500000.0), -exponent)
    angles = positions.astype(jnp.float32)[:, None] * inverse[None, :]
    cosine = jnp.cos(angles)
    sine_part = jnp.sin(angles)
    return (
        jnp.concatenate([cosine, cosine], axis=-1),
        jnp.concatenate([-sine_part, sine_part], axis=-1),
    )


def doc_starts(doc_sizes, positions):
    doc_ends = jnp.cumsum(doc_sizes)
    doc_begin = doc_ends - doc_sizes
    chosen = jnp.where(doc_begin[None, :] <= positions[:, None], doc_begin[None, :], 0)
    return jnp.max(chosen, axis=1)


def vmem(count):
    return [pl.BlockSpec(memory_space=pltpu.VMEM)] * count


def anywhere(count):
    return [pl.BlockSpec(memory_space=pl.ANY)] * count


def after(array, *earlier):
    return lax.optimization_barrier((array, *earlier))[0]


def cut_kernel(chips, places, query, tokens, *refs):
    *pieces, columns, sems = refs
    depth = query.shape[0]
    copies = []
    for i, piece in enumerate(pieces):
        rows = pl.ds(pl.multiple_of(places[chips + i], 16), piece.shape[0])
        copies.append((query.at[rows], piece))
    for chip in range(chips):
        window = pl.ds(pl.multiple_of(places[chip], 128), depth)
        copies.append((tokens.at[:, window], columns.at[:, chip * depth : (chip + 1) * depth]))
    copies = [pltpu.make_async_copy(*copy, sems.at[i]) for i, copy in enumerate(copies)]
    for copy in copies:
        copy.start()
    for copy in copies:
        copy.wait()


def cut(places, query, tokens, shapes):
    depth = query.shape[0]
    chips = len(places) - len(shapes)
    shapes = shapes + [(tokens.shape[0], chips * depth)]
    return pl.pallas_call(
        functools.partial(cut_kernel, chips),
        out_shape=[jax.ShapeDtypeStruct(shape, query.dtype) for shape in shapes],
        in_specs=[pl.BlockSpec(memory_space=pltpu.SMEM)] + anywhere(2),
        out_specs=vmem(len(shapes)),
        scratch_shapes=[pltpu.SemaphoreType.DMA((len(places),))],
        compiler_params=pltpu.CompilerParams(vmem_limit_bytes=40 * MIB),
        cost_estimate=pl.CostEstimate(
            flops=0,
            bytes_accessed=4 * sum(math.prod(shape) for shape in shapes),
            transcendentals=0,
        ),
    )(jnp.stack([jnp.int32(place) for place in places]), query, tokens)


def project_kernel(steps, starts, near, far, *refs):
    count = sum(len(spots) for _, spots in steps)
    weights, refs = refs[:count], refs[count:]
    *carry, far_out, near_out, held, sems = refs
    batches = []
    used = row = 0
    for step, (depth, spots) in enumerate(steps):
        batch = []
        for index, columns in enumerate(spots):
            batch.append(
                pltpu.make_async_copy(
                    weights[used], held.at[row : row + depth, columns], sems.at[step, index]
                )
            )
            batch[-1].start()
            used += 1
        batches.append((row, depth, batch))
        row += depth
    totals = [ref[...] for ref in carry]
    for step, (row, depth, batch) in enumerate(batches):
        for copy in batch:
            copy.wait()
        terms = []
        for side, ref in enumerate((far, near)):
            window = pl.ds(pl.multiple_of(starts[side, step], 128), depth)
            terms.append(
                jnp.dot(
                    ref[:, window],
                    held[row : row + depth, :],
                    preferred_element_type=jnp.float32,
                )
            )
        totals = [total + term for total, term in zip(totals, terms)] if totals else terms
    far_out[...], near_out[...] = totals


def project(terms, near, far, carry=()):
    rows = near.shape[0]
    width = sum(array.shape[1] for array in terms[0][0])
    steps = []
    for arrays, *_ in terms:
        edges = [sum(array.shape[1] for array in arrays[:i]) for i in range(len(arrays) + 1)]
        spots = [slice(*edge) for edge in zip(edges[:-1], edges[1:])]
        steps.append((arrays[0].shape[0], spots))
    depth = sum(step[0] for step in steps)
    starts = jnp.stack(
        [jnp.stack([jnp.int32(term[1 + side]) for term in terms]) for side in range(2)]
    )
    weights = [array for arrays, *_ in terms for array in arrays]
    return pl.pallas_call(
        functools.partial(project_kernel, steps),
        out_shape=[jax.ShapeDtypeStruct((rows, width), jnp.float32)] * 2,
        in_specs=[pl.BlockSpec(memory_space=pltpu.SMEM)]
        + vmem(2)
        + anywhere(len(weights))
        + vmem(len(carry)),
        out_specs=vmem(2),
        scratch_shapes=[
            pltpu.VMEM((depth, width), jnp.bfloat16),
            pltpu.SemaphoreType.DMA((len(steps), 2)),
        ],
        compiler_params=pltpu.CompilerParams(vmem_limit_bytes=32 * MIB),
        cost_estimate=pl.CostEstimate(
            flops=4 * rows * width * depth,
            bytes_accessed=2 * depth * (2 * rows + width),
            transcendentals=0,
        ),
    )(starts, near, far, *weights, *carry)


def turn(vectors, cosine, sine):
    return vectors * cosine + pltpu.roll(vectors, vectors.shape[1] // 2, 1) * sine


def pair_kernel(near, far, cosine, sine, out):
    head_size = cosine.shape[1]
    pair = near[...] + far[...]
    out[:, :head_size] = turn(pair[:, :head_size], cosine[...], sine[...]).astype(out.dtype)
    out[:, head_size:] = pair[:, head_size:].astype(out.dtype)


def finish_pair(near, far, cosine, sine):
    return pl.pallas_call(
        pair_kernel,
        out_shape=jax.ShapeDtypeStruct(near.shape, jnp.bfloat16),
        in_specs=vmem(4),
        out_specs=vmem(1)[0],
        compiler_params=pltpu.CompilerParams(vmem_limit_bytes=8 * MIB),
        cost_estimate=pl.CostEstimate(
            flops=6 * near.size, bytes_accessed=14 * near.size, transcendentals=0
        ),
    )(near, far, cosine, sine)


def attend_kernel(back, near, far, cosine, sine, first, keys_values, out, rotated):
    rows, head_size = cosine.shape
    head_count = near.shape[1] // head_size
    base = keys_values.shape[0] - rows
    tiles = rows // ROW_TILE
    for head in range(head_count):
        columns = slice(head * head_size, (head + 1) * head_size)
        turned = turn(near[:, columns] + far[:, columns], cosine[...], sine[...])
        turned = turned.astype(jnp.bfloat16)
        for tile in range(tiles):
            rotated[tile, head * ROW_TILE : (head + 1) * ROW_TILE, :] = turned[
                tile * ROW_TILE : (tile + 1) * ROW_TILE
            ]
    scale = jnp.float32(math.log2(math.e) / math.sqrt(head_size))
    for tile in range(tiles):
        begin = base + tile * ROW_TILE - back
        window = keys_values[begin : begin + back + ROW_TILE, :]
        scores = lax.dot_general(
            rotated[tile],
            window[:, :head_size],
            (((1,), (1,)), ((), ())),
            preferred_element_type=jnp.float32,
        )
        shape = (ROW_TILE, back + ROW_TILE)
        key_place = lax.broadcasted_iota(jnp.int32, shape, 1) + (tile * ROW_TILE - back)
        row_place = lax.broadcasted_iota(jnp.int32, shape, 0) + tile * ROW_TILE
        lower = first[tile * ROW_TILE : (tile + 1) * ROW_TILE, :]
        allowed = (key_place <= row_place) & (key_place >= lower)
        for head in range(head_count):
            part = scores[head * ROW_TILE : (head + 1) * ROW_TILE]
            part = jnp.where(allowed, part, jnp.float32(-1e30))
            largest = jnp.max(part, axis=-1, keepdims=True)
            exponents = jnp.exp2((part - largest) * scale)
            denominator = jnp.sum(exponents, axis=-1, keepdims=True)
            numerator = jnp.dot(
                exponents.astype(jnp.bfloat16),
                window[:, head_size:],
                preferred_element_type=jnp.float32,
            )
            left = head * head_size
            out[tile * ROW_TILE : (tile + 1) * ROW_TILE, left : left + head_size] = (
                numerator / denominator
            ).astype(out.dtype)


def attend(near, far, cosine, sine, first, keys_values, back):
    rows, width = near.shape
    head_size = cosine.shape[1]
    head_count = width // head_size
    window = back + ROW_TILE
    return pl.pallas_call(
        functools.partial(attend_kernel, back),
        out_shape=jax.ShapeDtypeStruct((rows, width), jnp.bfloat16),
        in_specs=vmem(6),
        out_specs=vmem(1)[0],
        scratch_shapes=[
            pltpu.VMEM((rows // ROW_TILE, head_count * ROW_TILE, head_size), jnp.bfloat16)
        ],
        compiler_params=pltpu.CompilerParams(
            vmem_limit_bytes=8 * MIB + 24 * head_count * ROW_TILE * window
        ),
        cost_estimate=pl.CostEstimate(
            flops=4 * rows * width * window,
            bytes_accessed=8 * rows * width,
            transcendentals=rows * head_count * window,
        ),
    )(near, far, cosine, sine, first, keys_values)


def shards(dp_size, ctx_size, tokens, w_query, w_key, w_value, doc_lengths):
    hidden = tokens[0]
    row_count = hidden.shape[0]
    depth, query_width = w_query.shape
    head_size = w_key.shape[1]
    chips = dp_size // 2
    bits = chips.bit_length() - 1
    me = lax.axis_index("dp")
    place = lax.axis_index("ctx")

    def swap(array, mask):
        return lax.ppermute(array, "dp", [(i, i ^ mask) for i in range(dp_size)])

    def fetch(pair, given, gate, later):
        held = []
        for side, array in enumerate(pair):
            pieces = {0: [(0, array)], **given[side]}
            reached = [0]
            for axis in list(range(bits))[:: 1 - 2 * side]:
                for source in list(reached):
                    target = source | (1 << axis)
                    reached.append(target)
                    if target not in pieces:
                        sent = after(pieces[source][0][1], *(later if source else gate))
                        pieces[target] = [(0, swap(sent, 2 << axis))]
            held.append(pieces)
        return held

    offset = place * row_count
    positions = offset + jnp.arange(row_count, dtype=jnp.int32)
    cosine, sine = rope_tables(positions, head_size)
    first = (doc_starts(doc_lengths[0], positions) - offset)[:, None]

    axes = [1 << axis for axis in range(bits)]
    half = depth // 2
    some = half // 2
    halved = ctx_size % 2 == 0
    begin = (place % 2) * some

    pair_held = fetch((w_key, w_value), [{}, {}], [], [])
    far_tokens = swap(hidden, 1)
    places = [(me ^ (2 * chip)) * depth for chip in range(chips)] + [0, half]
    shapes = [(half, query_width)] * 2
    if halved:
        places += [begin, half + begin]
        shapes += [(some, query_width)] * 2
    *halves, near_tokens = cut(places, w_query, hidden, shapes)
    parts = halves[2:]

    def term(arrays, chip, row):
        return (arrays, places[chip] + row, chip * depth + row)

    direct = [pair_held[side][chip][0][1] for side in range(2) for chip in axes]
    gate = [*direct, cosine, sine, first]
    given, other = [{}, {}], []
    mine = [swap(part, 2 << axis) for part, axis in zip(parts, (bits - 1, 0))]
    if halved:
        other = [lax.ppermute(part, "ctx", [(i, i ^ 1) for i in range(ctx_size)]) for part in mine]
        given = [
            {1 << axis: [(begin, mine[side]), (some - begin, other[side])]}
            for side, axis in enumerate((bits - 1, 0))
        ]
    pair_terms = [
        term([pair_held[side][chip][0][1] for side in range(2)], chip, 0) for chip in range(chips)
    ]
    far, near = project(pair_terms, near_tokens, far_tokens)
    query_held = fetch(halves[:2], given, [*gate, *mine], [near, *other])

    pair = finish_pair(near, swap(far, 1), cosine, sine)
    longest = ctx_size * row_count // 2
    back = -(-(longest - 1) // ROW_TILE) * ROW_TILE
    hops = min(ctx_size - 1, -(-back // row_count))
    blocks = [pair]
    for _ in range(hops):
        blocks.insert(0, lax.ppermute(blocks[0], "ctx", [(i, i + 1) for i in range(ctx_size - 1)]))
    keys_values = jnp.concatenate(blocks, axis=0)

    def query_terms(wanted, *gate):
        return [
            term([after(array, *gate)], chip, side * half + row)
            for side, chip in wanted
            for row, array in query_held[side][chip]
        ]

    everything = [(side, chip) for chip in range(chips) for side in range(2)]
    early = [(0, 0), (1, 0), (0, axes[0]), (1, axes[-1])]
    late = [wanted for wanted in everything if wanted not in early]
    carry = project(query_terms(early, pair), near_tokens, far_tokens)
    far, near = project(query_terms(late, blocks[-2]), near_tokens, far_tokens, carry)
    return attend(near, swap(far, 1), cosine, sine, first, keys_values, back)[None]


def solution(mesh):
    return jax.shard_map(
        functools.partial(shards, mesh.shape["dp"], mesh.shape["ctx"]),
        mesh=mesh,
        in_specs=(P("dp", "ctx", None), P("dp", None), P("dp", None), P("dp", None), P("dp", None)),
        out_specs=P("dp", "ctx", None),
        check_vma=False,
    )
```

```python
import functools
import math

import jax
import jax.numpy as jnp
from jax import lax
from jax.experimental import pallas as pl
from jax.experimental.pallas import tpu as pltpu
from jax.sharding import PartitionSpec as P

ROW_TILE = 128
MIB = 1024 * 1024


def rope_tables(positions, head_size):
    half_size = head_size // 2
    exponent = jnp.arange(half_size, dtype=jnp.float32) * (2.0 / head_size)
    inverse = jnp.power(jnp.float32(500000.0), -exponent)
    angles = positions.astype(jnp.float32)[:, None] * inverse[None, :]
    cosine = jnp.cos(angles)
    sine_part = jnp.sin(angles)
    return (
        jnp.concatenate([cosine, cosine], axis=-1),
        jnp.concatenate([-sine_part, sine_part], axis=-1),
    )


def doc_starts(doc_sizes, positions):
    doc_ends = jnp.cumsum(doc_sizes)
    doc_begin = doc_ends - doc_sizes
    chosen = jnp.where(doc_begin[None, :] <= positions[:, None], doc_begin[None, :], 0)
    return jnp.max(chosen, axis=1)


def vmem(count):
    return [pl.BlockSpec(memory_space=pltpu.VMEM)] * count


def anywhere(count):
    return [pl.BlockSpec(memory_space=pl.ANY)] * count


def after(array, *earlier):
    corners = [other[:8, : min(128, other.shape[1])] for other in earlier]
    return lax.optimization_barrier((array, *corners))[0]


def cut_kernel(chips, places, query, tokens, *refs):
    *pieces, columns, sems = refs
    depth = query.shape[0]
    copies = []
    for i, piece in enumerate(pieces):
        rows = pl.ds(pl.multiple_of(places[chips + i], 16), piece.shape[0])
        copies.append((query.at[rows], piece))
    for chip in range(chips):
        window = pl.ds(pl.multiple_of(places[chip], 128), depth)
        copies.append((tokens.at[:, window], columns.at[:, chip * depth : (chip + 1) * depth]))
    copies = [pltpu.make_async_copy(*copy, sems.at[i]) for i, copy in enumerate(copies)]
    for copy in copies:
        copy.start()
    for copy in copies:
        copy.wait()


def cut(places, query, tokens, shapes):
    depth = query.shape[0]
    chips = len(places) - len(shapes)
    shapes = shapes + [(tokens.shape[0], chips * depth)]
    return pl.pallas_call(
        functools.partial(cut_kernel, chips),
        out_shape=[jax.ShapeDtypeStruct(shape, query.dtype) for shape in shapes],
        in_specs=[pl.BlockSpec(memory_space=pltpu.SMEM)] + anywhere(2),
        out_specs=vmem(len(shapes)),
        scratch_shapes=[pltpu.SemaphoreType.DMA((len(places),))],
        compiler_params=pltpu.CompilerParams(vmem_limit_bytes=40 * MIB),
        cost_estimate=pl.CostEstimate(
            flops=0,
            bytes_accessed=4 * sum(math.prod(shape) for shape in shapes),
            transcendentals=0,
        ),
    )(jnp.stack([jnp.int32(place) for place in places]), query, tokens)


def project_kernel(depth, chips, pieces, places, near, far, *refs):
    weights, refs = refs[: len(pieces)], refs[len(pieces) :]
    *carry, far_out, near_out, held, sems = refs
    copies = []
    for index, (slot, column) in enumerate(pieces):
        rows, width = weights[index].shape
        row = pl.multiple_of(slot * depth + places[len(chips) + index], 16)
        spot = held.at[pl.ds(row, rows), column : column + width]
        copies.append(pltpu.make_async_copy(weights[index], spot, sems.at[index]))
        copies[-1].start()
    for copy in copies:
        copy.wait()

    def product(ref, window, rows):
        return jnp.dot(ref[:, window], held[rows, :], preferred_element_type=jnp.float32)

    total = carry[0][...] if carry else None
    for slot in range(len(chips)):
        window = pl.ds(pl.multiple_of(places[slot], 128), depth)
        term = product(far, window, slice(slot * depth, (slot + 1) * depth))
        total = term if total is None else total + term
    far_out[...] = total
    total = carry[1][...] if carry else None
    slot = 0
    while slot < len(chips):
        end = slot + 1
        while end < len(chips) and chips[end] == chips[end - 1] + 1:
            end += 1
        window = slice(chips[slot] * depth, (chips[end - 1] + 1) * depth)
        term = product(near, window, slice(slot * depth, end * depth))
        total = term if total is None else total + term
        slot = end
    near_out[...] = total


def project(depth, width, terms, near, far, carry=()):
    rows = near.shape[0]
    chips = [term[0] for term in terms]
    pieces = [(slot, *piece) for slot, term in enumerate(terms) for piece in term[2]]
    places = [term[1] for term in terms] + [row for _, _, row, _ in pieces]
    weights = [array for _, array, _, _ in pieces]
    return pl.pallas_call(
        functools.partial(
            project_kernel, depth, chips, [(slot, column) for slot, _, _, column in pieces]
        ),
        out_shape=[jax.ShapeDtypeStruct((rows, width), jnp.float32)] * 2,
        in_specs=[pl.BlockSpec(memory_space=pltpu.SMEM)]
        + vmem(2)
        + anywhere(len(weights))
        + vmem(len(carry)),
        out_specs=vmem(2),
        scratch_shapes=[
            pltpu.VMEM((len(chips) * depth, width), jnp.bfloat16),
            pltpu.SemaphoreType.DMA((len(pieces),)),
        ],
        compiler_params=pltpu.CompilerParams(vmem_limit_bytes=32 * MIB),
        cost_estimate=pl.CostEstimate(
            flops=4 * rows * width * depth * len(chips),
            bytes_accessed=2 * depth * len(chips) * (2 * rows + width),
            transcendentals=0,
        ),
    )(jnp.stack([jnp.int32(place) for place in places]), near, far, *weights, *carry)


def turn(vectors, cosine, sine):
    return vectors * cosine + pltpu.roll(vectors, vectors.shape[1] // 2, 1) * sine


def pair_kernel(near, far, cosine, sine, out):
    head_size = cosine.shape[1]
    pair = near[...] + far[...]
    out[:, :head_size] = turn(pair[:, :head_size], cosine[...], sine[...]).astype(out.dtype)
    out[:, head_size:] = pair[:, head_size:].astype(out.dtype)


def finish_pair(near, far, cosine, sine):
    return pl.pallas_call(
        pair_kernel,
        out_shape=jax.ShapeDtypeStruct(near.shape, jnp.bfloat16),
        in_specs=vmem(4),
        out_specs=vmem(1)[0],
        compiler_params=pltpu.CompilerParams(vmem_limit_bytes=8 * MIB),
        cost_estimate=pl.CostEstimate(
            flops=6 * near.size, bytes_accessed=14 * near.size, transcendentals=0
        ),
    )(near, far, cosine, sine)


def attend_kernel(back, near, far, cosine, sine, first, keys_values, out, rotated):
    rows, head_size = cosine.shape
    head_count = near.shape[1] // head_size
    base = keys_values.shape[0] - rows
    tiles = rows // ROW_TILE
    for head in range(head_count):
        columns = slice(head * head_size, (head + 1) * head_size)
        turned = turn(near[:, columns] + far[:, columns], cosine[...], sine[...])
        turned = turned.astype(jnp.bfloat16)
        for tile in range(tiles):
            rotated[tile, head * ROW_TILE : (head + 1) * ROW_TILE, :] = turned[
                tile * ROW_TILE : (tile + 1) * ROW_TILE
            ]
    scale = jnp.float32(math.log2(math.e) / math.sqrt(head_size))
    for tile in range(tiles):
        begin = base + tile * ROW_TILE - back
        window = keys_values[begin : begin + back + ROW_TILE, :]
        scores = lax.dot_general(
            rotated[tile],
            window[:, :head_size],
            (((1,), (1,)), ((), ())),
            preferred_element_type=jnp.float32,
        )
        shape = (ROW_TILE, back + ROW_TILE)
        key_place = lax.broadcasted_iota(jnp.int32, shape, 1) + (tile * ROW_TILE - back)
        row_place = lax.broadcasted_iota(jnp.int32, shape, 0) + tile * ROW_TILE
        lower = first[tile * ROW_TILE : (tile + 1) * ROW_TILE, :]
        allowed = (key_place <= row_place) & (key_place >= lower)
        for head in range(head_count):
            part = scores[head * ROW_TILE : (head + 1) * ROW_TILE]
            part = jnp.where(allowed, part, jnp.float32(-1e30))
            largest = jnp.max(part, axis=-1, keepdims=True)
            exponents = jnp.exp2((part - largest) * scale)
            denominator = jnp.sum(exponents, axis=-1, keepdims=True)
            numerator = jnp.dot(
                exponents.astype(jnp.bfloat16),
                window[:, head_size:],
                preferred_element_type=jnp.float32,
            )
            left = head * head_size
            out[tile * ROW_TILE : (tile + 1) * ROW_TILE, left : left + head_size] = (
                numerator / denominator
            ).astype(out.dtype)


def attend(near, far, cosine, sine, first, keys_values, back):
    rows, width = near.shape
    head_size = cosine.shape[1]
    head_count = width // head_size
    window = back + ROW_TILE
    return pl.pallas_call(
        functools.partial(attend_kernel, back),
        out_shape=jax.ShapeDtypeStruct((rows, width), jnp.bfloat16),
        in_specs=vmem(6),
        out_specs=vmem(1)[0],
        scratch_shapes=[
            pltpu.VMEM((rows // ROW_TILE, head_count * ROW_TILE, head_size), jnp.bfloat16)
        ],
        compiler_params=pltpu.CompilerParams(
            vmem_limit_bytes=8 * MIB + 24 * head_count * ROW_TILE * window
        ),
        cost_estimate=pl.CostEstimate(
            flops=4 * rows * width * window,
            bytes_accessed=8 * rows * width,
            transcendentals=rows * head_count * window,
        ),
    )(near, far, cosine, sine, first, keys_values)


def shards(dp_size, ctx_size, tokens, w_query, w_key, w_value, doc_lengths):
    hidden = tokens[0]
    row_count = hidden.shape[0]
    depth, query_width = w_query.shape
    head_size = w_key.shape[1]
    chips = dp_size // 2
    bits = chips.bit_length() - 1
    me = lax.axis_index("dp")
    place = lax.axis_index("ctx")

    def swap(array, mask):
        return lax.ppermute(array, "dp", [(i, i ^ mask) for i in range(dp_size)])

    def fetch(pair, given, gate, later):
        held = []
        for side, array in enumerate(pair):
            pieces = {0: [(0, array)], **given[side]}
            reached = [0]
            for axis in list(range(bits))[:: 1 - 2 * side]:
                for source in list(reached):
                    target = source | (1 << axis)
                    reached.append(target)
                    if target not in pieces:
                        sent = after(pieces[source][0][1], *(later if source else gate))
                        pieces[target] = [(0, swap(sent, 2 << axis))]
            held.append(pieces)
        return held

    offset = place * row_count
    positions = offset + jnp.arange(row_count, dtype=jnp.int32)
    cosine, sine = rope_tables(positions, head_size)
    first = (doc_starts(doc_lengths[0], positions) - offset)[:, None]

    axes = [1 << axis for axis in range(bits)]
    half = depth // 2
    some = half // 2
    halved = ctx_size % 2 == 0
    begin = (place % 2) * some

    pair_held = fetch((w_key, w_value), [{}, {}], [], [])
    far_tokens = swap(hidden, 1)
    places = [(me ^ (2 * chip)) * depth for chip in range(chips)] + [0, half]
    shapes = [(half, query_width)] * 2
    if halved:
        places += [begin, half + begin]
        shapes += [(some, query_width)] * 2
    *halves, near_tokens = cut(places, w_query, hidden, shapes)
    parts = halves[2:]

    direct = [pair_held[side][chip][0][1] for side in range(2) for chip in axes]
    gate = [*direct, cosine, sine, first]
    given, other = [{}, {}], []
    mine = [swap(part, 2 << axis) for part, axis in zip(parts, (bits - 1, 0))]
    if halved:
        other = [lax.ppermute(part, "ctx", [(i, i ^ 1) for i in range(ctx_size)]) for part in mine]
        given = [
            {1 << axis: [(begin, mine[side]), (some - begin, other[side])]}
            for side, axis in enumerate((bits - 1, 0))
        ]
    pair_terms = [
        (
            chip,
            places[chip],
            [(pair_held[side][chip][0][1], 0, side * head_size) for side in range(2)],
        )
        for chip in range(chips)
    ]
    far, near = project(depth, 2 * head_size, pair_terms, near_tokens, far_tokens)
    query_held = fetch(halves[:2], given, [*gate, *mine], [near, *other])

    pair = finish_pair(near, swap(far, 1), cosine, sine)
    longest = ctx_size * row_count // 2
    back = -(-(longest - 1) // ROW_TILE) * ROW_TILE
    hops = min(ctx_size - 1, -(-back // row_count))
    blocks = [
        lax.ppermute(pair, "ctx", [(i, i + hop) for i in range(ctx_size - hop)])
        for hop in range(hops, 0, -1)
    ]
    keys_values = jnp.concatenate(blocks + [pair], axis=0)

    def query_terms(wanted, *gate):
        return [
            (
                chip,
                places[chip],
                [
                    (after(array, *gate), side * half + row, 0)
                    for side in range(2)
                    for row, array in query_held[side][chip]
                ],
            )
            for chip in wanted
        ]

    early = [0] + axes
    late = [chip for chip in range(chips) if chip not in early]
    carry = project(depth, query_width, query_terms(early, pair), near_tokens, far_tokens)
    terms = query_terms(late, *blocks)
    far, near = project(depth, query_width, terms, near_tokens, far_tokens, carry)
    return attend(near, swap(far, 1), cosine, sine, first, keys_values, back)[None]


def solution(mesh):
    return jax.shard_map(
        functools.partial(shards, mesh.shape["dp"], mesh.shape["ctx"]),
        mesh=mesh,
        in_specs=(P("dp", "ctx", None), P("dp", None), P("dp", None), P("dp", None), P("dp", None)),
        out_specs=P("dp", "ctx", None),
        check_vma=False,
    )
```

```python
import functools
import math

import jax
import jax.numpy as jnp
from jax import lax
from jax.experimental import pallas as pl
from jax.experimental.pallas import tpu as pltpu
from jax.sharding import PartitionSpec as P

ROW_TILE = 128
MIB = 1024 * 1024


def rope_tables(positions, head_size):
    half_size = head_size // 2
    exponent = jnp.arange(half_size, dtype=jnp.float32) * (2.0 / head_size)
    inverse = jnp.power(jnp.float32(500000.0), -exponent)
    angles = positions.astype(jnp.float32)[:, None] * inverse[None, :]
    cosine = jnp.cos(angles)
    sine_part = jnp.sin(angles)
    return (
        jnp.concatenate([cosine, cosine], axis=-1),
        jnp.concatenate([-sine_part, sine_part], axis=-1),
    )


def doc_starts(doc_sizes, positions):
    doc_ends = jnp.cumsum(doc_sizes)
    doc_begin = doc_ends - doc_sizes
    chosen = jnp.where(doc_begin[None, :] <= positions[:, None], doc_begin[None, :], 0)
    return jnp.max(chosen, axis=1)


def vmem(count):
    return [pl.BlockSpec(memory_space=pltpu.VMEM)] * count


def anywhere(count):
    return [pl.BlockSpec(memory_space=pl.ANY)] * count


def after(array, *earlier):
    return lax.optimization_barrier((array, *earlier))[0]


def corner(array):
    return array[:8, :128]


def project_kernel(steps, carried, final, starts, near, far, *refs):
    count = sum(len(spots) for _, spots, _ in steps)
    weights, refs = refs[:count], refs[count:]
    if carried:
        carry, refs = refs[0], refs[1:]
    outs, (tokens, held, sems) = refs[:-3], refs[-3:]
    rows = near.shape[0]
    batches = ([], [], [])
    used = row = 0
    for step, (depth, spots, source) in enumerate(steps):
        here = slice(row, row + depth)
        row += depth
        window = pl.ds(pl.multiple_of(starts[step], 128), depth)
        for index, columns in enumerate(spots):
            batches[0].append(
                pltpu.make_async_copy(
                    weights[used].at[source : source + depth],
                    held.at[here, columns],
                    sems.at[step, 2 + index],
                )
            )
            used += 1
        for side, ref in enumerate((far, near)):
            batches[1 + side].append(
                pltpu.make_async_copy(
                    ref.at[:, window], tokens.at[side, :, here], sems.at[step, side]
                )
            )
    for batch in batches:
        for copy in batch:
            copy.start()
    for copy in batches[0]:
        copy.wait()
    for side in range(2):
        for copy in batches[1 + side]:
            copy.wait()
        total = jnp.dot(tokens[side], held[...], preferred_element_type=jnp.float32)
        place = slice((1 - side) * rows, (2 - side) * rows)
        if carried:
            total = total + carry[place, :]
        if final:
            outs[1 - side][...] = total
        else:
            outs[0][place, :] = total


def project(terms, near, far, carry=None, final=False):
    rows = near.shape[0]
    width = sum(array.shape[1] for array in terms[0][1])
    steps = []
    for _, arrays, source, depth in terms:
        edges = [sum(array.shape[1] for array in arrays[:i]) for i in range(len(arrays) + 1)]
        spots = [slice(*edge) for edge in zip(edges[:-1], edges[1:])]
        steps.append((depth, spots, source))
    depth = sum(step[0] for step in steps)
    starts = jnp.stack([start for start, *_ in terms]).astype(jnp.int32)
    weights = [array for _, arrays, *_ in terms for array in arrays]
    whole = jax.ShapeDtypeStruct((2 * rows, width), jnp.float32)
    part = jax.ShapeDtypeStruct((rows, width), jnp.float32)
    carries = [] if carry is None else [carry]
    return pl.pallas_call(
        functools.partial(project_kernel, steps, carry is not None, final),
        out_shape=(part, part) if final else whole,
        in_specs=[pl.BlockSpec(memory_space=pltpu.SMEM)]
        + anywhere(2 + len(weights))
        + vmem(len(carries)),
        out_specs=tuple(vmem(2)) if final else vmem(1)[0],
        scratch_shapes=[
            pltpu.VMEM((2, rows, depth), jnp.bfloat16),
            pltpu.VMEM((depth, width), jnp.bfloat16),
            pltpu.SemaphoreType.DMA((len(steps), 4)),
        ],
        compiler_params=pltpu.CompilerParams(vmem_limit_bytes=48 * MIB),
        cost_estimate=pl.CostEstimate(
            flops=4 * rows * width * depth,
            bytes_accessed=2 * depth * (2 * rows + width),
            transcendentals=0,
        ),
    )(starts, near, far, *weights, *carries)


def turn(vectors, cosine, sine):
    return vectors * cosine + pltpu.roll(vectors, vectors.shape[1] // 2, 1) * sine


def pair_kernel(near, far, cosine, sine, out):
    head_size = cosine.shape[1]
    pair = near[...] + far[...]
    out[:, :head_size] = turn(pair[:, :head_size], cosine[...], sine[...]).astype(out.dtype)
    out[:, head_size:] = pair[:, head_size:].astype(out.dtype)


def finish_pair(near, far, cosine, sine):
    return pl.pallas_call(
        pair_kernel,
        out_shape=jax.ShapeDtypeStruct(near.shape, jnp.bfloat16),
        in_specs=vmem(4),
        out_specs=vmem(1)[0],
        compiler_params=pltpu.CompilerParams(vmem_limit_bytes=8 * MIB),
        cost_estimate=pl.CostEstimate(
            flops=6 * near.size, bytes_accessed=14 * near.size, transcendentals=0
        ),
    )(near, far, cosine, sine)


def attend_kernel(back, near, far, cosine, sine, first, keys_values, out, rotated):
    rows, head_size = cosine.shape
    head_count = near.shape[1] // head_size
    base = keys_values.shape[0] - rows
    tiles = rows // ROW_TILE
    for head in range(head_count):
        columns = slice(head * head_size, (head + 1) * head_size)
        turned = turn(near[:, columns] + far[:, columns], cosine[...], sine[...])
        turned = turned.astype(jnp.bfloat16)
        for tile in range(tiles):
            rotated[tile, head * ROW_TILE : (head + 1) * ROW_TILE, :] = turned[
                tile * ROW_TILE : (tile + 1) * ROW_TILE
            ]
    scale = jnp.float32(math.log2(math.e) / math.sqrt(head_size))
    for tile in range(tiles):
        begin = base + tile * ROW_TILE - back
        window = keys_values[begin : begin + back + ROW_TILE, :]
        scores = lax.dot_general(
            rotated[tile],
            window[:, :head_size],
            (((1,), (1,)), ((), ())),
            preferred_element_type=jnp.float32,
        )
        shape = (ROW_TILE, back + ROW_TILE)
        key_place = lax.broadcasted_iota(jnp.int32, shape, 1) + (tile * ROW_TILE - back)
        row_place = lax.broadcasted_iota(jnp.int32, shape, 0) + tile * ROW_TILE
        lower = first[tile * ROW_TILE : (tile + 1) * ROW_TILE, :]
        allowed = (key_place <= row_place) & (key_place >= lower)
        for head in range(head_count):
            part = scores[head * ROW_TILE : (head + 1) * ROW_TILE]
            part = jnp.where(allowed, part, jnp.float32(-1e30))
            largest = jnp.max(part, axis=-1, keepdims=True)
            exponents = jnp.exp2((part - largest) * scale)
            denominator = jnp.sum(exponents, axis=-1, keepdims=True)
            numerator = jnp.dot(
                exponents.astype(jnp.bfloat16),
                window[:, head_size:],
                preferred_element_type=jnp.float32,
            )
            left = head * head_size
            out[tile * ROW_TILE : (tile + 1) * ROW_TILE, left : left + head_size] = (
                numerator / denominator
            ).astype(out.dtype)


def attend(near, far, cosine, sine, first, keys_values, back):
    rows, width = near.shape
    head_size = cosine.shape[1]
    head_count = width // head_size
    window = back + ROW_TILE
    return pl.pallas_call(
        functools.partial(attend_kernel, back),
        out_shape=jax.ShapeDtypeStruct((rows, width), jnp.bfloat16),
        in_specs=vmem(6),
        out_specs=vmem(1)[0],
        scratch_shapes=[
            pltpu.VMEM((rows // ROW_TILE, head_count * ROW_TILE, head_size), jnp.bfloat16)
        ],
        compiler_params=pltpu.CompilerParams(
            vmem_limit_bytes=8 * MIB + 24 * head_count * ROW_TILE * window
        ),
        cost_estimate=pl.CostEstimate(
            flops=4 * rows * width * window,
            bytes_accessed=8 * rows * width,
            transcendentals=rows * head_count * window,
        ),
    )(near, far, cosine, sine, first, keys_values)


def shards(dp_size, ctx_size, tokens, w_query, w_key, w_value, doc_lengths):
    hidden = tokens[0]
    row_count = hidden.shape[0]
    depth, query_width = w_query.shape
    head_size = w_key.shape[1]
    chips = dp_size // 2
    bits = chips.bit_length() - 1
    me = lax.axis_index("dp")
    place = lax.axis_index("ctx")

    def swap(array, mask):
        return lax.ppermute(array, "dp", [(i, i ^ mask) for i in range(dp_size)])

    def fetch(pair, given, gate, later):
        held = []
        for side, array in enumerate(pair):
            pieces = {0: array, **given[side]}
            reached = [0]
            for axis in list(range(bits))[:: 1 - 2 * side]:
                for source in list(reached):
                    target = source | (1 << axis)
                    reached.append(target)
                    if target not in pieces:
                        sent = after(pieces[source], *(later if source else gate))
                        pieces[target] = swap(sent, 2 << axis)
            held.append(pieces)
        return held

    sibling_hidden = swap(hidden, 1)

    offset = place * row_count
    positions = offset + jnp.arange(row_count, dtype=jnp.int32)
    cosine, sine = rope_tables(positions, head_size)
    first = (doc_starts(doc_lengths[0], positions) - offset)[:, None]

    def begins(chip):
        return (me ^ (2 * chip)) * depth

    axes = [1 << axis for axis in range(bits)]
    half = depth // 2
    some = half // 2
    halved = ctx_size % 2 == 0 and bits > 1
    begin = (place % 2) * some
    halves = [w_query[:half], w_query[half:]]

    pair_held = fetch((w_key, w_value), [{}, {}], [], [])
    pair_terms = [
        (begins(chip), [pair_held[side][chip] for side in range(2)], 0, depth)
        for chip in range(chips)
    ]
    early_chips = [0] + axes
    late_chips = [chip for chip in range(chips) if chip not in early_chips]
    carry = project([pair_terms[chip] for chip in early_chips], hidden, sibling_hidden)
    terms = [pair_terms[chip] for chip in late_chips]
    near, far = project(terms, hidden, sibling_hidden, carry, True)
    pair = finish_pair(near, swap(far, 1), cosine, sine)
    longest = ctx_size * row_count // 2
    back = -(-(longest - 1) // ROW_TILE) * ROW_TILE
    blocks = [pair]
    for _ in range(min(ctx_size - 1, -(-back // row_count))):
        blocks.insert(0, lax.ppermute(blocks[0], "ctx", [(i, i + 1) for i in range(ctx_size - 1)]))
    keys_values = jnp.concatenate(blocks, axis=0)
    direct = [corner(pair_held[side][chip]) for side in range(2) for chip in axes]
    gate = [*direct, cosine, sine, first]
    later = [corner(blocks[-2])]

    early, late = [], []
    given = [{}, {}]
    if halved:
        ends = (0, bits - 1)
        joined = [
            jnp.concatenate(
                [
                    halves[side],
                    lax.dynamic_slice_in_dim(w_query, (1 - side) * half + begin, some, 0),
                ],
                axis=0,
            )
            for side in range(2)
        ]
        got = [swap(after(joined[side], *gate), 2 << ends[side]) for side in range(2)]
        both = jnp.concatenate([after(got[1 - side], *later)[half:] for side in range(2)], axis=0)
        both = lax.ppermute(both, "ctx", [(i, i ^ 1) for i in range(ctx_size)])
        for side in range(2):
            chip = 1 << ends[side]
            given[side][chip] = after(got[side], *later)[:half]
            given[1 - side][chip] = None
            early.append((begins(chip) + side * half, [got[side]], 0, half))
            early.append((begins(chip) + (1 - side) * half + begin, [got[side]], half, some))
            late.append(
                (
                    begins(chip) + (1 - side) * half + some - begin,
                    [both],
                    (1 - side) * some,
                    some,
                )
            )
    query_held = fetch(halves, given, gate, later)
    for side in range(2):
        for chip in range(chips):
            if chip == 0 or chip in late_chips or chip not in given[side]:
                term = (begins(chip) + side * half, [query_held[side][chip]], 0, half)
                (late if chip in late_chips else early).append(term)

    def gated(terms, *gate):
        return [(start, [after(array, *gate) for array in arrays], *rest) for start, arrays, *rest in terms]

    carry = project(gated(early, *later), hidden, sibling_hidden)
    terms = gated(late, corner(blocks[0]))
    near, far = project(terms, hidden, sibling_hidden, carry, True)
    return attend(near, swap(far, 1), cosine, sine, first, keys_values, back)[None]


def solution(mesh):
    return jax.shard_map(
        functools.partial(shards, mesh.shape["dp"], mesh.shape["ctx"]),
        mesh=mesh,
        in_specs=(P("dp", "ctx", None), P("dp", None), P("dp", None), P("dp", None), P("dp", None)),
        out_specs=P("dp", "ctx", None),
        check_vma=False,
    )
```

```python
import functools
import math

import jax
import jax.numpy as jnp
from jax import lax
from jax.experimental import pallas as pl
from jax.experimental.pallas import tpu as pltpu
from jax.sharding import PartitionSpec as P

ROW_TILE = 128
MIB = 1024 * 1024


def rope_tables(positions, head_size):
    half_size = head_size // 2
    exponent = jnp.arange(half_size, dtype=jnp.float32) * (2.0 / head_size)
    inverse = jnp.power(jnp.float32(500000.0), -exponent)
    angles = positions.astype(jnp.float32)[:, None] * inverse[None, :]
    cosine = jnp.cos(angles)
    sine_part = jnp.sin(angles)
    return (
        jnp.concatenate([cosine, cosine], axis=-1),
        jnp.concatenate([-sine_part, sine_part], axis=-1),
    )


def doc_starts(doc_sizes, positions):
    doc_ends = jnp.cumsum(doc_sizes)
    doc_begin = doc_ends - doc_sizes
    chosen = jnp.where(doc_begin[None, :] <= positions[:, None], doc_begin[None, :], 0)
    return jnp.max(chosen, axis=1)


def vmem(count):
    return [pl.BlockSpec(memory_space=pltpu.VMEM)] * count


def anywhere(count):
    return [pl.BlockSpec(memory_space=pl.ANY)] * count


def after(array, *earlier):
    return lax.optimization_barrier((array, *earlier))[0]


def corner(array):
    return array[:8, :128]


def project_kernel(steps, carried, final, starts, near, far, *refs):
    count = sum(len(spots) for _, spots, _ in steps)
    weights, refs = refs[:count], refs[count:]
    if carried:
        carry, refs = refs[0], refs[1:]
    outs, (tokens, held, sems) = refs[:-3], refs[-3:]
    rows = near.shape[0]
    batches = ([], [], [])
    used = row = 0
    for step, (depth, spots, source) in enumerate(steps):
        here = slice(row, row + depth)
        row += depth
        window = pl.ds(pl.multiple_of(starts[step], 128), depth)
        for index, columns in enumerate(spots):
            batches[0].append(
                pltpu.make_async_copy(
                    weights[used].at[source : source + depth],
                    held.at[here, columns],
                    sems.at[step, 2 + index],
                )
            )
            used += 1
        for side, ref in enumerate((far, near)):
            batches[1 + side].append(
                pltpu.make_async_copy(
                    ref.at[:, window], tokens.at[side, :, here], sems.at[step, side]
                )
            )
    for batch in batches:
        for copy in batch:
            copy.start()
    for copy in batches[0]:
        copy.wait()
    for side in range(2):
        for copy in batches[1 + side]:
            copy.wait()
        total = jnp.dot(tokens[side], held[...], preferred_element_type=jnp.float32)
        place = slice((1 - side) * rows, (2 - side) * rows)
        if carried:
            total = total + carry[place, :]
        if final:
            outs[1 - side][...] = total
        else:
            outs[0][place, :] = total


def project(terms, near, far, carry=None, final=False):
    rows = near.shape[0]
    width = sum(array.shape[1] for array in terms[0][1])
    steps = []
    for _, arrays, source, depth in terms:
        edges = [sum(array.shape[1] for array in arrays[:i]) for i in range(len(arrays) + 1)]
        spots = [slice(*edge) for edge in zip(edges[:-1], edges[1:])]
        steps.append((depth, spots, source))
    depth = sum(step[0] for step in steps)
    starts = jnp.stack([start for start, *_ in terms]).astype(jnp.int32)
    weights = [array for _, arrays, *_ in terms for array in arrays]
    whole = jax.ShapeDtypeStruct((2 * rows, width), jnp.float32)
    part = jax.ShapeDtypeStruct((rows, width), jnp.float32)
    carries = [] if carry is None else [carry]
    return pl.pallas_call(
        functools.partial(project_kernel, steps, carry is not None, final),
        out_shape=(part, part) if final else whole,
        in_specs=[pl.BlockSpec(memory_space=pltpu.SMEM)]
        + anywhere(2 + len(weights))
        + vmem(len(carries)),
        out_specs=tuple(vmem(2)) if final else vmem(1)[0],
        scratch_shapes=[
            pltpu.VMEM((2, rows, depth), jnp.bfloat16),
            pltpu.VMEM((depth, width), jnp.bfloat16),
            pltpu.SemaphoreType.DMA((len(steps), 4)),
        ],
        compiler_params=pltpu.CompilerParams(vmem_limit_bytes=48 * MIB),
        cost_estimate=pl.CostEstimate(
            flops=4 * rows * width * depth,
            bytes_accessed=2 * depth * (2 * rows + width),
            transcendentals=0,
        ),
    )(starts, near, far, *weights, *carries)


def turn(vectors, cosine, sine):
    return vectors * cosine + pltpu.roll(vectors, vectors.shape[1] // 2, 1) * sine


def pair_kernel(near, far, cosine, sine, out):
    head_size = cosine.shape[1]
    pair = near[...] + far[...]
    out[:, :head_size] = turn(pair[:, :head_size], cosine[...], sine[...]).astype(out.dtype)
    out[:, head_size:] = pair[:, head_size:].astype(out.dtype)


def finish_pair(near, far, cosine, sine):
    return pl.pallas_call(
        pair_kernel,
        out_shape=jax.ShapeDtypeStruct(near.shape, jnp.bfloat16),
        in_specs=vmem(4),
        out_specs=vmem(1)[0],
        compiler_params=pltpu.CompilerParams(vmem_limit_bytes=8 * MIB),
        cost_estimate=pl.CostEstimate(
            flops=6 * near.size, bytes_accessed=14 * near.size, transcendentals=0
        ),
    )(near, far, cosine, sine)


def attend_kernel(back, near, far, cosine, sine, first, keys_values, out, rotated):
    rows, head_size = cosine.shape
    head_count = near.shape[1] // head_size
    base = keys_values.shape[0] - rows
    tiles = rows // ROW_TILE
    for head in range(head_count):
        columns = slice(head * head_size, (head + 1) * head_size)
        turned = turn(near[:, columns] + far[:, columns], cosine[...], sine[...])
        turned = turned.astype(jnp.bfloat16)
        for tile in range(tiles):
            rotated[tile, head * ROW_TILE : (head + 1) * ROW_TILE, :] = turned[
                tile * ROW_TILE : (tile + 1) * ROW_TILE
            ]
    scale = jnp.float32(math.log2(math.e) / math.sqrt(head_size))
    for tile in range(tiles):
        begin = base + tile * ROW_TILE - back
        window = keys_values[begin : begin + back + ROW_TILE, :]
        scores = lax.dot_general(
            rotated[tile],
            window[:, :head_size],
            (((1,), (1,)), ((), ())),
            preferred_element_type=jnp.float32,
        )
        shape = (ROW_TILE, back + ROW_TILE)
        key_place = lax.broadcasted_iota(jnp.int32, shape, 1) + (tile * ROW_TILE - back)
        row_place = lax.broadcasted_iota(jnp.int32, shape, 0) + tile * ROW_TILE
        lower = first[tile * ROW_TILE : (tile + 1) * ROW_TILE, :]
        allowed = (key_place <= row_place) & (key_place >= lower)
        for head in range(head_count):
            part = scores[head * ROW_TILE : (head + 1) * ROW_TILE]
            part = jnp.where(allowed, part, jnp.float32(-1e30))
            largest = jnp.max(part, axis=-1, keepdims=True)
            exponents = jnp.exp2((part - largest) * scale)
            denominator = jnp.sum(exponents, axis=-1, keepdims=True)
            numerator = jnp.dot(
                exponents.astype(jnp.bfloat16),
                window[:, head_size:],
                preferred_element_type=jnp.float32,
            )
            left = head * head_size
            out[tile * ROW_TILE : (tile + 1) * ROW_TILE, left : left + head_size] = (
                numerator / denominator
            ).astype(out.dtype)


def attend(near, far, cosine, sine, first, keys_values, back):
    rows, width = near.shape
    head_size = cosine.shape[1]
    head_count = width // head_size
    window = back + ROW_TILE
    return pl.pallas_call(
        functools.partial(attend_kernel, back),
        out_shape=jax.ShapeDtypeStruct((rows, width), jnp.bfloat16),
        in_specs=vmem(6),
        out_specs=vmem(1)[0],
        scratch_shapes=[
            pltpu.VMEM((rows // ROW_TILE, head_count * ROW_TILE, head_size), jnp.bfloat16)
        ],
        compiler_params=pltpu.CompilerParams(
            vmem_limit_bytes=8 * MIB + 24 * head_count * ROW_TILE * window
        ),
        cost_estimate=pl.CostEstimate(
            flops=4 * rows * width * window,
            bytes_accessed=8 * rows * width,
            transcendentals=rows * head_count * window,
        ),
    )(near, far, cosine, sine, first, keys_values)


def shards(dp_size, ctx_size, tokens, w_query, w_key, w_value, doc_lengths):
    hidden = tokens[0]
    row_count = hidden.shape[0]
    depth, query_width = w_query.shape
    head_size = w_key.shape[1]
    chips = dp_size // 2
    bits = chips.bit_length() - 1
    me = lax.axis_index("dp")
    place = lax.axis_index("ctx")

    def swap(array, mask):
        return lax.ppermute(array, "dp", [(i, i ^ mask) for i in range(dp_size)])

    def fetch(pair, given, gate, later):
        held = []
        for side, array in enumerate(pair):
            pieces = {0: array, **given[side]}
            reached = [0]
            for axis in list(range(bits))[:: 1 - 2 * side]:
                for source in list(reached):
                    target = source | (1 << axis)
                    reached.append(target)
                    if target not in pieces:
                        sent = after(pieces[source], *(later if source else gate))
                        pieces[target] = swap(sent, 2 << axis)
            held.append(pieces)
        return held

    sibling_hidden = swap(hidden, 1)

    offset = place * row_count
    positions = offset + jnp.arange(row_count, dtype=jnp.int32)
    cosine, sine = rope_tables(positions, head_size)
    first = (doc_starts(doc_lengths[0], positions) - offset)[:, None]

    def begins(chip):
        return (me ^ (2 * chip)) * depth

    axes = [1 << axis for axis in range(bits)]
    half = depth // 2
    lack = 128
    keep = half - lack
    halved = ctx_size % 2 == 0 and bits > 1 and keep > 0
    odd = place % 2
    halves = [w_query[:half], w_query[half:]]

    pair_held = fetch((w_key, w_value), [{}, {}], [], [])
    pair_terms = [
        (begins(chip), [pair_held[side][chip] for side in range(2)], 0, depth)
        for chip in range(chips)
    ]
    early_chips = [0] + axes
    late_chips = [chip for chip in range(chips) if chip not in early_chips]
    carry = project([pair_terms[chip] for chip in early_chips], hidden, sibling_hidden)
    terms = [pair_terms[chip] for chip in late_chips]
    near, far = project(terms, hidden, sibling_hidden, carry, True)
    pair = finish_pair(near, swap(far, 1), cosine, sine)
    longest = ctx_size * row_count // 2
    back = -(-(longest - 1) // ROW_TILE) * ROW_TILE
    blocks = [pair]
    for _ in range(min(ctx_size - 1, -(-back // row_count))):
        blocks.insert(0, lax.ppermute(blocks[0], "ctx", [(i, i + 1) for i in range(ctx_size - 1)]))
    keys_values = jnp.concatenate(blocks, axis=0)
    direct = [pair_held[0][axes[-1]], pair_held[1][axes[0]]]
    gate = [*direct, cosine, sine, first]
    later = [corner(blocks[-2])]

    early, late = [], []
    given = [{}, {}]
    if halved:
        ends = (0, bits - 1)
        joined = [
            jnp.concatenate(
                [
                    halves[side],
                    lax.dynamic_slice_in_dim(w_query, (1 - side) * half + odd * lack, keep, 0),
                ],
                axis=0,
            )
            for side in range(2)
        ]
        got = [swap(after(joined[side], *gate), 2 << ends[side]) for side in range(2)]
        row = half + odd * (keep - lack)
        both = [
            lax.dynamic_slice_in_dim(after(got[1 - side], *later), row, lack, 0)
            for side in range(2)
        ]
        both = jnp.concatenate(both, axis=0)
        both = lax.ppermute(both, "ctx", [(i, i ^ 1) for i in range(ctx_size)])
        for side in range(2):
            chip = 1 << ends[side]
            given[side][chip] = after(got[side], *later)[:half]
            given[1 - side][chip] = None
            early.append((begins(chip) + side * half, [got[side]], 0, half))
            first_row = begins(chip) + (1 - side) * half
            early.append((first_row + odd * lack, [got[side]], half, keep))
            late.append((first_row + (1 - odd) * keep, [both], (1 - side) * lack, lack))
    query_held = fetch(halves, given, gate, later)
    for side in range(2):
        for chip in range(chips):
            if chip == 0 or chip in late_chips or chip not in given[side]:
                term = (begins(chip) + side * half, [query_held[side][chip]], 0, half)
                (late if chip in late_chips else early).append(term)

    def gated(terms, *gate):
        return [(start, [after(array, *gate) for array in arrays], *rest) for start, arrays, *rest in terms]

    carry = project(gated(early, *later), hidden, sibling_hidden)
    terms = gated(late, corner(blocks[0]))
    near, far = project(terms, hidden, sibling_hidden, carry, True)
    return attend(near, swap(far, 1), cosine, sine, first, keys_values, back)[None]


def solution(mesh):
    return jax.shard_map(
        functools.partial(shards, mesh.shape["dp"], mesh.shape["ctx"]),
        mesh=mesh,
        in_specs=(P("dp", "ctx", None), P("dp", None), P("dp", None), P("dp", None), P("dp", None)),
        out_specs=P("dp", "ctx", None),
        check_vma=False,
    )
```

```python
import functools
import math

import jax
import jax.numpy as jnp
from jax import lax
from jax.experimental import pallas as pl
from jax.experimental.pallas import tpu as pltpu
from jax.sharding import PartitionSpec as P

ROW_TILE = 128
MIB = 1024 * 1024


def rope_tables(positions, head_size):
    half_size = head_size // 2
    exponent = jnp.arange(half_size, dtype=jnp.float32) * (2.0 / head_size)
    inverse = jnp.power(jnp.float32(500000.0), -exponent)
    angles = positions.astype(jnp.float32)[:, None] * inverse[None, :]
    cosine = jnp.cos(angles)
    sine_part = jnp.sin(angles)
    return (
        jnp.concatenate([cosine, cosine], axis=-1),
        jnp.concatenate([-sine_part, sine_part], axis=-1),
    )


def doc_starts(doc_sizes, positions):
    doc_ends = jnp.cumsum(doc_sizes)
    doc_begin = doc_ends - doc_sizes
    chosen = jnp.where(doc_begin[None, :] <= positions[:, None], doc_begin[None, :], 0)
    return jnp.max(chosen, axis=1)


def vmem(count):
    return [pl.BlockSpec(memory_space=pltpu.VMEM)] * count


def anywhere(count):
    return [pl.BlockSpec(memory_space=pl.ANY)] * count


def after(array, *earlier):
    return lax.optimization_barrier((array, *earlier))[0]


def corner(array):
    return array[:8, :128]


def project_kernel(steps, carried, final, starts, near, far, *refs):
    count = sum(len(spots) for _, spots, _ in steps)
    weights, refs = refs[:count], refs[count:]
    if carried:
        carry, refs = refs[0], refs[1:]
    outs, (tokens, held, sems) = refs[:-3], refs[-3:]
    rows = near.shape[0]
    batches = ([], [], [])
    used = row = 0
    for step, (depth, spots, source) in enumerate(steps):
        here = slice(row, row + depth)
        row += depth
        window = pl.ds(pl.multiple_of(starts[step], 128), depth)
        for index, columns in enumerate(spots):
            batches[0].append(
                pltpu.make_async_copy(
                    weights[used].at[source : source + depth],
                    held.at[here, columns],
                    sems.at[step, 2 + index],
                )
            )
            used += 1
        for side, ref in enumerate((far, near)):
            batches[1 + side].append(
                pltpu.make_async_copy(
                    ref.at[:, window], tokens.at[side, :, here], sems.at[step, side]
                )
            )
    for batch in batches:
        for copy in batch:
            copy.start()
    for copy in batches[0]:
        copy.wait()
    for side in range(2):
        for copy in batches[1 + side]:
            copy.wait()
        total = jnp.dot(tokens[side], held[...], preferred_element_type=jnp.float32)
        place = slice((1 - side) * rows, (2 - side) * rows)
        if carried:
            total = total + carry[place, :]
        if final:
            outs[1 - side][...] = total
        else:
            outs[0][place, :] = total


def project(terms, near, far, carry=None, final=False):
    rows = near.shape[0]
    width = sum(array.shape[1] for array in terms[0][1])
    steps = []
    for _, arrays, source, depth in terms:
        edges = [sum(array.shape[1] for array in arrays[:i]) for i in range(len(arrays) + 1)]
        spots = [slice(*edge) for edge in zip(edges[:-1], edges[1:])]
        steps.append((depth, spots, source))
    depth = sum(step[0] for step in steps)
    starts = jnp.stack([start for start, *_ in terms]).astype(jnp.int32)
    weights = [array for _, arrays, *_ in terms for array in arrays]
    whole = jax.ShapeDtypeStruct((2 * rows, width), jnp.float32)
    part = jax.ShapeDtypeStruct((rows, width), jnp.float32)
    carries = [] if carry is None else [carry]
    return pl.pallas_call(
        functools.partial(project_kernel, steps, carry is not None, final),
        out_shape=(part, part) if final else whole,
        in_specs=[pl.BlockSpec(memory_space=pltpu.SMEM)]
        + anywhere(2 + len(weights))
        + vmem(len(carries)),
        out_specs=tuple(vmem(2)) if final else vmem(1)[0],
        scratch_shapes=[
            pltpu.VMEM((2, rows, depth), jnp.bfloat16),
            pltpu.VMEM((depth, width), jnp.bfloat16),
            pltpu.SemaphoreType.DMA((len(steps), 4)),
        ],
        compiler_params=pltpu.CompilerParams(vmem_limit_bytes=48 * MIB),
        cost_estimate=pl.CostEstimate(
            flops=4 * rows * width * depth,
            bytes_accessed=2 * depth * (2 * rows + width),
            transcendentals=0,
        ),
    )(starts, near, far, *weights, *carries)


def turn(vectors, cosine, sine):
    return vectors * cosine + pltpu.roll(vectors, vectors.shape[1] // 2, 1) * sine


def pair_kernel(near, far, cosine, sine, out):
    head_size = cosine.shape[1]
    pair = near[...] + far[...]
    out[:, :head_size] = turn(pair[:, :head_size], cosine[...], sine[...]).astype(out.dtype)
    out[:, head_size:] = pair[:, head_size:].astype(out.dtype)


def finish_pair(near, far, cosine, sine):
    return pl.pallas_call(
        pair_kernel,
        out_shape=jax.ShapeDtypeStruct(near.shape, jnp.bfloat16),
        in_specs=vmem(4),
        out_specs=vmem(1)[0],
        compiler_params=pltpu.CompilerParams(vmem_limit_bytes=8 * MIB),
        cost_estimate=pl.CostEstimate(
            flops=6 * near.size, bytes_accessed=14 * near.size, transcendentals=0
        ),
    )(near, far, cosine, sine)


def attend_kernel(back, near, far, cosine, sine, first, keys_values, out, rotated):
    rows, head_size = cosine.shape
    head_count = near.shape[1] // head_size
    base = keys_values.shape[0] - rows
    tiles = rows // ROW_TILE
    for head in range(head_count):
        columns = slice(head * head_size, (head + 1) * head_size)
        turned = turn(near[:, columns] + far[:, columns], cosine[...], sine[...])
        turned = turned.astype(jnp.bfloat16)
        for tile in range(tiles):
            rotated[tile, head * ROW_TILE : (head + 1) * ROW_TILE, :] = turned[
                tile * ROW_TILE : (tile + 1) * ROW_TILE
            ]
    scale = jnp.float32(math.log2(math.e) / math.sqrt(head_size))
    for tile in range(tiles):
        begin = base + tile * ROW_TILE - back
        window = keys_values[begin : begin + back + ROW_TILE, :]
        scores = lax.dot_general(
            rotated[tile],
            window[:, :head_size],
            (((1,), (1,)), ((), ())),
            preferred_element_type=jnp.float32,
        )
        shape = (ROW_TILE, back + ROW_TILE)
        key_place = lax.broadcasted_iota(jnp.int32, shape, 1) + (tile * ROW_TILE - back)
        row_place = lax.broadcasted_iota(jnp.int32, shape, 0) + tile * ROW_TILE
        lower = first[tile * ROW_TILE : (tile + 1) * ROW_TILE, :]
        allowed = (key_place <= row_place) & (key_place >= lower)
        for head in range(head_count):
            part = scores[head * ROW_TILE : (head + 1) * ROW_TILE]
            part = jnp.where(allowed, part, jnp.float32(-1e30))
            largest = jnp.max(part, axis=-1, keepdims=True)
            exponents = jnp.exp2((part - largest) * scale)
            denominator = jnp.sum(exponents, axis=-1, keepdims=True)
            numerator = jnp.dot(
                exponents.astype(jnp.bfloat16),
                window[:, head_size:],
                preferred_element_type=jnp.float32,
            )
            left = head * head_size
            out[tile * ROW_TILE : (tile + 1) * ROW_TILE, left : left + head_size] = (
                numerator / denominator
            ).astype(out.dtype)


def attend(near, far, cosine, sine, first, keys_values, back):
    rows, width = near.shape
    head_size = cosine.shape[1]
    head_count = width // head_size
    window = back + ROW_TILE
    return pl.pallas_call(
        functools.partial(attend_kernel, back),
        out_shape=jax.ShapeDtypeStruct((rows, width), jnp.bfloat16),
        in_specs=vmem(6),
        out_specs=vmem(1)[0],
        scratch_shapes=[
            pltpu.VMEM((rows // ROW_TILE, head_count * ROW_TILE, head_size), jnp.bfloat16)
        ],
        compiler_params=pltpu.CompilerParams(
            vmem_limit_bytes=8 * MIB + 24 * head_count * ROW_TILE * window
        ),
        cost_estimate=pl.CostEstimate(
            flops=4 * rows * width * window,
            bytes_accessed=8 * rows * width,
            transcendentals=rows * head_count * window,
        ),
    )(near, far, cosine, sine, first, keys_values)


def shards(dp_size, ctx_size, tokens, w_query, w_key, w_value, doc_lengths):
    hidden = tokens[0]
    row_count = hidden.shape[0]
    depth, query_width = w_query.shape
    head_size = w_key.shape[1]
    chips = dp_size // 2
    bits = chips.bit_length() - 1
    me = lax.axis_index("dp")
    place = lax.axis_index("ctx")

    def swap(array, mask):
        return lax.ppermute(array, "dp", [(i, i ^ mask) for i in range(dp_size)])

    def fetch(pair, given, gate, later):
        held = []
        for side, array in enumerate(pair):
            pieces = {0: array, **given[side]}
            reached = [0]
            for axis in list(range(bits))[:: 1 - 2 * side]:
                for source in list(reached):
                    target = source | (1 << axis)
                    reached.append(target)
                    if target not in pieces:
                        sent = after(pieces[source], *(later if source else gate))
                        pieces[target] = swap(sent, 2 << axis)
            held.append(pieces)
        return held

    sibling_hidden = swap(hidden, 1)

    offset = place * row_count
    positions = offset + jnp.arange(row_count, dtype=jnp.int32)
    cosine, sine = rope_tables(positions, head_size)
    first = (doc_starts(doc_lengths[0], positions) - offset)[:, None]

    def begins(chip):
        return (me ^ (2 * chip)) * depth

    axes = [1 << axis for axis in range(bits)]
    half = depth // 2
    some = half // 2
    halved = ctx_size % 2 == 0 and bits > 1
    odd = place % 2
    begin = odd * some
    lack = some // 2 if some % 256 == 0 else some
    more = some - lack
    halves = [w_query[:half], w_query[half:]]

    pair_held = fetch((w_key, w_value), [{}, {}], [], [])
    pair_terms = [
        (begins(chip), [pair_held[side][chip] for side in range(2)], 0, depth)
        for chip in range(chips)
    ]
    early_chips = [0] + axes
    late_chips = [chip for chip in range(chips) if chip not in early_chips]
    carry = project([pair_terms[chip] for chip in early_chips], hidden, sibling_hidden)
    terms = [pair_terms[chip] for chip in late_chips]
    near, far = project(terms, hidden, sibling_hidden, carry, True)
    pair = finish_pair(near, swap(far, 1), cosine, sine)
    longest = ctx_size * row_count // 2
    back = -(-(longest - 1) // ROW_TILE) * ROW_TILE
    blocks = [pair]
    for _ in range(min(ctx_size - 1, -(-back // row_count))):
        blocks.insert(0, lax.ppermute(blocks[0], "ctx", [(i, i + 1) for i in range(ctx_size - 1)]))
    keys_values = jnp.concatenate(blocks, axis=0)
    direct = [corner(pair_held[side][chip]) for side in range(2) for chip in axes]
    gate = [*direct, cosine, sine, first]
    later = [corner(blocks[-2])]

    early, late = [], []
    given = [{}, {}]
    if halved:
        ends = (0, bits - 1)
        joined = [
            jnp.concatenate(
                [
                    halves[side],
                    lax.dynamic_slice_in_dim(w_query, (1 - side) * half + begin, some, 0),
                ],
                axis=0,
            )
            for side in range(2)
        ]
        got = [swap(after(joined[side], *gate), 2 << ends[side]) for side in range(2)]
        both = [
            lax.dynamic_slice_in_dim(after(got[1 - side], *later), half + odd * more, lack, 0)
            for side in range(2)
        ]
        both = jnp.concatenate(both, axis=0)
        both = lax.ppermute(both, "ctx", [(i, i ^ 1) for i in range(ctx_size)])
        for side in range(2):
            chip = 1 << ends[side]
            given[side][chip] = after(got[side], *later)[:half]
            given[1 - side][chip] = None
            early.append((begins(chip) + side * half, [got[side]], 0, half))
            early.append((begins(chip) + (1 - side) * half + begin, [got[side]], half, some))
            first_row = begins(chip) + (1 - side) * half
            if more:
                row = some - odd * more
                part = lax.dynamic_slice_in_dim(w_query, (1 - side) * half + row, more, 0)
                part = swap(after(part, corner(near)), 2 << ends[side])
                early.append((first_row + row, [part], 0, more))
            late.append((first_row + (1 - odd) * (half - lack), [both], (1 - side) * lack, lack))
    query_held = fetch(halves, given, gate, later)
    for side in range(2):
        for chip in range(chips):
            if chip == 0 or chip in late_chips or chip not in given[side]:
                term = (begins(chip) + side * half, [query_held[side][chip]], 0, half)
                (late if chip in late_chips else early).append(term)

    def gated(terms, *gate):
        return [(start, [after(array, *gate) for array in arrays], *rest) for start, arrays, *rest in terms]

    carry = project(gated(early, *later), hidden, sibling_hidden)
    terms = gated(late, corner(blocks[0]))
    near, far = project(terms, hidden, sibling_hidden, carry, True)
    return attend(near, swap(far, 1), cosine, sine, first, keys_values, back)[None]


def solution(mesh):
    return jax.shard_map(
        functools.partial(shards, mesh.shape["dp"], mesh.shape["ctx"]),
        mesh=mesh,
        in_specs=(P("dp", "ctx", None), P("dp", None), P("dp", None), P("dp", None), P("dp", None)),
        out_specs=P("dp", "ctx", None),
        check_vma=False,
    )
```

```python
import functools
import math

import jax
import jax.numpy as jnp
from jax import lax
from jax.experimental import pallas as pl
from jax.experimental.pallas import tpu as pltpu
from jax.sharding import PartitionSpec as P

ROW_TILE = 128
MIB = 1024 * 1024


def rope_tables(positions, head_size):
    half_size = head_size // 2
    exponent = jnp.arange(half_size, dtype=jnp.float32) * (2.0 / head_size)
    inverse = jnp.power(jnp.float32(500000.0), -exponent)
    angles = positions.astype(jnp.float32)[:, None] * inverse[None, :]
    cosine = jnp.cos(angles)
    sine_part = jnp.sin(angles)
    return (
        jnp.concatenate([cosine, cosine], axis=-1),
        jnp.concatenate([-sine_part, sine_part], axis=-1),
    )


def doc_starts(doc_sizes, positions):
    doc_ends = jnp.cumsum(doc_sizes)
    doc_begin = doc_ends - doc_sizes
    chosen = jnp.where(doc_begin[None, :] <= positions[:, None], doc_begin[None, :], 0)
    return jnp.max(chosen, axis=1)


def vmem(count):
    return [pl.BlockSpec(memory_space=pltpu.VMEM)] * count


def anywhere(count):
    return [pl.BlockSpec(memory_space=pl.ANY)] * count


def after(array, *earlier):
    return lax.optimization_barrier((array, *earlier))[0]


def corner(array):
    return array[:8, :128]


def project_kernel(steps, carried, final, starts, near, far, *refs):
    count = sum(len(spots) for _, spots, _ in steps)
    weights, refs = refs[:count], refs[count:]
    if carried:
        carry, refs = refs[0], refs[1:]
    outs, (tokens, held, sems) = refs[:-3], refs[-3:]
    rows = near.shape[0]
    batches = ([], [], [])
    used = row = 0
    for step, (depth, spots, source) in enumerate(steps):
        here = slice(row, row + depth)
        row += depth
        window = pl.ds(pl.multiple_of(starts[step], 128), depth)
        for index, columns in enumerate(spots):
            batches[0].append(
                pltpu.make_async_copy(
                    weights[used].at[source : source + depth],
                    held.at[here, columns],
                    sems.at[step, 2 + index],
                )
            )
            used += 1
        for side, ref in enumerate((far, near)):
            batches[1 + side].append(
                pltpu.make_async_copy(
                    ref.at[:, window], tokens.at[side, :, here], sems.at[step, side]
                )
            )
    for batch in batches:
        for copy in batch:
            copy.start()
    for copy in batches[0]:
        copy.wait()
    for side in range(2):
        for copy in batches[1 + side]:
            copy.wait()
        total = jnp.dot(tokens[side], held[...], preferred_element_type=jnp.float32)
        place = slice((1 - side) * rows, (2 - side) * rows)
        if carried:
            total = total + carry[place, :]
        if final:
            outs[1 - side][...] = total
        else:
            outs[0][place, :] = total


def project(terms, near, far, carry=None, final=False):
    rows = near.shape[0]
    width = sum(array.shape[1] for array in terms[0][1])
    steps = []
    for _, arrays, source, depth in terms:
        edges = [sum(array.shape[1] for array in arrays[:i]) for i in range(len(arrays) + 1)]
        spots = [slice(*edge) for edge in zip(edges[:-1], edges[1:])]
        steps.append((depth, spots, source))
    depth = sum(step[0] for step in steps)
    starts = jnp.stack([start for start, *_ in terms]).astype(jnp.int32)
    weights = [array for _, arrays, *_ in terms for array in arrays]
    whole = jax.ShapeDtypeStruct((2 * rows, width), jnp.float32)
    part = jax.ShapeDtypeStruct((rows, width), jnp.float32)
    carries = [] if carry is None else [carry]
    return pl.pallas_call(
        functools.partial(project_kernel, steps, carry is not None, final),
        out_shape=(part, part) if final else whole,
        in_specs=[pl.BlockSpec(memory_space=pltpu.SMEM)]
        + anywhere(2 + len(weights))
        + vmem(len(carries)),
        out_specs=tuple(vmem(2)) if final else vmem(1)[0],
        scratch_shapes=[
            pltpu.VMEM((2, rows, depth), jnp.bfloat16),
            pltpu.VMEM((depth, width), jnp.bfloat16),
            pltpu.SemaphoreType.DMA((len(steps), 4)),
        ],
        compiler_params=pltpu.CompilerParams(vmem_limit_bytes=48 * MIB),
        cost_estimate=pl.CostEstimate(
            flops=4 * rows * width * depth,
            bytes_accessed=2 * depth * (2 * rows + width),
            transcendentals=0,
        ),
    )(starts, near, far, *weights, *carries)


def turn(vectors, cosine, sine):
    return vectors * cosine + pltpu.roll(vectors, vectors.shape[1] // 2, 1) * sine


def pair_kernel(near, far, cosine, sine, out):
    head_size = cosine.shape[1]
    pair = near[...] + far[...]
    out[:, :head_size] = turn(pair[:, :head_size], cosine[...], sine[...]).astype(out.dtype)
    out[:, head_size:] = pair[:, head_size:].astype(out.dtype)


def finish_pair(near, far, cosine, sine):
    return pl.pallas_call(
        pair_kernel,
        out_shape=jax.ShapeDtypeStruct(near.shape, jnp.bfloat16),
        in_specs=vmem(4),
        out_specs=vmem(1)[0],
        compiler_params=pltpu.CompilerParams(vmem_limit_bytes=8 * MIB),
        cost_estimate=pl.CostEstimate(
            flops=6 * near.size, bytes_accessed=14 * near.size, transcendentals=0
        ),
    )(near, far, cosine, sine)


def attend_kernel(back, near, far, cosine, sine, first, keys_values, out, rotated):
    rows, head_size = cosine.shape
    head_count = near.shape[1] // head_size
    base = keys_values.shape[0] - rows
    tiles = rows // ROW_TILE
    for head in range(head_count):
        columns = slice(head * head_size, (head + 1) * head_size)
        turned = turn(near[:, columns] + far[:, columns], cosine[...], sine[...])
        turned = turned.astype(jnp.bfloat16)
        for tile in range(tiles):
            rotated[tile, head * ROW_TILE : (head + 1) * ROW_TILE, :] = turned[
                tile * ROW_TILE : (tile + 1) * ROW_TILE
            ]
    scale = jnp.float32(math.log2(math.e) / math.sqrt(head_size))
    for tile in range(tiles):
        begin = base + tile * ROW_TILE - back
        window = keys_values[begin : begin + back + ROW_TILE, :]
        scores = lax.dot_general(
            rotated[tile],
            window[:, :head_size],
            (((1,), (1,)), ((), ())),
            preferred_element_type=jnp.float32,
        )
        shape = (ROW_TILE, back + ROW_TILE)
        key_place = lax.broadcasted_iota(jnp.int32, shape, 1) + (tile * ROW_TILE - back)
        row_place = lax.broadcasted_iota(jnp.int32, shape, 0) + tile * ROW_TILE
        lower = first[tile * ROW_TILE : (tile + 1) * ROW_TILE, :]
        allowed = (key_place <= row_place) & (key_place >= lower)
        for head in range(head_count):
            part = scores[head * ROW_TILE : (head + 1) * ROW_TILE]
            part = jnp.where(allowed, part, jnp.float32(-1e30))
            largest = jnp.max(part, axis=-1, keepdims=True)
            exponents = jnp.exp2((part - largest) * scale)
            denominator = jnp.sum(exponents, axis=-1, keepdims=True)
            numerator = jnp.dot(
                exponents.astype(jnp.bfloat16),
                window[:, head_size:],
                preferred_element_type=jnp.float32,
            )
            left = head * head_size
            out[tile * ROW_TILE : (tile + 1) * ROW_TILE, left : left + head_size] = (
                numerator / denominator
            ).astype(out.dtype)


def attend(near, far, cosine, sine, first, keys_values, back):
    rows, width = near.shape
    head_size = cosine.shape[1]
    head_count = width // head_size
    window = back + ROW_TILE
    return pl.pallas_call(
        functools.partial(attend_kernel, back),
        out_shape=jax.ShapeDtypeStruct((rows, width), jnp.bfloat16),
        in_specs=vmem(6),
        out_specs=vmem(1)[0],
        scratch_shapes=[
            pltpu.VMEM((rows // ROW_TILE, head_count * ROW_TILE, head_size), jnp.bfloat16)
        ],
        compiler_params=pltpu.CompilerParams(
            vmem_limit_bytes=8 * MIB + 24 * head_count * ROW_TILE * window
        ),
        cost_estimate=pl.CostEstimate(
            flops=4 * rows * width * window,
            bytes_accessed=8 * rows * width,
            transcendentals=rows * head_count * window,
        ),
    )(near, far, cosine, sine, first, keys_values)


def shards(dp_size, ctx_size, tokens, w_query, w_key, w_value, doc_lengths):
    hidden = tokens[0]
    row_count = hidden.shape[0]
    depth, query_width = w_query.shape
    head_size = w_key.shape[1]
    chips = dp_size // 2
    bits = chips.bit_length() - 1
    me = lax.axis_index("dp")
    place = lax.axis_index("ctx")

    def swap(array, mask):
        return lax.ppermute(array, "dp", [(i, i ^ mask) for i in range(dp_size)])

    def fetch(pair, given, gate, later):
        held = []
        for side, array in enumerate(pair):
            pieces = {0: array, **given[side]}
            reached = [0]
            for axis in list(range(bits))[:: 1 - 2 * side]:
                for source in list(reached):
                    target = source | (1 << axis)
                    reached.append(target)
                    if target not in pieces:
                        sent = after(pieces[source], *(later if source else gate))
                        pieces[target] = swap(sent, 2 << axis)
            held.append(pieces)
        return held

    sibling_hidden = swap(hidden, 1)

    offset = place * row_count
    positions = offset + jnp.arange(row_count, dtype=jnp.int32)
    cosine, sine = rope_tables(positions, head_size)
    first = (doc_starts(doc_lengths[0], positions) - offset)[:, None]

    def begins(chip):
        return (me ^ (2 * chip)) * depth

    axes = [1 << axis for axis in range(bits)]
    half = depth // 2
    some = half // 2
    halved = ctx_size % 2 == 0 and bits > 1
    odd = place % 2
    begin = odd * some
    lack = some // 2 if some % 256 == 0 else some
    more = some - lack
    halves = [w_query[:half], w_query[half:]]

    pair_held = fetch((w_key, w_value), [{}, {}], [], [])
    pair_terms = [
        (begins(chip), [pair_held[side][chip] for side in range(2)], 0, depth)
        for chip in range(chips)
    ]
    early_chips = [0] + axes
    late_chips = [chip for chip in range(chips) if chip not in early_chips]
    carry = project([pair_terms[chip] for chip in early_chips], hidden, sibling_hidden)
    terms = [pair_terms[chip] for chip in late_chips]
    near, far = project(terms, hidden, sibling_hidden, carry, True)
    pair = finish_pair(near, swap(far, 1), cosine, sine)
    longest = ctx_size * row_count // 2
    back = -(-(longest - 1) // ROW_TILE) * ROW_TILE
    blocks = [pair]
    for _ in range(min(ctx_size - 1, -(-back // row_count))):
        blocks.insert(0, lax.ppermute(blocks[0], "ctx", [(i, i + 1) for i in range(ctx_size - 1)]))
    keys_values = jnp.concatenate(blocks, axis=0)
    direct = [corner(pair_held[0][axes[0]]), corner(pair_held[1][axes[-1]])]
    gate = [*direct, cosine, sine, first]
    later = [corner(blocks[-2])]

    early, late = [], []
    given = [{}, {}]
    if halved:
        ends = (0, bits - 1)
        joined = [
            jnp.concatenate(
                [
                    halves[side],
                    lax.dynamic_slice_in_dim(w_query, (1 - side) * half + begin, some, 0),
                ],
                axis=0,
            )
            for side in range(2)
        ]
        got = [swap(after(joined[side], *gate), 2 << ends[side]) for side in range(2)]
        both = [
            lax.dynamic_slice_in_dim(after(got[1 - side], *later), half + odd * more, lack, 0)
            for side in range(2)
        ]
        both = jnp.concatenate(both, axis=0)
        both = lax.ppermute(both, "ctx", [(i, i ^ 1) for i in range(ctx_size)])
        for side in range(2):
            chip = 1 << ends[side]
            given[side][chip] = after(got[side], *later)[:half]
            given[1 - side][chip] = None
            early.append((begins(chip) + side * half, [got[side]], 0, half))
            early.append((begins(chip) + (1 - side) * half + begin, [got[side]], half, some))
            first_row = begins(chip) + (1 - side) * half
            if more:
                row = some - odd * more
                part = lax.dynamic_slice_in_dim(w_query, (1 - side) * half + row, more, 0)
                part = swap(after(part, corner(near)), 2 << ends[side])
                early.append((first_row + row, [part], 0, more))
            late.append((first_row + (1 - odd) * (half - lack), [both], (1 - side) * lack, lack))
    query_held = fetch(halves, given, gate, later)
    for side in range(2):
        for chip in range(chips):
            if chip == 0 or chip in late_chips or chip not in given[side]:
                term = (begins(chip) + side * half, [query_held[side][chip]], 0, half)
                (late if chip in late_chips else early).append(term)

    def gated(terms, *gate):
        return [(start, [after(array, *gate) for array in arrays], *rest) for start, arrays, *rest in terms]

    carry = project(gated(early, *later), hidden, sibling_hidden)
    terms = gated(late, corner(blocks[0]))
    near, far = project(terms, hidden, sibling_hidden, carry, True)
    return attend(near, swap(far, 1), cosine, sine, first, keys_values, back)[None]


def solution(mesh):
    return jax.shard_map(
        functools.partial(shards, mesh.shape["dp"], mesh.shape["ctx"]),
        mesh=mesh,
        in_specs=(P("dp", "ctx", None), P("dp", None), P("dp", None), P("dp", None), P("dp", None)),
        out_specs=P("dp", "ctx", None),
        check_vma=False,
    )
```

```python
import functools
import math

import jax
import jax.numpy as jnp
from jax import lax
from jax.experimental import pallas as pl
from jax.experimental.pallas import tpu as pltpu
from jax.sharding import PartitionSpec as P

ROW_TILE = 128
MIB = 1024 * 1024


def rope_tables(positions, head_size):
    half_size = head_size // 2
    exponent = jnp.arange(half_size, dtype=jnp.float32) * (2.0 / head_size)
    inverse = jnp.power(jnp.float32(500000.0), -exponent)
    angles = positions.astype(jnp.float32)[:, None] * inverse[None, :]
    cosine = jnp.cos(angles)
    sine_part = jnp.sin(angles)
    return (
        jnp.concatenate([cosine, cosine], axis=-1),
        jnp.concatenate([-sine_part, sine_part], axis=-1),
    )


def doc_starts(doc_sizes, positions):
    doc_ends = jnp.cumsum(doc_sizes)
    doc_begin = doc_ends - doc_sizes
    chosen = jnp.where(doc_begin[None, :] <= positions[:, None], doc_begin[None, :], 0)
    return jnp.max(chosen, axis=1)


def vmem(count):
    return [pl.BlockSpec(memory_space=pltpu.VMEM)] * count


def anywhere(count):
    return [pl.BlockSpec(memory_space=pl.ANY)] * count


def after(array, *earlier):
    return lax.optimization_barrier((array, *earlier))[0]


def corner(array):
    return array[:8, :128]


def project_kernel(steps, carried, final, starts, near, far, *refs):
    count = sum(len(spots) for _, spots, _ in steps)
    weights, refs = refs[:count], refs[count:]
    if carried:
        carry, refs = refs[0], refs[1:]
    outs, (tokens, held, sems) = refs[:-3], refs[-3:]
    rows = near.shape[0]
    batches = ([], [], [])
    used = row = 0
    for step, (depth, spots, source) in enumerate(steps):
        here = slice(row, row + depth)
        row += depth
        window = pl.ds(pl.multiple_of(starts[step], 128), depth)
        for index, columns in enumerate(spots):
            batches[0].append(
                pltpu.make_async_copy(
                    weights[used].at[source : source + depth],
                    held.at[here, columns],
                    sems.at[step, 2 + index],
                )
            )
            used += 1
        for side, ref in enumerate((far, near)):
            batches[1 + side].append(
                pltpu.make_async_copy(
                    ref.at[:, window], tokens.at[side, :, here], sems.at[step, side]
                )
            )
    for batch in batches:
        for copy in batch:
            copy.start()
    for copy in batches[0]:
        copy.wait()
    for side in range(2):
        for copy in batches[1 + side]:
            copy.wait()
        total = jnp.dot(tokens[side], held[...], preferred_element_type=jnp.float32)
        place = slice((1 - side) * rows, (2 - side) * rows)
        if carried:
            total = total + carry[place, :]
        if final:
            outs[1 - side][...] = total
        else:
            outs[0][place, :] = total


def project(terms, near, far, carry=None, final=False):
    rows = near.shape[0]
    width = sum(array.shape[1] for array in terms[0][1])
    steps = []
    for _, arrays, source, depth in terms:
        edges = [sum(array.shape[1] for array in arrays[:i]) for i in range(len(arrays) + 1)]
        spots = [slice(*edge) for edge in zip(edges[:-1], edges[1:])]
        steps.append((depth, spots, source))
    depth = sum(step[0] for step in steps)
    starts = jnp.stack([start for start, *_ in terms]).astype(jnp.int32)
    weights = [array for _, arrays, *_ in terms for array in arrays]
    whole = jax.ShapeDtypeStruct((2 * rows, width), jnp.float32)
    part = jax.ShapeDtypeStruct((rows, width), jnp.float32)
    carries = [] if carry is None else [carry]
    return pl.pallas_call(
        functools.partial(project_kernel, steps, carry is not None, final),
        out_shape=(part, part) if final else whole,
        in_specs=[pl.BlockSpec(memory_space=pltpu.SMEM)]
        + anywhere(2 + len(weights))
        + vmem(len(carries)),
        out_specs=tuple(vmem(2)) if final else vmem(1)[0],
        scratch_shapes=[
            pltpu.VMEM((2, rows, depth), jnp.bfloat16),
            pltpu.VMEM((depth, width), jnp.bfloat16),
            pltpu.SemaphoreType.DMA((len(steps), 4)),
        ],
        compiler_params=pltpu.CompilerParams(vmem_limit_bytes=48 * MIB),
        cost_estimate=pl.CostEstimate(
            flops=4 * rows * width * depth,
            bytes_accessed=2 * depth * (2 * rows + width),
            transcendentals=0,
        ),
    )(starts, near, far, *weights, *carries)


def turn(vectors, cosine, sine):
    return vectors * cosine + pltpu.roll(vectors, vectors.shape[1] // 2, 1) * sine


def pair_kernel(near, far, cosine, sine, out):
    head_size = cosine.shape[1]
    pair = near[...] + far[...]
    out[:, :head_size] = turn(pair[:, :head_size], cosine[...], sine[...]).astype(out.dtype)
    out[:, head_size:] = pair[:, head_size:].astype(out.dtype)


def finish_pair(near, far, cosine, sine):
    return pl.pallas_call(
        pair_kernel,
        out_shape=jax.ShapeDtypeStruct(near.shape, jnp.bfloat16),
        in_specs=vmem(4),
        out_specs=vmem(1)[0],
        compiler_params=pltpu.CompilerParams(vmem_limit_bytes=8 * MIB),
        cost_estimate=pl.CostEstimate(
            flops=6 * near.size, bytes_accessed=14 * near.size, transcendentals=0
        ),
    )(near, far, cosine, sine)


def attend_kernel(back, near, far, cosine, sine, first, keys_values, out, rotated):
    rows, head_size = cosine.shape
    head_count = near.shape[1] // head_size
    base = keys_values.shape[0] - rows
    tiles = rows // ROW_TILE
    for head in range(head_count):
        columns = slice(head * head_size, (head + 1) * head_size)
        turned = turn(near[:, columns] + far[:, columns], cosine[...], sine[...])
        turned = turned.astype(jnp.bfloat16)
        for tile in range(tiles):
            rotated[tile, head * ROW_TILE : (head + 1) * ROW_TILE, :] = turned[
                tile * ROW_TILE : (tile + 1) * ROW_TILE
            ]
    scale = jnp.float32(math.log2(math.e) / math.sqrt(head_size))
    for tile in range(tiles):
        begin = base + tile * ROW_TILE - back
        window = keys_values[begin : begin + back + ROW_TILE, :]
        scores = lax.dot_general(
            rotated[tile],
            window[:, :head_size],
            (((1,), (1,)), ((), ())),
            preferred_element_type=jnp.float32,
        )
        shape = (ROW_TILE, back + ROW_TILE)
        key_place = lax.broadcasted_iota(jnp.int32, shape, 1) + (tile * ROW_TILE - back)
        row_place = lax.broadcasted_iota(jnp.int32, shape, 0) + tile * ROW_TILE
        lower = first[tile * ROW_TILE : (tile + 1) * ROW_TILE, :]
        allowed = (key_place <= row_place) & (key_place >= lower)
        for head in range(head_count):
            part = scores[head * ROW_TILE : (head + 1) * ROW_TILE]
            part = jnp.where(allowed, part, jnp.float32(-1e30))
            largest = jnp.max(part, axis=-1, keepdims=True)
            exponents = jnp.exp2((part - largest) * scale)
            denominator = jnp.sum(exponents, axis=-1, keepdims=True)
            numerator = jnp.dot(
                exponents.astype(jnp.bfloat16),
                window[:, head_size:],
                preferred_element_type=jnp.float32,
            )
            left = head * head_size
            out[tile * ROW_TILE : (tile + 1) * ROW_TILE, left : left + head_size] = (
                numerator / denominator
            ).astype(out.dtype)


def attend(near, far, cosine, sine, first, keys_values, back):
    rows, width = near.shape
    head_size = cosine.shape[1]
    head_count = width // head_size
    window = back + ROW_TILE
    return pl.pallas_call(
        functools.partial(attend_kernel, back),
        out_shape=jax.ShapeDtypeStruct((rows, width), jnp.bfloat16),
        in_specs=vmem(6),
        out_specs=vmem(1)[0],
        scratch_shapes=[
            pltpu.VMEM((rows // ROW_TILE, head_count * ROW_TILE, head_size), jnp.bfloat16)
        ],
        compiler_params=pltpu.CompilerParams(
            vmem_limit_bytes=8 * MIB + 24 * head_count * ROW_TILE * window
        ),
        cost_estimate=pl.CostEstimate(
            flops=4 * rows * width * window,
            bytes_accessed=8 * rows * width,
            transcendentals=rows * head_count * window,
        ),
    )(near, far, cosine, sine, first, keys_values)


def shards(dp_size, ctx_size, tokens, w_query, w_key, w_value, doc_lengths):
    hidden = tokens[0]
    row_count = hidden.shape[0]
    depth, query_width = w_query.shape
    head_size = w_key.shape[1]
    chips = dp_size // 2
    bits = chips.bit_length() - 1
    me = lax.axis_index("dp")
    place = lax.axis_index("ctx")

    def swap(array, mask):
        return lax.ppermute(array, "dp", [(i, i ^ mask) for i in range(dp_size)])

    def fetch(pair, given, gate, later):
        held = []
        for side, array in enumerate(pair):
            pieces = {0: array, **given[side]}
            reached = [0]
            for axis in list(range(bits))[:: 1 - 2 * side]:
                for source in list(reached):
                    target = source | (1 << axis)
                    reached.append(target)
                    if target not in pieces:
                        sent = after(pieces[source], *(later if source else gate))
                        pieces[target] = swap(sent, 2 << axis)
            held.append(pieces)
        return held

    sibling_hidden = swap(hidden, 1)

    offset = place * row_count
    positions = offset + jnp.arange(row_count, dtype=jnp.int32)
    cosine, sine = rope_tables(positions, head_size)
    first = (doc_starts(doc_lengths[0], positions) - offset)[:, None]

    def begins(chip):
        return (me ^ (2 * chip)) * depth

    axes = [1 << axis for axis in range(bits)]
    half = depth // 2
    some = half // 2
    halved = ctx_size % 2 == 0 and bits > 1
    odd = place % 2
    begin = odd * some
    lack = some // 2 if some % 256 == 0 else some
    more = some - lack
    halves = [w_query[:half], w_query[half:]]

    pair_held = fetch((w_key, w_value), [{}, {}], [], [])
    pair_terms = [
        (begins(chip), [pair_held[side][chip] for side in range(2)], 0, depth)
        for chip in range(chips)
    ]
    early_chips = [0] + axes
    late_chips = [chip for chip in range(chips) if chip not in early_chips]
    near, far = project(pair_terms, hidden, sibling_hidden, None, True)
    pair = finish_pair(near, swap(far, 1), cosine, sine)
    longest = ctx_size * row_count // 2
    back = -(-(longest - 1) // ROW_TILE) * ROW_TILE
    blocks = [pair]
    for _ in range(min(ctx_size - 1, -(-back // row_count))):
        blocks.insert(0, lax.ppermute(blocks[0], "ctx", [(i, i + 1) for i in range(ctx_size - 1)]))
    keys_values = jnp.concatenate(blocks, axis=0)
    direct = [corner(pair_held[side][chip]) for side in range(2) for chip in axes]
    gate = [*direct, cosine, sine, first]
    later = [corner(blocks[-2])]

    early, late = [], []
    given = [{}, {}]
    if halved:
        ends = (0, bits - 1)
        joined = [
            jnp.concatenate(
                [
                    halves[side],
                    lax.dynamic_slice_in_dim(w_query, (1 - side) * half + begin, some, 0),
                ],
                axis=0,
            )
            for side in range(2)
        ]
        got = [swap(after(joined[side], *gate), 2 << ends[side]) for side in range(2)]
        both = [
            lax.dynamic_slice_in_dim(after(got[1 - side], *later), half + odd * more, lack, 0)
            for side in range(2)
        ]
        both = jnp.concatenate(both, axis=0)
        both = lax.ppermute(both, "ctx", [(i, i ^ 1) for i in range(ctx_size)])
        for side in range(2):
            chip = 1 << ends[side]
            given[side][chip] = after(got[side], *later)[:half]
            given[1 - side][chip] = None
            early.append((begins(chip) + side * half, [got[side]], 0, half))
            early.append((begins(chip) + (1 - side) * half + begin, [got[side]], half, some))
            first_row = begins(chip) + (1 - side) * half
            if more:
                row = some - odd * more
                part = lax.dynamic_slice_in_dim(w_query, (1 - side) * half + row, more, 0)
                part = swap(after(part, corner(near)), 2 << ends[side])
                early.append((first_row + row, [part], 0, more))
            late.append((first_row + (1 - odd) * (half - lack), [both], (1 - side) * lack, lack))
    query_held = fetch(halves, given, gate, later)
    for side in range(2):
        for chip in range(chips):
            if chip == 0 or chip in late_chips or chip not in given[side]:
                term = (begins(chip) + side * half, [query_held[side][chip]], 0, half)
                (late if chip in late_chips else early).append(term)

    def gated(terms, *gate):
        return [(start, [after(array, *gate) for array in arrays], *rest) for start, arrays, *rest in terms]

    carry = project(gated(early, *later), hidden, sibling_hidden)
    terms = gated(late, corner(blocks[0]))
    near, far = project(terms, hidden, sibling_hidden, carry, True)
    return attend(near, swap(far, 1), cosine, sine, first, keys_values, back)[None]


def solution(mesh):
    return jax.shard_map(
        functools.partial(shards, mesh.shape["dp"], mesh.shape["ctx"]),
        mesh=mesh,
        in_specs=(P("dp", "ctx", None), P("dp", None), P("dp", None), P("dp", None), P("dp", None)),
        out_specs=P("dp", "ctx", None),
        check_vma=False,
    )
```

```python
import functools
import math

import jax
import jax.numpy as jnp
from jax import lax
from jax.experimental import pallas as pl
from jax.experimental.pallas import tpu as pltpu
from jax.sharding import PartitionSpec as P

ROW_TILE = 128
MIB = 1024 * 1024


def rope_tables(positions, head_size):
    half_size = head_size // 2
    exponent = jnp.arange(half_size, dtype=jnp.float32) * (2.0 / head_size)
    inverse = jnp.power(jnp.float32(500000.0), -exponent)
    angles = positions.astype(jnp.float32)[:, None] * inverse[None, :]
    cosine = jnp.cos(angles)
    sine_part = jnp.sin(angles)
    return (
        jnp.concatenate([cosine, cosine], axis=-1),
        jnp.concatenate([-sine_part, sine_part], axis=-1),
    )


def doc_starts(doc_sizes, positions):
    doc_ends = jnp.cumsum(doc_sizes)
    doc_begin = doc_ends - doc_sizes
    chosen = jnp.where(doc_begin[None, :] <= positions[:, None], doc_begin[None, :], 0)
    return jnp.max(chosen, axis=1)


def vmem(count):
    return [pl.BlockSpec(memory_space=pltpu.VMEM)] * count


def anywhere(count):
    return [pl.BlockSpec(memory_space=pl.ANY)] * count


def after(array, *earlier):
    return lax.optimization_barrier((array, *earlier))[0]


def corner(array):
    return array[:8, :128]


def project_kernel(steps, carried, final, starts, near, far, *refs):
    count = sum(len(spots) for _, spots, _ in steps)
    weights, refs = refs[:count], refs[count:]
    if carried:
        carry, refs = refs[0], refs[1:]
    outs, (tokens, held, sems) = refs[:-3], refs[-3:]
    rows = near.shape[0]
    batches = ([], [], [])
    used = row = 0
    for step, (depth, spots, source) in enumerate(steps):
        here = slice(row, row + depth)
        row += depth
        window = pl.ds(pl.multiple_of(starts[step], 128), depth)
        for index, columns in enumerate(spots):
            batches[0].append(
                pltpu.make_async_copy(
                    weights[used].at[source : source + depth],
                    held.at[here, columns],
                    sems.at[step, 2 + index],
                )
            )
            used += 1
        for side, ref in enumerate((far, near)):
            batches[1 + side].append(
                pltpu.make_async_copy(
                    ref.at[:, window], tokens.at[side, :, here], sems.at[step, side]
                )
            )
    for batch in batches:
        for copy in batch:
            copy.start()
    for copy in batches[0]:
        copy.wait()
    for side in range(2):
        for copy in batches[1 + side]:
            copy.wait()
        total = jnp.dot(tokens[side], held[...], preferred_element_type=jnp.float32)
        place = slice((1 - side) * rows, (2 - side) * rows)
        if carried:
            total = total + carry[place, :]
        if final:
            outs[1 - side][...] = total.astype(outs[1 - side].dtype)
        else:
            outs[0][place, :] = total


def project(terms, near, far, carry=None, final=None):
    rows = near.shape[0]
    width = sum(array.shape[1] for array in terms[0][1])
    steps = []
    for _, arrays, source, depth in terms:
        edges = [sum(array.shape[1] for array in arrays[:i]) for i in range(len(arrays) + 1)]
        spots = [slice(*edge) for edge in zip(edges[:-1], edges[1:])]
        steps.append((depth, spots, source))
    depth = sum(step[0] for step in steps)
    starts = jnp.stack([start for start, *_ in terms]).astype(jnp.int32)
    weights = [array for _, arrays, *_ in terms for array in arrays]
    whole = jax.ShapeDtypeStruct((2 * rows, width), jnp.float32)
    part = jax.ShapeDtypeStruct((rows, width), jnp.float32)
    sent = jax.ShapeDtypeStruct((rows, width), final or jnp.float32)
    carries = [] if carry is None else [carry]
    return pl.pallas_call(
        functools.partial(project_kernel, steps, carry is not None, final),
        out_shape=(part, sent) if final else whole,
        in_specs=[pl.BlockSpec(memory_space=pltpu.SMEM)]
        + anywhere(2 + len(weights))
        + vmem(len(carries)),
        out_specs=tuple(vmem(2)) if final else vmem(1)[0],
        scratch_shapes=[
            pltpu.VMEM((2, rows, depth), jnp.bfloat16),
            pltpu.VMEM((depth, width), jnp.bfloat16),
            pltpu.SemaphoreType.DMA((len(steps), 4)),
        ],
        compiler_params=pltpu.CompilerParams(vmem_limit_bytes=48 * MIB),
        cost_estimate=pl.CostEstimate(
            flops=4 * rows * width * depth,
            bytes_accessed=2 * depth * (2 * rows + width),
            transcendentals=0,
        ),
    )(starts, near, far, *weights, *carries)


def turn(vectors, cosine, sine):
    return vectors * cosine + pltpu.roll(vectors, vectors.shape[1] // 2, 1) * sine


def pair_kernel(near, far, cosine, sine, out):
    head_size = cosine.shape[1]
    pair = near[...] + far[...].astype(jnp.float32)
    out[:, :head_size] = turn(pair[:, :head_size], cosine[...], sine[...]).astype(out.dtype)
    out[:, head_size:] = pair[:, head_size:].astype(out.dtype)


def finish_pair(near, far, cosine, sine):
    return pl.pallas_call(
        pair_kernel,
        out_shape=jax.ShapeDtypeStruct(near.shape, jnp.bfloat16),
        in_specs=vmem(4),
        out_specs=vmem(1)[0],
        compiler_params=pltpu.CompilerParams(vmem_limit_bytes=8 * MIB),
        cost_estimate=pl.CostEstimate(
            flops=6 * near.size, bytes_accessed=14 * near.size, transcendentals=0
        ),
    )(near, far, cosine, sine)


def attend_kernel(back, near, far, cosine, sine, first, keys_values, out, rotated):
    rows, head_size = cosine.shape
    head_count = near.shape[1] // head_size
    base = keys_values.shape[0] - rows
    tiles = rows // ROW_TILE
    for head in range(head_count):
        columns = slice(head * head_size, (head + 1) * head_size)
        turned = turn(near[:, columns] + far[:, columns].astype(jnp.float32), cosine[...], sine[...])
        turned = turned.astype(jnp.bfloat16)
        for tile in range(tiles):
            rotated[tile, head * ROW_TILE : (head + 1) * ROW_TILE, :] = turned[
                tile * ROW_TILE : (tile + 1) * ROW_TILE
            ]
    scale = jnp.float32(math.log2(math.e) / math.sqrt(head_size))
    for tile in range(tiles):
        begin = base + tile * ROW_TILE - back
        window = keys_values[begin : begin + back + ROW_TILE, :]
        scores = lax.dot_general(
            rotated[tile],
            window[:, :head_size],
            (((1,), (1,)), ((), ())),
            preferred_element_type=jnp.float32,
        )
        shape = (ROW_TILE, back + ROW_TILE)
        key_place = lax.broadcasted_iota(jnp.int32, shape, 1) + (tile * ROW_TILE - back)
        row_place = lax.broadcasted_iota(jnp.int32, shape, 0) + tile * ROW_TILE
        lower = first[tile * ROW_TILE : (tile + 1) * ROW_TILE, :]
        allowed = (key_place <= row_place) & (key_place >= lower)
        for head in range(head_count):
            part = scores[head * ROW_TILE : (head + 1) * ROW_TILE]
            part = jnp.where(allowed, part, jnp.float32(-1e30))
            largest = jnp.max(part, axis=-1, keepdims=True)
            exponents = jnp.exp2((part - largest) * scale)
            denominator = jnp.sum(exponents, axis=-1, keepdims=True)
            numerator = jnp.dot(
                exponents.astype(jnp.bfloat16),
                window[:, head_size:],
                preferred_element_type=jnp.float32,
            )
            left = head * head_size
            out[tile * ROW_TILE : (tile + 1) * ROW_TILE, left : left + head_size] = (
                numerator / denominator
            ).astype(out.dtype)


def attend(near, far, cosine, sine, first, keys_values, back):
    rows, width = near.shape
    head_size = cosine.shape[1]
    head_count = width // head_size
    window = back + ROW_TILE
    return pl.pallas_call(
        functools.partial(attend_kernel, back),
        out_shape=jax.ShapeDtypeStruct((rows, width), jnp.bfloat16),
        in_specs=vmem(6),
        out_specs=vmem(1)[0],
        scratch_shapes=[
            pltpu.VMEM((rows // ROW_TILE, head_count * ROW_TILE, head_size), jnp.bfloat16)
        ],
        compiler_params=pltpu.CompilerParams(
            vmem_limit_bytes=8 * MIB + 24 * head_count * ROW_TILE * window
        ),
        cost_estimate=pl.CostEstimate(
            flops=4 * rows * width * window,
            bytes_accessed=8 * rows * width,
            transcendentals=rows * head_count * window,
        ),
    )(near, far, cosine, sine, first, keys_values)


def shards(dp_size, ctx_size, tokens, w_query, w_key, w_value, doc_lengths):
    hidden = tokens[0]
    row_count = hidden.shape[0]
    depth, query_width = w_query.shape
    head_size = w_key.shape[1]
    chips = dp_size // 2
    bits = chips.bit_length() - 1
    me = lax.axis_index("dp")
    place = lax.axis_index("ctx")

    def swap(array, mask):
        return lax.ppermute(array, "dp", [(i, i ^ mask) for i in range(dp_size)])

    def fetch(pair, given, gate, later):
        held = []
        for side, array in enumerate(pair):
            pieces = {0: array, **given[side]}
            reached = [0]
            for axis in list(range(bits))[:: 1 - 2 * side]:
                for source in list(reached):
                    target = source | (1 << axis)
                    reached.append(target)
                    if target not in pieces:
                        sent = after(pieces[source], *(later if source else gate))
                        pieces[target] = swap(sent, 2 << axis)
            held.append(pieces)
        return held

    sibling_hidden = swap(hidden, 1)

    offset = place * row_count
    positions = offset + jnp.arange(row_count, dtype=jnp.int32)
    cosine, sine = rope_tables(positions, head_size)
    first = (doc_starts(doc_lengths[0], positions) - offset)[:, None]

    def begins(chip):
        return (me ^ (2 * chip)) * depth

    axes = [1 << axis for axis in range(bits)]
    half = depth // 2
    some = half // 2
    halved = ctx_size % 2 == 0 and bits > 1
    odd = place % 2
    begin = odd * some
    lack = some // 2 if some % 256 == 0 else some
    more = some - lack
    halves = [w_query[:half], w_query[half:]]

    pair_held = fetch((w_key, w_value), [{}, {}], [], [])
    pair_terms = [
        (begins(chip), [pair_held[side][chip] for side in range(2)], 0, depth)
        for chip in range(chips)
    ]
    early_chips = [0] + axes
    late_chips = [chip for chip in range(chips) if chip not in early_chips]
    carry = project([pair_terms[chip] for chip in early_chips], hidden, sibling_hidden)
    terms = [pair_terms[chip] for chip in late_chips]
    near, far = project(terms, hidden, sibling_hidden, carry, jnp.float32)
    pair = finish_pair(near, swap(far, 1), cosine, sine)
    longest = ctx_size * row_count // 2
    back = -(-(longest - 1) // ROW_TILE) * ROW_TILE
    blocks = [pair]
    for _ in range(min(ctx_size - 1, -(-back // row_count))):
        blocks.insert(0, lax.ppermute(blocks[0], "ctx", [(i, i + 1) for i in range(ctx_size - 1)]))
    keys_values = jnp.concatenate(blocks, axis=0)
    direct = [corner(pair_held[side][chip]) for side in range(2) for chip in axes]
    gate = [*direct, cosine, sine, first]
    later = [corner(blocks[-2])]

    early, late = [], []
    given = [{}, {}]
    if halved:
        ends = (0, bits - 1)
        joined = [
            jnp.concatenate(
                [
                    halves[side],
                    lax.dynamic_slice_in_dim(w_query, (1 - side) * half + begin, some, 0),
                ],
                axis=0,
            )
            for side in range(2)
        ]
        got = [swap(after(joined[side], *gate), 2 << ends[side]) for side in range(2)]
        both = [
            lax.dynamic_slice_in_dim(after(got[1 - side], *later), half + odd * more, lack, 0)
            for side in range(2)
        ]
        both = jnp.concatenate(both, axis=0)
        both = lax.ppermute(both, "ctx", [(i, i ^ 1) for i in range(ctx_size)])
        for side in range(2):
            chip = 1 << ends[side]
            given[side][chip] = after(got[side], *later)[:half]
            given[1 - side][chip] = None
            early.append((begins(chip) + side * half, [got[side]], 0, half))
            early.append((begins(chip) + (1 - side) * half + begin, [got[side]], half, some))
            first_row = begins(chip) + (1 - side) * half
            if more:
                row = some - odd * more
                part = lax.dynamic_slice_in_dim(w_query, (1 - side) * half + row, more, 0)
                part = swap(after(part, corner(near)), 2 << ends[side])
                early.append((first_row + row, [part], 0, more))
            late.append((first_row + (1 - odd) * (half - lack), [both], (1 - side) * lack, lack))
    query_held = fetch(halves, given, gate, later)
    for side in range(2):
        for chip in range(chips):
            if chip == 0 or chip in late_chips or chip not in given[side]:
                term = (begins(chip) + side * half, [query_held[side][chip]], 0, half)
                (late if chip in late_chips else early).append(term)

    def gated(terms, *gate):
        return [(start, [after(array, *gate) for array in arrays], *rest) for start, arrays, *rest in terms]

    carry = project(gated(early, *later), hidden, sibling_hidden)
    terms = gated(late, corner(blocks[0]))
    near, far = project(terms, hidden, sibling_hidden, carry, jnp.bfloat16)
    return attend(near, swap(far, 1), cosine, sine, first, keys_values, back)[None]


def solution(mesh):
    return jax.shard_map(
        functools.partial(shards, mesh.shape["dp"], mesh.shape["ctx"]),
        mesh=mesh,
        in_specs=(P("dp", "ctx", None), P("dp", None), P("dp", None), P("dp", None), P("dp", None)),
        out_specs=P("dp", "ctx", None),
        check_vma=False,
    )
```
